128 devices in a mesh: pts: 16 (over x, z), cent: 8 (over y, core).
Axes of the slice: x: 4, y: 4, z: 4, core: 2. Of those that a mesh axis runs over, the one named last changes fastest.
Arguments:
- points: bfloat16 [262144, 1024], P(('pts', 'cent')), may hold values from -40 to 40, as said below
- centroids: bfloat16 [65536, 1024], P('cent'), may hold values from -3 to 3, as said below
- prev_loads: bfloat16 [65536], P('cent'), may hold values from 0.25 to 4
- candidates: int32 [256, 4], P(('pts', 'cent')), may hold values from 0 to 511, as said below
- panel_home: int32 [512], replicated, may hold values from 0 to 511, as said below
Outputs:
- new_centroids: bfloat16 [65536, 1024], P(('cent', 'pts'))
- new_loads: float32 [65536], P(('cent', 'pts'))
The draws below stay inside these ranges and needn't reach their ends.
Inputs may be any that keep to these rules, and one draw needn't show every extreme that they name: `candidates`: within a row the 4 panels sit in slots of 4 different owners (slot // 64); the 2 rows of one device name the same owner in each column, so one device asks each of 4 owners for 2 panels, not always distinct, and the others for none. Low slots of an owner are asked for more often. `panel_home`: A permutation of the panel ids. `points`: Real-valued embeddings. Real-valued centroids.
All inputs are finite; a program needn't handle non-finite values.
Results may differ from the reference program's by a relative error of at most 0.0095.
Values may be sent and summed in bfloat16 or wider, within the bound.
No kernel may reach another device: no remote copies, remote signals or barrier semaphores. Data moves between devices by JAX's collectives and lax.ppermute only.
A program may use at most 320 MiB of HBM per device.

```python
import math
import jax
import jax.numpy as jnp
from jax import lax

D = 1024
PANEL = 128
CAND = 4
GROUP = 1024
GROUPS_DEV = 2
PAN_DEV = 64
PANELS = 512
CENTROIDS = 65536
GROUPS = 256
POINTS = 262144
N_CENT = 8


def centroid_values(key):
    return jnp.clip(0.5 * jax.random.normal(key, (CENTROIDS, D), jnp.float32), -3.0, 3.0)


def layout(key):
    key = jax.random.fold_in(key, 101)
    first, second, third, fourth = jax.random.split(key, 4)
    home = jax.random.permutation(first, PANELS).astype(jnp.int32)
    devices = GROUPS // GROUPS_DEV
    scores = jax.random.randint(second, (devices, N_CENT), 0, 1 << 20) * N_CENT + jnp.arange(N_CENT, dtype=jnp.int32)[None, :]
    owner_pick = jnp.argsort(scores, axis=1)[:, :CAND].astype(jnp.int32)
    upper = jax.random.randint(third, (devices, GROUPS_DEV, CAND), 0, PAN_DEV)
    lower = jax.random.randint(fourth, (devices, GROUPS_DEV, CAND), 0, PAN_DEV)
    local_ids = jnp.minimum(upper, lower)
    slot_ids = (owner_pick[:, None, :] * PAN_DEV + local_ids).reshape(GROUPS, CAND).astype(jnp.int32)
    inverse = jnp.argsort(home).astype(jnp.int32)
    panel_ids = jnp.take(inverse, slot_ids, axis=0).astype(jnp.int32)
    return (home, panel_ids)


def draw_points(key, part):
    key = jax.random.fold_in(key, 7)
    first = jax.random.fold_in(key, 0)
    point_values = jax.random.normal(first, (POINTS, D), jnp.float32)
    point_values = jnp.clip(point_values, -6.0, 6.0)
    return point_values.astype(jnp.bfloat16)


def draw_centroids(key, part):
    return centroid_values(key).astype(jnp.bfloat16)


def draw_candidates(key, part):
    home, panel_ids = layout(key)
    return panel_ids


def draw_panel_home(key, part):
    home, panel_ids = layout(key)
    return home


def shard_levels(stream_key, extent, pieces, low, high):
    level, own = 1.0, jax.random.fold_in(stream_key, 6)
    for dim, shards_of in pieces:
        steps = jnp.exp(jax.random.uniform(jax.random.fold_in(own, dim), (shards_of,), jnp.float32, low / len(pieces), high / len(pieces)))
        level = level * jnp.repeat(steps, extent[dim] // shards_of).reshape([-1 if axis == dim else 1 for axis in range(len(extent))])
    return level


def setup_inputs(seed: int = 0) -> dict:
    keys = jax.random.split(jax.random.key(seed), 6)
    return {
        "points": draw_points(jax.random.fold_in(keys[5], 71), 0),
        "centroids": draw_centroids(jax.random.fold_in(keys[5], 71), 0),
        "prev_loads": jnp.clip(jnp.exp(math.log(4.0) - 2.7725887 * jax.random.uniform(keys[2], (CENTROIDS,), jnp.float32) ** shard_levels(keys[2], (CENTROIDS,), ((0, 8),), -0.2, 0.2)), 0.25, 4.0).astype(jnp.bfloat16),
        "candidates": draw_candidates(jax.random.fold_in(keys[5], 71), 0),
        "panel_home": draw_panel_home(jax.random.fold_in(keys[5], 71), 0),
    }


sharpness_divisor = 16.0
evenness_coefficient = 1.0
prior_mass = 1.0


def score_group(members, centers, evenness_surcharge):
    inner_pairwise_matrix = lax.dot_general(members, centers, (((1,), (1,)), ((), ())), preferred_element_type=jnp.float32)
    length_quadratics = jnp.sum(jnp.square(centers.astype(jnp.float32)), axis=1)
    cluster_affinity_scores = (2.0 * inner_pairwise_matrix - length_quadratics[None, :]) / sharpness_divisor - evenness_coefficient * evenness_surcharge[None, :]
    highest = jnp.max(cluster_affinity_scores, axis=1, keepdims=True)
    raised = jnp.exp(cluster_affinity_scores - highest)
    shares = (raised / jnp.sum(raised, axis=1, keepdims=True)).astype(jnp.bfloat16)
    partial_sums = lax.dot_general(shares, members, (((0,), (0,)), ((), ())), preferred_element_type=jnp.float32).astype(jnp.bfloat16)
    membership_weights = jnp.sum(shares.astype(jnp.float32), axis=0).astype(jnp.bfloat16)
    return partial_sums, membership_weights


def reference(points, centroids, prev_loads, candidates, panel_home):
    shelf = centroids.reshape(PANELS, PANEL, D)
    load_shelf = prev_loads.reshape(PANELS, PANEL)
    slot_ids = jnp.take(panel_home, candidates, axis=0).astype(jnp.int32)
    clustered_rows = points.reshape(GROUPS, GROUP, D)

    def accumulate(totals, sample_matrix):
        members, picked = sample_matrix
        centers = jnp.take(shelf, picked, axis=0).reshape(CAND * PANEL, D)
        evenness_surcharge = jnp.log(jnp.take(load_shelf, picked, axis=0).reshape(CAND * PANEL).astype(jnp.float32))
        partial_sums, membership_weights = score_group(members, centers, evenness_surcharge)
        sum_acc = totals[0].at[picked].add(partial_sums.reshape(CAND, PANEL, D).astype(jnp.float32))
        weight_acc = totals[1].at[picked].add(membership_weights.reshape(CAND, PANEL).astype(jnp.float32))
        return (sum_acc, weight_acc), None

    start_acc = (jnp.zeros((PANELS, PANEL, D), jnp.float32), jnp.zeros((PANELS, PANEL), jnp.float32))
    (sum_acc, weight_acc), unused = lax.scan(accumulate, start_acc, (clustered_rows, slot_ids))
    weight_rows = weight_acc.reshape(CENTROIDS)
    new_centroids = ((sum_acc.reshape(CENTROIDS, D) + prior_mass * centroids.astype(jnp.float32)) / (weight_rows[:, None] + prior_mass)).astype(jnp.bfloat16)
    return new_centroids, weight_rows
```

```python
import functools

import jax
import jax.numpy as jnp
from jax import lax
from jax.experimental import pallas as pl
from jax.experimental.pallas import tpu as pltpu
from jax.sharding import PartitionSpec as P

PANEL = 128
GROUP = 1024
CAND = 4
GROUPS_DEV = 2
REQ = CAND * GROUPS_DEV
PAN_DEV = 64
WIDTH = 1024
N_CENT = 8
CHIPS = 4
N_PTS = 16
ROWS = 16
HALF = 512
LANE = 128
TILES = HALF // LANE
SEND_TILES = REQ * TILES + 1
DENSE = PAN_DEV * TILES
CHUNK_TILES = DENSE + 1
LAST_TILES = CAND * TILES + 1

sharpness_divisor = 16.0
evenness_coefficient = 1.0
prior_mass = 1.0

BF16 = jnp.bfloat16
F32 = jnp.float32
MIB = 1 << 20


def params(mib):
    return pltpu.CompilerParams(vmem_limit_bytes=mib * MIB)


def pick_kernel(ids, table, out, sems):
    for n in range(ids.shape[0]):
        pltpu.make_async_copy(table.at[ids[n]], out.at[n], sems.at[n]).start()
    for n in range(ids.shape[0]):
        pltpu.make_async_copy(table.at[ids[n]], out.at[n], sems.at[n]).wait()


def pick_panels(ids, table):
    count = ids.shape[0]
    return pl.pallas_call(
        pick_kernel,
        out_shape=jax.ShapeDtypeStruct((count, PANEL, WIDTH), BF16),
        in_specs=[pl.BlockSpec(memory_space=pltpu.SMEM), pl.BlockSpec(memory_space=pl.ANY)],
        out_specs=pl.BlockSpec(memory_space=pl.ANY),
        scratch_shapes=[pltpu.SemaphoreType.DMA((count,))],
        cost_estimate=pl.CostEstimate(flops=0, bytes_accessed=4 * count * PANEL * WIDTH, transcendentals=0),
    )(ids, table)


def score_kernel(target, points, c0, c1, c2, c3, surcharge, tags, out, centers, shares, marks):
    del target
    group = pl.program_id(0)
    for j, panel in enumerate((c0, c1, c2, c3)):
        centers[j * PANEL : (j + 1) * PANEL, :] = panel[0]
    wide = centers[...].astype(F32)
    squares = jnp.sum(wide * wide, axis=1, keepdims=True)
    bias = squares * (1.0 / sharpness_divisor) + evenness_coefficient * surcharge[0]
    step = 256
    weights = jnp.zeros((CAND * PANEL, LANE), F32)
    for s in range(GROUP // step):
        block = points[s * step : (s + 1) * step, :]
        inner = lax.dot_general(centers[...], block, (((1,), (1,)), ((), ())), preferred_element_type=F32)
        logits = inner * (2.0 / sharpness_divisor) - bias
        highest = jnp.max(logits, axis=0, keepdims=True)
        raised = jnp.exp(logits - highest)
        scale = 1.0 / jnp.sum(raised, axis=0, keepdims=True)
        share = (raised * scale).astype(BF16)
        shares[:, s * step : (s + 1) * step] = share
        rounded = share.astype(F32)
        for part in range(step // LANE):
            weights = weights + rounded[:, part * LANE : (part + 1) * LANE]
    weight = jnp.sum(weights, axis=1, keepdims=True)
    coarse = weight.astype(BF16).astype(F32)
    fine = weight - coarse
    lane = lax.broadcasted_iota(jnp.int32, (PANEL, LANE), 1)

    @pl.when(group == 0)
    def _():
        marks[...] = jnp.broadcast_to(tags[0:1, :], (PANEL, LANE))

    tile = marks[...]
    for j in range(CAND):
        place = group * CAND + j
        rows = slice(j * PANEL, (j + 1) * PANEL)
        tile = jnp.where(lane == place, coarse[rows], tile)
        tile = jnp.where(lane == REQ + place, fine[rows], tile)
    marks[...] = tile

    wide_step = 256
    for s in range(WIDTH // wide_step):
        part = lax.dot_general(
            shares[...], points[:, s * wide_step : (s + 1) * wide_step], (((1,), (0,)), ((), ())),
            preferred_element_type=F32,
        ).astype(BF16)
        for t in range(wide_step // LANE):
            column = s * (wide_step // LANE) + t
            half, tile_at = divmod(column, TILES)
            for j in range(CAND):
                for block_at in range(PANEL // ROWS):
                    row = j * PANEL + block_at * ROWS
                    out[block_at * 2 + half, (group * CAND + j) * TILES + tile_at] = part[
                        row : row + ROWS, t * LANE : (t + 1) * LANE
                    ]

    @pl.when(group == GROUPS_DEV - 1)
    def _():
        last = marks[...].astype(BF16)
        for block_at in range(PANEL // ROWS):
            for half in range(2):
                out[block_at * 2 + half, REQ * TILES] = last[block_at * ROWS : (block_at + 1) * ROWS]


def score(target, points, arrived, surcharge, tags):
    def panel(j):
        return pl.BlockSpec((1, PANEL, WIDTH), lambda g, t: (t[g * CAND + j], 0, 0))

    return pl.pallas_call(
        score_kernel,
        grid_spec=pltpu.PrefetchScalarGridSpec(
            num_scalar_prefetch=1,
            grid=(GROUPS_DEV,),
            in_specs=[
                pl.BlockSpec((GROUP, WIDTH), lambda g, t: (g, 0)),
                panel(0), panel(1), panel(2), panel(3),
                pl.BlockSpec((1, CAND * PANEL, 1), lambda g, t: (g, 0, 0)),
                pl.BlockSpec((ROWS, LANE), lambda g, t: (0, 0)),
            ],
            out_specs=pl.BlockSpec((N_PTS, SEND_TILES, ROWS, LANE), lambda g, t: (0, 0, 0, 0)),
            scratch_shapes=[
                pltpu.VMEM((CAND * PANEL, WIDTH), BF16),
                pltpu.VMEM((CAND * PANEL, GROUP), BF16),
                pltpu.VMEM((PANEL, LANE), F32),
            ],
        ),
        out_shape=jax.ShapeDtypeStruct((N_PTS, SEND_TILES, ROWS, LANE), BF16),
        compiler_params=params(48),
        cost_estimate=pl.CostEstimate(flops=4294967296, bytes_accessed=10 * MIB, transcendentals=1 << 20),
    )(target, points, arrived, arrived, arrived, arrived, surcharge, tags)


def spread_kernel(places, mine, mate, lanes, own, own_weights, out1, out2, out3, total):
    total[...] = jnp.zeros_like(total)
    count = N_PTS * REQ
    for first, source in ((0, mine), (count, mate)):
        def add(s, carry, first=first, source=source):
            for i in range(REQ):
                at = places[first + s * REQ + i] * TILES
                total[pl.ds(at, TILES)] += source[s, i * TILES : (i + 1) * TILES].astype(F32)
            return carry

        lax.fori_loop(0, N_PTS, add, 0)
    panel = lax.broadcasted_iota(jnp.int32, (CHIPS * PAN_DEV, LANE), 0)
    weights = jnp.zeros((ROWS, CHIPS * PAN_DEV), F32)
    for n in range(2 * N_PTS):
        source = mine if n < N_PTS else mate
        chosen = jnp.where(panel == lanes[n : n + 1, :], 1.0, 0.0).astype(BF16)
        weights = weights + lax.dot_general(
            source[n % N_PTS, REQ * TILES], chosen, (((1,), (1,)), ((), ())), preferred_element_type=F32
        )
    own[...] = total[0:DENSE]
    coarse = weights.astype(BF16)
    fine = (weights - coarse.astype(F32)).astype(BF16)
    own_weights[...] = weights[:, 0:LANE]
    for d, out in ((1, out1), (2, out2), (3, out3)):
        out[0:DENSE] = total[d * DENSE : (d + 1) * DENSE].astype(BF16)
        out[DENSE, :, 0:PAN_DEV] = coarse[:, d * PAN_DEV : (d + 1) * PAN_DEV]
        out[DENSE, :, PAN_DEV:LANE] = fine[:, d * PAN_DEV : (d + 1) * PAN_DEV]


def spread(places, mine, mate, lanes):
    vmem = pl.BlockSpec(memory_space=pltpu.VMEM)
    chunk = jax.ShapeDtypeStruct((CHUNK_TILES, ROWS, LANE), BF16)
    return pl.pallas_call(
        spread_kernel,
        in_specs=[pl.BlockSpec(memory_space=pltpu.SMEM), vmem, vmem, vmem],
        out_specs=[vmem] * 5,
        out_shape=[
            jax.ShapeDtypeStruct((DENSE, ROWS, LANE), F32),
            jax.ShapeDtypeStruct((ROWS, LANE), F32),
            chunk, chunk, chunk,
        ],
        scratch_shapes=[pltpu.VMEM((CHIPS * DENSE + TILES, ROWS, LANE), F32)],
        compiler_params=params(48),
        cost_estimate=pl.CostEstimate(flops=1 << 22, bytes_accessed=10 * MIB, transcendentals=0),
    )(places, mine, mate, lanes)


def finish_kernel(me, own, own_weights, in1, in2, in3, old, out):
    del me
    weights = own_weights[:, 0:PAN_DEV]
    for arrived in (in1, in2, in3):
        pair = arrived[DENSE].astype(F32)
        weights = weights + (pair[:, 0:PAN_DEV] + pair[:, PAN_DEV:LANE])
    inverse = 1.0 / (weights + prior_mass)
    for q in range(PAN_DEV):
        scale = jnp.broadcast_to(inverse[:, q : q + 1], (ROWS, LANE))
        for t in range(TILES):
            at = q * TILES + t
            total = own[at] + in1[at].astype(F32) + in2[at].astype(F32) + in3[at].astype(F32)
            previous = old[q, :, t * LANE : (t + 1) * LANE].astype(F32)
            fresh = (total + prior_mass * previous) * scale
            out[q // CAND, (q % CAND) * TILES + t] = fresh.astype(BF16)
    coarse = weights.astype(BF16)
    fine = (weights - coarse.astype(F32)).astype(BF16)
    for p in range(N_PTS):
        out[p, CAND * TILES, :, 0:PAN_DEV] = coarse
        out[p, CAND * TILES, :, PAN_DEV:LANE] = fine


def finish(me, own, own_weights, arrived, table):
    whole = lambda shape: pl.BlockSpec(shape, lambda g, me: (0,) * len(shape))
    chunk = whole((CHUNK_TILES, ROWS, LANE))
    return pl.pallas_call(
        finish_kernel,
        grid_spec=pltpu.PrefetchScalarGridSpec(
            num_scalar_prefetch=1,
            grid=(1,),
            in_specs=[
                whole((DENSE, ROWS, LANE)), whole((ROWS, LANE)), chunk, chunk, chunk,
                pl.BlockSpec((PAN_DEV, ROWS, HALF), lambda g, me: (0, me[0] // 2, me[0] % 2)),
            ],
            out_specs=whole((N_PTS, LAST_TILES, ROWS, LANE)),
        ),
        out_shape=jax.ShapeDtypeStruct((N_PTS, LAST_TILES, ROWS, LANE), BF16),
        compiler_params=params(48),
        cost_estimate=pl.CostEstimate(flops=1 << 22, bytes_accessed=8 * MIB, transcendentals=0),
    )(me, own, own_weights, *arrived, table)


def place_kernel(me, pieces, out, loads):
    for block_at in range(PANEL // ROWS):
        for half in range(2):
            for q in range(CAND):
                for t in range(TILES):
                    column = half * HALF + t * LANE
                    out[q, block_at * ROWS : (block_at + 1) * ROWS, column : column + LANE] = pieces[
                        block_at * 2 + half, q * TILES + t
                    ]
    lane = lax.broadcasted_iota(jnp.int32, (ROWS, LANE), 1)
    row = lax.broadcasted_iota(jnp.int32, (ROWS, LANE), 0)
    wanted = me[0] * CAND + row
    chosen = jnp.where((row < CAND) & (lane % PAN_DEV == wanted), 1.0, 0.0).astype(BF16)
    for block_at in range(PANEL // ROWS):
        pair = pieces[block_at * 2, CAND * TILES]
        part = lax.dot_general(chosen, pair, (((1,), (1,)), ((), ())), preferred_element_type=F32)
        loads[:, block_at * ROWS : (block_at + 1) * ROWS] = part[0:8]


def place(me, pieces):
    vmem = pl.BlockSpec(memory_space=pltpu.VMEM)
    return pl.pallas_call(
        place_kernel,
        in_specs=[pl.BlockSpec(memory_space=pltpu.SMEM), vmem],
        out_specs=[vmem, vmem],
        out_shape=[
            jax.ShapeDtypeStruct((CAND, PANEL, WIDTH), BF16),
            jax.ShapeDtypeStruct((8, PANEL), F32),
        ],
        compiler_params=params(32),
        cost_estimate=pl.CostEstimate(flops=1 << 20, bytes_accessed=2 * MIB, transcendentals=0),
    )(me, pieces)


def shift(dy, dk):
    return [(y * 2 + k, ((y + dy) % CHIPS) * 2 + (k + dk) % 2) for y in range(CHIPS) for k in range(2)]


def exchange(x, axis):
    return lax.all_to_all(x, axis, split_axis=0, concat_axis=0, tiled=True)


def local(points, centroids, prev_loads, candidates, panel_home):
    me = lax.axis_index("pts")
    here = lax.axis_index("cent")
    chip, core = here // 2, here % 2
    shelf = centroids.reshape(PAN_DEV, PANEL, WIDTH)

    with jax.named_scope("requests"):
        wanted_ids = candidates.reshape(REQ)
        slots = jnp.sum(
            jnp.where(wanted_ids[:, None] == jnp.arange(panel_home.shape[0], dtype=jnp.int32), panel_home[None, :], 0),
            axis=1,
        )
        owners, local_ids = slots // PAN_DEV, slots % PAN_DEV
        target = owners * GROUPS_DEV + jnp.arange(REQ, dtype=jnp.int32) // CAND
        spots = jnp.arange(N_CENT * GROUPS_DEV, dtype=jnp.int32)
        wanted = jnp.sum(jnp.where(target[None, :] == spots[:, None], local_ids[None, :], 0), axis=1)
        ask = jnp.zeros((N_CENT, 1, ROWS, LANE), BF16)
        ask = ask.at[:, 0, 0, 0:GROUPS_DEV].set(wanted.reshape(N_CENT, GROUPS_DEV).astype(BF16))
        table = jnp.broadcast_to(
            prev_loads.reshape(1, PAN_DEV // ROWS, ROWS, LANE), (N_CENT, PAN_DEV // ROWS, ROWS, LANE)
        )
        answered = exchange(jnp.concatenate([table, ask], axis=1), "cent")
        asked = answered[:, PAN_DEV // ROWS, 0, 0:GROUPS_DEV].astype(jnp.int32).reshape(-1)

    with jax.named_scope("gather_panels"):
        arrived = exchange(pick_panels(asked, shelf).reshape(N_CENT, GROUPS_DEV, PANEL, WIDTH), "cent")
        arrived = arrived.reshape(N_CENT * GROUPS_DEV, PANEL, WIDTH)

    with jax.named_scope("loads"):
        load_table = answered[:, : PAN_DEV // ROWS].reshape(N_CENT * PAN_DEV, PANEL)
        loads = jnp.take(load_table, slots, axis=0, mode="clip").astype(F32)
        surcharge = jnp.log(loads).reshape(GROUPS_DEV, CAND * PANEL, 1)
        marks = jnp.concatenate([jnp.zeros((2 * REQ,), F32), (slots // 16).astype(F32), (slots % 16).astype(F32)])
        tags = jnp.broadcast_to(jnp.pad(marks, (0, LANE - 4 * REQ)), (ROWS, LANE))

    with jax.named_scope("score"):
        pieces = score(target, points, arrived, surcharge, tags)

    with jax.named_scope("split_pieces"):
        mine = exchange(pieces, "pts")
        mate = lax.ppermute(mine, "cent", shift(0, 1))

    with jax.named_scope("spread"):
        heads = jnp.stack([mine[:, REQ * TILES, 0, 2 * REQ : 4 * REQ], mate[:, REQ * TILES, 0, 2 * REQ : 4 * REQ]])
        heads = heads.reshape(2 * N_PTS, 2, REQ).astype(jnp.int32)
        homes = heads[:, 0] * 16 + heads[:, 1]
        owner = homes // PAN_DEV
        relative = (owner // 2 - chip) % CHIPS
        places = jnp.where(owner % 2 == core, relative * PAN_DEV + homes % PAN_DEV, CHIPS * PAN_DEV)
        lanes = jnp.pad(
            jnp.concatenate([places, places], axis=1), ((0, 0), (0, LANE - 2 * REQ)), constant_values=CHIPS * PAN_DEV
        )
        own, own_weights, far1, far2, far3 = spread(places.reshape(-1), mine, mate, lanes)

    with jax.named_scope("sum_over_chips"):
        back = [lax.ppermute(far, "cent", shift(d, 0)) for d, far in ((2, far2), (1, far1), (3, far3))]

    with jax.named_scope("finish"):
        where = me.reshape(1)
        fresh = finish(where, own, own_weights, back, shelf)
        new_centroids, new_loads = place(where, exchange(fresh, "pts"))
    return new_centroids.reshape(CAND * PANEL, WIDTH), new_loads[0:CAND].reshape(CAND * PANEL)


def solution(mesh):
    placed = (P(("pts", "cent"), None), P("cent", None), P("cent"), P(("pts", "cent"), None), P())
    return jax.shard_map(
        local,
        mesh=mesh,
        in_specs=placed,
        out_specs=(P(("cent", "pts"), None), P(("cent", "pts"))),
        check_vma=False,
    )
```

```python
import functools

import jax
import jax.numpy as jnp
from jax import lax
from jax.experimental import pallas as pl
from jax.experimental.pallas import tpu as pltpu
from jax.sharding import PartitionSpec as P

PANEL = 128
GROUP = 1024
CAND = 4
GROUPS_DEV = 2
REQ = CAND * GROUPS_DEV
PAN_DEV = 64
WIDTH = 1024
N_CENT = 8
CHIPS = 4
N_PTS = 16
ROWS = 16
HALF = 512
LANE = 128
TILES = HALF // LANE
SEND_TILES = REQ * TILES + 1
DENSE = PAN_DEV * TILES
CHUNK_TILES = DENSE + 1
LAST_TILES = CAND * TILES + 1

sharpness_divisor = 16.0
evenness_coefficient = 1.0
prior_mass = 1.0

BF16 = jnp.bfloat16
F32 = jnp.float32
MIB = 1 << 20


def params(mib):
    return pltpu.CompilerParams(vmem_limit_bytes=mib * MIB)


def pick_kernel(ids, table, out, sems):
    for n in range(ids.shape[0]):
        pltpu.make_async_copy(table.at[ids[n]], out.at[n], sems.at[n]).start()
    for n in range(ids.shape[0]):
        pltpu.make_async_copy(table.at[ids[n]], out.at[n], sems.at[n]).wait()


def pick_panels(ids, table):
    count = ids.shape[0]
    return pl.pallas_call(
        pick_kernel,
        out_shape=jax.ShapeDtypeStruct((count, PANEL, WIDTH), BF16),
        in_specs=[pl.BlockSpec(memory_space=pltpu.SMEM), pl.BlockSpec(memory_space=pl.ANY)],
        out_specs=pl.BlockSpec(memory_space=pltpu.VMEM),
        scratch_shapes=[pltpu.SemaphoreType.DMA((count,))],
        compiler_params=params(16),
        cost_estimate=pl.CostEstimate(flops=0, bytes_accessed=4 * count * PANEL * WIDTH, transcendentals=0),
    )(ids, table)


def score_kernel(target, points, c0, c1, c2, c3, surcharge, tags, out, centers, shares, marks):
    del target
    group = pl.program_id(0)
    for j, panel in enumerate((c0, c1, c2, c3)):
        centers[j * PANEL : (j + 1) * PANEL, :] = panel[0]
    wide = centers[...].astype(F32)
    squares = jnp.sum(wide * wide, axis=1, keepdims=True)
    bias = squares * (1.0 / sharpness_divisor) + evenness_coefficient * surcharge[0]
    step = 256
    weights = jnp.zeros((CAND * PANEL, LANE), F32)
    for s in range(GROUP // step):
        block = points[s * step : (s + 1) * step, :]
        inner = lax.dot_general(centers[...], block, (((1,), (1,)), ((), ())), preferred_element_type=F32)
        logits = inner * (2.0 / sharpness_divisor) - bias
        highest = jnp.max(logits, axis=0, keepdims=True)
        raised = jnp.exp(logits - highest)
        scale = 1.0 / jnp.sum(raised, axis=0, keepdims=True)
        share = (raised * scale).astype(BF16)
        shares[:, s * step : (s + 1) * step] = share
        rounded = share.astype(F32)
        for part in range(step // LANE):
            weights = weights + rounded[:, part * LANE : (part + 1) * LANE]
    weight = jnp.sum(weights, axis=1, keepdims=True)
    coarse = weight.astype(BF16).astype(F32)
    fine = weight - coarse
    lane = lax.broadcasted_iota(jnp.int32, (PANEL, LANE), 1)

    @pl.when(group == 0)
    def _():
        marks[...] = jnp.broadcast_to(tags[0:1, :], (PANEL, LANE))

    tile = marks[...]
    for j in range(CAND):
        place = group * CAND + j
        rows = slice(j * PANEL, (j + 1) * PANEL)
        tile = jnp.where(lane == place, coarse[rows], tile)
        tile = jnp.where(lane == REQ + place, fine[rows], tile)
    marks[...] = tile

    wide_step = 256
    for s in range(WIDTH // wide_step):
        part = lax.dot_general(
            shares[...], points[:, s * wide_step : (s + 1) * wide_step], (((1,), (0,)), ((), ())),
            preferred_element_type=F32,
        ).astype(BF16)
        for t in range(wide_step // LANE):
            column = s * (wide_step // LANE) + t
            half, tile_at = divmod(column, TILES)
            for j in range(CAND):
                for block_at in range(PANEL // ROWS):
                    row = j * PANEL + block_at * ROWS
                    out[block_at * 2 + half, (group * CAND + j) * TILES + tile_at] = part[
                        row : row + ROWS, t * LANE : (t + 1) * LANE
                    ]

    @pl.when(group == GROUPS_DEV - 1)
    def _():
        last = marks[...].astype(BF16)
        for block_at in range(PANEL // ROWS):
            for half in range(2):
                out[block_at * 2 + half, REQ * TILES] = last[block_at * ROWS : (block_at + 1) * ROWS]


def score(target, points, arrived, surcharge, tags):
    def panel(j):
        return pl.BlockSpec((1, PANEL, WIDTH), lambda g, t: (t[g * CAND + j], 0, 0))

    return pl.pallas_call(
        score_kernel,
        grid_spec=pltpu.PrefetchScalarGridSpec(
            num_scalar_prefetch=1,
            grid=(GROUPS_DEV,),
            in_specs=[
                pl.BlockSpec((GROUP, WIDTH), lambda g, t: (g, 0)),
                panel(0), panel(1), panel(2), panel(3),
                pl.BlockSpec((1, CAND * PANEL, 1), lambda g, t: (g, 0, 0)),
                pl.BlockSpec((ROWS, LANE), lambda g, t: (0, 0)),
            ],
            out_specs=pl.BlockSpec((N_PTS, SEND_TILES, ROWS, LANE), lambda g, t: (0, 0, 0, 0)),
            scratch_shapes=[
                pltpu.VMEM((CAND * PANEL, WIDTH), BF16),
                pltpu.VMEM((CAND * PANEL, GROUP), BF16),
                pltpu.VMEM((PANEL, LANE), F32),
            ],
        ),
        out_shape=jax.ShapeDtypeStruct((N_PTS, SEND_TILES, ROWS, LANE), BF16),
        compiler_params=params(48),
        cost_estimate=pl.CostEstimate(flops=4294967296, bytes_accessed=10 * MIB, transcendentals=1 << 20),
    )(target, points, arrived, arrived, arrived, arrived, surcharge, tags)


def spread_kernel(places, mine, mate, lanes, own, own_weights, out1, out2, out3, total):
    total[...] = jnp.zeros_like(total)
    count = N_PTS * REQ
    for first, source in ((0, mine), (count, mate)):
        def add(s, carry, first=first, source=source):
            for i in range(REQ):
                at = places[first + s * REQ + i] * TILES
                total[pl.ds(at, TILES)] += source[s, i * TILES : (i + 1) * TILES].astype(F32)
            return carry

        lax.fori_loop(0, N_PTS, add, 0)
    panel = lax.broadcasted_iota(jnp.int32, (CHIPS * PAN_DEV, LANE), 0)
    weights = jnp.zeros((ROWS, CHIPS * PAN_DEV), F32)
    for n in range(2 * N_PTS):
        source = mine if n < N_PTS else mate
        chosen = jnp.where(panel == lanes[n : n + 1, :], 1.0, 0.0).astype(BF16)
        weights = weights + lax.dot_general(
            source[n % N_PTS, REQ * TILES], chosen, (((1,), (1,)), ((), ())), preferred_element_type=F32
        )
    own[...] = total[0:DENSE]
    coarse = weights.astype(BF16)
    fine = (weights - coarse.astype(F32)).astype(BF16)
    own_weights[...] = weights[:, 0:LANE]
    for d, out in ((1, out1), (2, out2), (3, out3)):
        out[0:DENSE] = total[d * DENSE : (d + 1) * DENSE].astype(BF16)
        out[DENSE, :, 0:PAN_DEV] = coarse[:, d * PAN_DEV : (d + 1) * PAN_DEV]
        out[DENSE, :, PAN_DEV:LANE] = fine[:, d * PAN_DEV : (d + 1) * PAN_DEV]


def spread(places, mine, mate, lanes):
    vmem = pl.BlockSpec(memory_space=pltpu.VMEM)
    chunk = jax.ShapeDtypeStruct((CHUNK_TILES, ROWS, LANE), BF16)
    return pl.pallas_call(
        spread_kernel,
        in_specs=[pl.BlockSpec(memory_space=pltpu.SMEM), vmem, vmem, vmem],
        out_specs=[vmem] * 5,
        out_shape=[
            jax.ShapeDtypeStruct((DENSE, ROWS, LANE), F32),
            jax.ShapeDtypeStruct((ROWS, LANE), F32),
            chunk, chunk, chunk,
        ],
        scratch_shapes=[pltpu.VMEM((CHIPS * DENSE + TILES, ROWS, LANE), F32)],
        compiler_params=params(48),
        cost_estimate=pl.CostEstimate(flops=1 << 22, bytes_accessed=10 * MIB, transcendentals=0),
    )(places, mine, mate, lanes)


def finish_kernel(me, own, own_weights, in1, in2, in3, old, out):
    del me
    weights = own_weights[:, 0:PAN_DEV]
    for arrived in (in1, in2, in3):
        pair = arrived[DENSE].astype(F32)
        weights = weights + (pair[:, 0:PAN_DEV] + pair[:, PAN_DEV:LANE])
    inverse = 1.0 / (weights + prior_mass)
    for q in range(PAN_DEV):
        scale = jnp.broadcast_to(inverse[:, q : q + 1], (ROWS, LANE))
        for t in range(TILES):
            at = q * TILES + t
            total = own[at] + in1[at].astype(F32) + in2[at].astype(F32) + in3[at].astype(F32)
            previous = old[q, :, t * LANE : (t + 1) * LANE].astype(F32)
            fresh = (total + prior_mass * previous) * scale
            out[q // CAND, (q % CAND) * TILES + t] = fresh.astype(BF16)
    coarse = weights.astype(BF16)
    fine = (weights - coarse.astype(F32)).astype(BF16)
    for p in range(N_PTS):
        out[p, CAND * TILES, :, 0:PAN_DEV] = coarse
        out[p, CAND * TILES, :, PAN_DEV:LANE] = fine


def finish(me, own, own_weights, arrived, table):
    whole = lambda shape: pl.BlockSpec(shape, lambda g, me: (0,) * len(shape))
    chunk = whole((CHUNK_TILES, ROWS, LANE))
    return pl.pallas_call(
        finish_kernel,
        grid_spec=pltpu.PrefetchScalarGridSpec(
            num_scalar_prefetch=1,
            grid=(1,),
            in_specs=[
                whole((DENSE, ROWS, LANE)), whole((ROWS, LANE)), chunk, chunk, chunk,
                pl.BlockSpec((PAN_DEV, ROWS, HALF), lambda g, me: (0, me[0] // 2, me[0] % 2)),
            ],
            out_specs=whole((N_PTS, LAST_TILES, ROWS, LANE)),
        ),
        out_shape=jax.ShapeDtypeStruct((N_PTS, LAST_TILES, ROWS, LANE), BF16),
        compiler_params=params(48),
        cost_estimate=pl.CostEstimate(flops=1 << 22, bytes_accessed=8 * MIB, transcendentals=0),
    )(me, own, own_weights, *arrived, table)


def place_kernel(me, pieces, out, loads):
    for block_at in range(PANEL // ROWS):
        for half in range(2):
            for q in range(CAND):
                for t in range(TILES):
                    column = half * HALF + t * LANE
                    out[q, block_at * ROWS : (block_at + 1) * ROWS, column : column + LANE] = pieces[
                        block_at * 2 + half, q * TILES + t
                    ]
    lane = lax.broadcasted_iota(jnp.int32, (ROWS, LANE), 1)
    row = lax.broadcasted_iota(jnp.int32, (ROWS, LANE), 0)
    wanted = me[0] * CAND + row
    chosen = jnp.where((row < CAND) & (lane % PAN_DEV == wanted), 1.0, 0.0).astype(BF16)
    for block_at in range(PANEL // ROWS):
        pair = pieces[block_at * 2, CAND * TILES]
        part = lax.dot_general(chosen, pair, (((1,), (1,)), ((), ())), preferred_element_type=F32)
        loads[:, block_at * ROWS : (block_at + 1) * ROWS] = part[0:8]


def place(me, pieces):
    vmem = pl.BlockSpec(memory_space=pltpu.VMEM)
    return pl.pallas_call(
        place_kernel,
        in_specs=[pl.BlockSpec(memory_space=pltpu.SMEM), vmem],
        out_specs=[vmem, vmem],
        out_shape=[
            jax.ShapeDtypeStruct((CAND, PANEL, WIDTH), BF16),
            jax.ShapeDtypeStruct((8, PANEL), F32),
        ],
        compiler_params=params(32),
        cost_estimate=pl.CostEstimate(flops=1 << 20, bytes_accessed=2 * MIB, transcendentals=0),
    )(me, pieces)


def shift(dy, dk):
    return [(y * 2 + k, ((y + dy) % CHIPS) * 2 + (k + dk) % 2) for y in range(CHIPS) for k in range(2)]


def exchange(x, axis):
    return lax.all_to_all(x, axis, split_axis=0, concat_axis=0, tiled=True)


def local(points, centroids, prev_loads, candidates, panel_home):
    me = lax.axis_index("pts")
    here = lax.axis_index("cent")
    chip, core = here // 2, here % 2
    shelf = centroids.reshape(PAN_DEV, PANEL, WIDTH)

    with jax.named_scope("requests"):
        wanted_ids = candidates.reshape(REQ)
        slots = jnp.sum(
            jnp.where(wanted_ids[:, None] == jnp.arange(panel_home.shape[0], dtype=jnp.int32), panel_home[None, :], 0),
            axis=1,
        )
        owners, local_ids = slots // PAN_DEV, slots % PAN_DEV
        target = owners * GROUPS_DEV + jnp.arange(REQ, dtype=jnp.int32) // CAND
        spots = jnp.arange(N_CENT * GROUPS_DEV, dtype=jnp.int32)
        wanted = jnp.sum(jnp.where(target[None, :] == spots[:, None], local_ids[None, :], 0), axis=1)
        ask = jnp.zeros((N_CENT, 1, ROWS, LANE), BF16)
        ask = ask.at[:, 0, 0, 0:GROUPS_DEV].set(wanted.reshape(N_CENT, GROUPS_DEV).astype(BF16))
        table = jnp.broadcast_to(
            prev_loads.reshape(1, PAN_DEV // ROWS, ROWS, LANE), (N_CENT, PAN_DEV // ROWS, ROWS, LANE)
        )
        answered = exchange(jnp.concatenate([table, ask], axis=1), "cent")
        asked = answered[:, PAN_DEV // ROWS, 0, 0:GROUPS_DEV].astype(jnp.int32).reshape(-1)

    with jax.named_scope("gather_panels"):
        arrived = exchange(pick_panels(asked, shelf).reshape(N_CENT, GROUPS_DEV, PANEL, WIDTH), "cent")
        arrived = arrived.reshape(N_CENT * GROUPS_DEV, PANEL, WIDTH)

    with jax.named_scope("loads"):
        load_table = answered[:, : PAN_DEV // ROWS].reshape(N_CENT * PAN_DEV, PANEL)
        loads = jnp.take(load_table, slots, axis=0, mode="clip").astype(F32)
        surcharge = jnp.log(loads).reshape(GROUPS_DEV, CAND * PANEL, 1)
        marks = jnp.concatenate([jnp.zeros((2 * REQ,), F32), (slots // 16).astype(F32), (slots % 16).astype(F32)])
        tags = jnp.broadcast_to(jnp.pad(marks, (0, LANE - 4 * REQ)), (ROWS, LANE))

    with jax.named_scope("score"):
        pieces = score(target, points, arrived, surcharge, tags)

    with jax.named_scope("split_pieces"):
        mine = exchange(pieces, "pts")
        mate = lax.ppermute(mine, "cent", shift(0, 1))

    with jax.named_scope("spread"):
        heads = jnp.stack([mine[:, REQ * TILES, 0, 2 * REQ : 4 * REQ], mate[:, REQ * TILES, 0, 2 * REQ : 4 * REQ]])
        heads = heads.reshape(2 * N_PTS, 2, REQ).astype(jnp.int32)
        homes = heads[:, 0] * 16 + heads[:, 1]
        owner = homes // PAN_DEV
        relative = (owner // 2 - chip) % CHIPS
        places = jnp.where(owner % 2 == core, relative * PAN_DEV + homes % PAN_DEV, CHIPS * PAN_DEV)
        lanes = jnp.pad(
            jnp.concatenate([places, places], axis=1), ((0, 0), (0, LANE - 2 * REQ)), constant_values=CHIPS * PAN_DEV
        )
        own, own_weights, far1, far2, far3 = spread(places.reshape(-1), mine, mate, lanes)

    with jax.named_scope("sum_over_chips"):
        back = [lax.ppermute(far, "cent", shift(d, 0)) for d, far in ((2, far2), (1, far1), (3, far3))]

    with jax.named_scope("finish"):
        where = me.reshape(1)
        fresh = finish(where, own, own_weights, back, shelf)
        new_centroids, new_loads = place(where, exchange(fresh, "pts"))
    return new_centroids.reshape(CAND * PANEL, WIDTH), new_loads[0:CAND].reshape(CAND * PANEL)


def solution(mesh):
    placed = (P(("pts", "cent"), None), P("cent", None), P("cent"), P(("pts", "cent"), None), P())
    return jax.shard_map(
        local,
        mesh=mesh,
        in_specs=placed,
        out_specs=(P(("cent", "pts"), None), P(("cent", "pts"))),
        check_vma=False,
    )
```

```python
import functools

import jax
import jax.numpy as jnp
from jax import lax
from jax.experimental import pallas as pl
from jax.experimental.pallas import tpu as pltpu
from jax.sharding import PartitionSpec as P

PANEL = 128
GROUP = 1024
CAND = 4
GROUPS_DEV = 2
REQ = CAND * GROUPS_DEV
PAN_DEV = 64
WIDTH = 1024
N_CENT = 8
CHIPS = 4
N_PTS = 16
SIDE = 4
ROWS = 16
HALF = 512
LANE = 128
TILES = HALF // LANE
PARTS = 2
WIDE = TILES // PARTS
DENSE = PAN_DEV * WIDE

sharpness_divisor = 16.0
evenness_coefficient = 1.0
prior_mass = 1.0

BF16 = jnp.bfloat16
F32 = jnp.float32
MIB = 1 << 20


def params(mib):
    return pltpu.CompilerParams(vmem_limit_bytes=mib * MIB)


def pick_kernel(ids, table, out, held, sems):
    def fetch(n):
        return pltpu.make_async_copy(table.at[ids[n]], held.at[n], sems.at[0, n])

    def put(n):
        return pltpu.make_async_copy(held.at[n], out.at[n], sems.at[1, n])

    for n in range(ids.shape[0]):
        fetch(n).start()
    for n in range(ids.shape[0]):
        fetch(n).wait()
        put(n).start()
    for n in range(ids.shape[0]):
        put(n).wait()


def pick_panels(ids, table):
    count = ids.shape[0]
    return pl.pallas_call(
        pick_kernel,
        out_shape=jax.ShapeDtypeStruct((count, PANEL, WIDTH), BF16),
        in_specs=[pl.BlockSpec(memory_space=pltpu.SMEM), pl.BlockSpec(memory_space=pltpu.HBM)],
        out_specs=pl.BlockSpec(memory_space=pltpu.HBM),
        scratch_shapes=[pltpu.VMEM((count, PANEL, WIDTH), BF16), pltpu.SemaphoreType.DMA((2, count))],
        compiler_params=params(60),
        cost_estimate=pl.CostEstimate(flops=0, bytes_accessed=4 * count * PANEL * WIDTH, transcendentals=0),
    )(ids, table)


def whole(shape):
    return pl.BlockSpec(shape, lambda *_: (0,) * len(shape))


def smem_spec():
    return pl.BlockSpec(memory_space=pltpu.SMEM)


def send_part(h, group, shares, columns, out):
    for half in range(2):
        part = lax.dot_general(
            shares, columns(half), (((1,), (0,)), ((), ())), preferred_element_type=F32
        ).astype(BF16)
        for t in range(WIDE):
            for j in range(CAND):
                for block_at in range(PANEL // ROWS):
                    row = j * PANEL + block_at * ROWS
                    out[block_at * 2 + half, (group * CAND + j) * WIDE + t] = part[
                        row : row + ROWS, t * LANE : (t + 1) * LANE
                    ]


def score_kernel(target, points, c0, c1, c2, c3, surcharge, out, shares, centers, marks):
    del target
    group = pl.program_id(0)
    for j, panel in enumerate((c0, c1, c2, c3)):
        centers[j * PANEL : (j + 1) * PANEL, :] = panel[0]
    wide = centers[...].astype(F32)
    squares = jnp.sum(wide * wide, axis=1, keepdims=True)
    bias = squares * (1.0 / sharpness_divisor) + evenness_coefficient * surcharge[0]
    step = 256
    weights = jnp.zeros((CAND * PANEL, LANE), F32)
    for s in range(GROUP // step):
        block = points[s * step : (s + 1) * step, :]
        inner = lax.dot_general(centers[...], block, (((1,), (1,)), ((), ())), preferred_element_type=F32)
        logits = inner * (2.0 / sharpness_divisor) - bias
        highest = jnp.max(logits, axis=0, keepdims=True)
        raised = jnp.exp(logits - highest)
        scale = 1.0 / jnp.sum(raised, axis=0, keepdims=True)
        share = (raised * scale).astype(BF16)
        shares[0, :, s * step : (s + 1) * step] = share
        rounded = share.astype(F32)
        for part in range(step // LANE):
            weights = weights + rounded[:, part * LANE : (part + 1) * LANE]
    weight = jnp.sum(weights, axis=1, keepdims=True)
    coarse = weight.astype(BF16).astype(F32)
    fine = weight - coarse
    lane = lax.broadcasted_iota(jnp.int32, (PANEL, LANE), 1)

    @pl.when(group == 0)
    def _():
        marks[...] = jnp.zeros_like(marks)

    tile = marks[...]
    for j in range(CAND):
        place = group * CAND + j
        rows = slice(j * PANEL, (j + 1) * PANEL)
        tile = jnp.where(lane == place, coarse[rows], tile)
        tile = jnp.where(lane == REQ + place, fine[rows], tile)
    marks[...] = tile
    send_part(0, group, shares[0], lambda half: points[:, half * HALF : half * HALF + WIDE * LANE], out)

    @pl.when(group == GROUPS_DEV - 1)
    def _():
        last = marks[...].astype(BF16)
        for block_at in range(PANEL // ROWS):
            for half in range(2):
                out[block_at * 2 + half, REQ * WIDE] = last[block_at * ROWS : (block_at + 1) * ROWS]


def score(target, points, arrived, surcharge):
    def panel(j):
        return pl.BlockSpec((1, PANEL, WIDTH), lambda g, t: (t[g * CAND + j], 0, 0))

    tiles = REQ * WIDE + 1
    return pl.pallas_call(
        score_kernel,
        grid_spec=pltpu.PrefetchScalarGridSpec(
            num_scalar_prefetch=1,
            grid=(GROUPS_DEV,),
            in_specs=[
                pl.BlockSpec((GROUP, WIDTH), lambda g, t: (g, 0)),
                panel(0), panel(1), panel(2), panel(3),
                pl.BlockSpec((1, CAND * PANEL, 1), lambda g, t: (g, 0, 0)),
            ],
            out_specs=[
                pl.BlockSpec((N_PTS, tiles, ROWS, LANE), lambda g, t: (0, 0, 0, 0)),
                pl.BlockSpec((1, CAND * PANEL, GROUP), lambda g, t: (g, 0, 0)),
            ],
            scratch_shapes=[pltpu.VMEM((CAND * PANEL, WIDTH), BF16), pltpu.VMEM((PANEL, LANE), F32)],
        ),
        out_shape=[
            jax.ShapeDtypeStruct((N_PTS, tiles, ROWS, LANE), BF16),
            jax.ShapeDtypeStruct((GROUPS_DEV, CAND * PANEL, GROUP), BF16),
        ],
        compiler_params=params(48),
        cost_estimate=pl.CostEstimate(flops=3 << 30, bytes_accessed=10 * MIB, transcendentals=1 << 20),
    )(target, points, arrived, arrived, arrived, arrived, surcharge)


def second_kernel(shares, left, right, out):
    group = pl.program_id(0)
    send_part(1, group, shares[0], lambda half: (left, right)[half][...], out)


def second(shares, points):
    width = WIDE * LANE
    tiles = REQ * WIDE
    return pl.pallas_call(
        second_kernel,
        grid=(GROUPS_DEV,),
        in_specs=[
            pl.BlockSpec((1, CAND * PANEL, GROUP), lambda g: (g, 0, 0)),
            pl.BlockSpec((GROUP, width), lambda g: (g, 1)),
            pl.BlockSpec((GROUP, width), lambda g: (g, HALF // width + 1)),
        ],
        out_specs=pl.BlockSpec((N_PTS, tiles, ROWS, LANE), lambda g: (0, 0, 0, 0)),
        out_shape=jax.ShapeDtypeStruct((N_PTS, tiles, ROWS, LANE), BF16),
        compiler_params=params(48),
        cost_estimate=pl.CostEstimate(flops=1 << 30, bytes_accessed=6 * MIB, transcendentals=0),
    )(shares, points, points)


def spread_kernel(has_weights, places, mine, mate, *refs):
    if has_weights:
        lanes, own, own_weights, out1, out2, out3, total = refs
    else:
        own, out1, out2, out3, total = refs
    total[...] = jnp.zeros_like(total)
    sources = (mine, mate)
    for n, source in enumerate(sources):
        def add(s, carry, n=n, source=source):
            for i in range(REQ):
                at = places[(n * N_PTS + s) * REQ + i] * WIDE
                total[pl.ds(at, WIDE)] += source[s, i * WIDE : (i + 1) * WIDE].astype(F32)
            return carry

        lax.fori_loop(0, N_PTS, add, 0)
    own[...] = total[0:DENSE]
    for d, out in ((1, out1), (2, out2), (3, out3)):
        out[0:DENSE] = total[d * DENSE : (d + 1) * DENSE].astype(BF16)
    if has_weights:
        panel = lax.broadcasted_iota(jnp.int32, (CHIPS * PAN_DEV, LANE), 0)
        weights = jnp.zeros((ROWS, CHIPS * PAN_DEV), F32)
        for n in range(2 * N_PTS):
            chosen = jnp.where(panel == lanes[n : n + 1, :], 1.0, 0.0).astype(BF16)
            weights = weights + lax.dot_general(
                sources[n // N_PTS][n % N_PTS, REQ * WIDE], chosen, (((1,), (1,)), ((), ())),
                preferred_element_type=F32,
            )
        coarse = weights.astype(BF16)
        fine = (weights - coarse.astype(F32)).astype(BF16)
        own_weights[...] = weights[:, 0:LANE]
        for d, out in ((1, out1), (2, out2), (3, out3)):
            out[DENSE, :, 0:PAN_DEV] = coarse[:, d * PAN_DEV : (d + 1) * PAN_DEV]
            out[DENSE, :, PAN_DEV:LANE] = fine[:, d * PAN_DEV : (d + 1) * PAN_DEV]


def spread(places, mine, mate, lanes=None):
    has_weights = lanes is not None
    chunk = jax.ShapeDtypeStruct((DENSE + has_weights, ROWS, LANE), BF16)
    return pl.pallas_call(
        functools.partial(spread_kernel, has_weights),
        grid=(1,),
        in_specs=[smem_spec()] + [whole(mine.shape)] * 2 + [whole((2 * N_PTS, LANE))] * has_weights,
        out_specs=[whole((DENSE, ROWS, LANE))] + [whole((ROWS, LANE))] * has_weights + [whole(chunk.shape)] * 3,
        out_shape=[jax.ShapeDtypeStruct((DENSE, ROWS, LANE), F32)]
        + [jax.ShapeDtypeStruct((ROWS, LANE), F32)] * has_weights
        + [chunk, chunk, chunk],
        scratch_shapes=[pltpu.VMEM((CHIPS * DENSE + WIDE, ROWS, LANE), F32)],
        compiler_params=params(48),
        cost_estimate=pl.CostEstimate(flops=1 << 22, bytes_accessed=5 * MIB, transcendentals=0),
    )(places, mine, mate, *([lanes] if has_weights else []))


def finish_kernel(has_weights, me, own, in1, in2, in3, old, *refs):
    del me
    if has_weights:
        own_weights, out, scales = refs
        weights = own_weights[:, 0:PAN_DEV]
        for arrived in (in1, in2, in3):
            pair = arrived[DENSE].astype(F32)
            weights = weights + (pair[:, 0:PAN_DEV] + pair[:, PAN_DEV:LANE])
        inverse = 1.0 / (weights + prior_mass)
        scales[:, 0:PAN_DEV] = inverse
        coarse = weights.astype(BF16)
        fine = (weights - coarse.astype(F32)).astype(BF16)
        for p in range(N_PTS):
            out[p, CAND * WIDE, :, 0:PAN_DEV] = coarse
            out[p, CAND * WIDE, :, PAN_DEV:LANE] = fine
    else:
        scales, out = refs
        inverse = scales[:, 0:PAN_DEV]
    for q in range(PAN_DEV):
        scale = jnp.broadcast_to(inverse[:, q : q + 1], (ROWS, LANE))
        for t in range(WIDE):
            at = q * WIDE + t
            total = own[at] + in1[at].astype(F32) + in2[at].astype(F32) + in3[at].astype(F32)
            previous = old[q, :, t * LANE : (t + 1) * LANE].astype(F32)
            fresh = (total + prior_mass * previous) * scale
            out[q // CAND, (q % CAND) * WIDE + t] = fresh.astype(BF16)


def finish(h, me, own, arrived, table, weights):
    has_weights = h == 0
    chunk = whole((DENSE + has_weights, ROWS, LANE))
    fresh = (N_PTS, CAND * WIDE + has_weights, ROWS, LANE)
    return pl.pallas_call(
        functools.partial(finish_kernel, has_weights),
        grid_spec=pltpu.PrefetchScalarGridSpec(
            num_scalar_prefetch=1,
            grid=(1,),
            in_specs=[
                whole((DENSE, ROWS, LANE)), chunk, chunk, chunk,
                pl.BlockSpec((PAN_DEV, ROWS, WIDE * LANE), lambda g, me: (0, me[0] // 2, (me[0] % 2) * PARTS + h)),
                whole((ROWS, LANE)),
            ],
            out_specs=[whole(fresh)] + [whole((ROWS, LANE))] * has_weights,
        ),
        out_shape=[jax.ShapeDtypeStruct(fresh, BF16)] + [jax.ShapeDtypeStruct((ROWS, LANE), F32)] * has_weights,
        compiler_params=params(48),
        cost_estimate=pl.CostEstimate(flops=1 << 22, bytes_accessed=4 * MIB, transcendentals=0),
    )(me, own, *arrived, table, weights)


def place_kernel(me, part0, part1, out, loads):
    for h, pieces in enumerate((part0, part1)):
        for block_at in range(PANEL // ROWS):
            for half in range(2):
                for q in range(CAND):
                    for t in range(WIDE):
                        column = half * HALF + (h * WIDE + t) * LANE
                        out[q, block_at * ROWS : (block_at + 1) * ROWS, column : column + LANE] = pieces[
                            block_at * 2 + half, q * WIDE + t
                        ]
    lane = lax.broadcasted_iota(jnp.int32, (ROWS, LANE), 1)
    row = lax.broadcasted_iota(jnp.int32, (ROWS, LANE), 0)
    wanted = me[0] * CAND + row
    chosen = jnp.where((row < CAND) & (lane % PAN_DEV == wanted), 1.0, 0.0).astype(BF16)
    for block_at in range(PANEL // ROWS):
        pair = part0[block_at * 2, CAND * WIDE]
        part = lax.dot_general(chosen, pair, (((1,), (1,)), ((), ())), preferred_element_type=F32)
        loads[:, block_at * ROWS : (block_at + 1) * ROWS] = part[0:8]


def place(me, part0, part1):
    return pl.pallas_call(
        place_kernel,
        grid=(1,),
        in_specs=[smem_spec(), whole(part0.shape), whole(part1.shape)],
        out_specs=[whole((CAND, PANEL, WIDTH)), whole((8, PANEL))],
        out_shape=[
            jax.ShapeDtypeStruct((CAND, PANEL, WIDTH), BF16),
            jax.ShapeDtypeStruct((8, PANEL), F32),
        ],
        compiler_params=params(32),
        cost_estimate=pl.CostEstimate(flops=1 << 20, bytes_accessed=2 * MIB, transcendentals=0),
    )(me, part0, part1)


def shift(dy, dk):
    return [(y * 2 + k, ((y + dy) % CHIPS) * 2 + (k + dk) % 2) for y in range(CHIPS) for k in range(2)]


def spread_out(x, place, dz, dx):
    held = [x]
    for d in range(1, SIDE):
        pairs = [
            (ix * SIDE + iz, (ix + d * dx) % SIDE * SIDE + (iz + d * dz) % SIDE)
            for ix in range(SIDE)
            for iz in range(SIDE)
        ]
        held.append(lax.ppermute(x, "pts", pairs))
    held = jnp.stack(held)
    at = (place - jnp.arange(SIDE, dtype=jnp.int32)) % SIDE
    return jnp.stack([jnp.sum(jnp.where((at == n).reshape((SIDE,) + (1,) * x.ndim), held, 0), axis=0) for n in range(SIDE)])


def exchange(x, axis):
    return lax.all_to_all(x, axis, split_axis=0, concat_axis=0, tiled=True)


def local(points, centroids, prev_loads, candidates, panel_home):
    me = lax.axis_index("pts")
    here = lax.axis_index("cent")
    chip, core = here // 2, here % 2
    shelf = centroids.reshape(PAN_DEV, PANEL, WIDTH)

    with jax.named_scope("requests"):
        wanted_ids = candidates.reshape(REQ)
        slots = jnp.sum(
            jnp.where(wanted_ids[:, None] == jnp.arange(panel_home.shape[0], dtype=jnp.int32), panel_home[None, :], 0),
            axis=1,
        )
        owners, local_ids = slots // PAN_DEV, slots % PAN_DEV
        target = owners * GROUPS_DEV + jnp.arange(REQ, dtype=jnp.int32) // CAND
        spots = jnp.arange(N_CENT * GROUPS_DEV, dtype=jnp.int32)
        wanted = jnp.sum(jnp.where(target[None, :] == spots[:, None], local_ids[None, :], 0), axis=1)
        ask = jnp.stack(
            [
                jnp.pad(wanted.reshape(N_CENT, GROUPS_DEV), ((0, 0), (0, LANE - GROUPS_DEV))),
                jnp.broadcast_to(jnp.pad(owners, (0, LANE - REQ)), (N_CENT, LANE)),
                jnp.broadcast_to(jnp.pad(local_ids, (0, LANE - REQ)), (N_CENT, LANE)),
            ],
            axis=1,
        ).astype(BF16)
        ask = jnp.pad(ask, ((0, 0), (0, ROWS - 3), (0, 0))).reshape(N_CENT, 1, ROWS, LANE)
        table = jnp.broadcast_to(
            prev_loads.reshape(1, PAN_DEV // ROWS, ROWS, LANE), (N_CENT, PAN_DEV // ROWS, ROWS, LANE)
        )
        answered = exchange(jnp.concatenate([table, ask], axis=1), "cent")
        asked = answered[:, PAN_DEV // ROWS, 0, 0:GROUPS_DEV].astype(jnp.int32).reshape(-1)

    with jax.named_scope("gather_panels"):
        arrived = exchange(pick_panels(asked, shelf).reshape(N_CENT, GROUPS_DEV, PANEL, WIDTH), "cent")
        arrived = arrived.reshape(N_CENT * GROUPS_DEV, PANEL, WIDTH)

    with jax.named_scope("all_requests"):
        ring = answered[:, PAN_DEV // ROWS, 1:3, 0:REQ].astype(jnp.int32)
        ring = ring[:, 0] * PAN_DEV + ring[:, 1]
        line = spread_out(ring, me % SIDE, 1, 0)
        everyone = spread_out(line, me // SIDE, 0, 1).reshape(N_PTS, N_CENT, REQ)
        pair = jnp.stack(
            [lax.dynamic_index_in_dim(everyone, at, 1, keepdims=False) for at in (here, chip * 2 + 1 - core)]
        ).reshape(2 * N_PTS, REQ)
        owner = pair // PAN_DEV
        relative = (owner // 2 - chip) % CHIPS
        places = jnp.where(owner % 2 == core, relative * PAN_DEV + pair % PAN_DEV, CHIPS * PAN_DEV)
        lanes = jnp.pad(
            jnp.concatenate([places, places], axis=1), ((0, 0), (0, LANE - 2 * REQ)), constant_values=CHIPS * PAN_DEV
        )
        places = places.reshape(-1)
        target, places, lanes = lax.optimization_barrier((target, places, lanes))

    with jax.named_scope("loads"):
        load_table = answered[:, : PAN_DEV // ROWS].reshape(N_CENT * PAN_DEV, PANEL)
        loads = jnp.take(load_table, slots, axis=0, mode="clip").astype(F32)
        surcharge = jnp.log(loads).reshape(GROUPS_DEV, CAND * PANEL, 1)

    with jax.named_scope("score"):
        pieces0, shares = score(target, points, arrived, surcharge)
        pieces1 = second(shares, points)

    where = me.reshape(1)
    tie = lax.optimization_barrier
    with jax.named_scope("split_pieces"):
        mine0 = exchange(pieces0, "pts")
        mine0, pieces1 = tie((mine0, pieces1))
        mine1 = exchange(pieces1, "pts")
        mate0 = lax.ppermute(mine0, "cent", shift(0, 1))
    with jax.named_scope("spread"):
        own0, weights, *far0 = spread(places, mine0, mate0, lanes)
    with jax.named_scope("sum_over_chips"):
        back0 = [lax.ppermute(far0[d - 1], "cent", shift(d, 0)) for d in (2, 1, 3)]
    with jax.named_scope("split_pieces"):
        mine1, back0 = tie((mine1, back0))
        mate1 = lax.ppermute(mine1, "cent", shift(0, 1))
    with jax.named_scope("spread"):
        own1, *far1 = spread(places, mine1, mate1)
    with jax.named_scope("sum_over_chips"):
        back1 = [lax.ppermute(far1[d - 1], "cent", shift(d, 0)) for d in (2, 1, 3)]
    with jax.named_scope("finish"):
        own0, own1 = tie((own0, own1))
        fresh0, scales = finish(0, where, own0, back0, shelf, weights)
        done0 = exchange(fresh0, "pts")
        own1, done0 = tie((own1, done0))
        fresh1, = finish(1, where, own1, back1, shelf, scales)
        done1 = exchange(fresh1, "pts")
    with jax.named_scope("place"):
        new_centroids, new_loads = place(where, done0, done1)
    return new_centroids.reshape(CAND * PANEL, WIDTH), new_loads[0:CAND].reshape(CAND * PANEL)


def solution(mesh):
    placed = (P(("pts", "cent"), None), P("cent", None), P("cent"), P(("pts", "cent"), None), P())
    return jax.shard_map(
        local,
        mesh=mesh,
        in_specs=placed,
        out_specs=(P(("cent", "pts"), None), P(("cent", "pts"))),
        check_vma=False,
    )
```

```python
import functools

import jax
import jax.numpy as jnp
from jax import lax
from jax.experimental import pallas as pl
from jax.experimental.pallas import tpu as pltpu
from jax.sharding import PartitionSpec as P

PANEL = 128
GROUP = 1024
CAND = 4
GROUPS_DEV = 2
REQ = CAND * GROUPS_DEV
PAN_DEV = 64
WIDTH = 1024
N_CENT = 8
CHIPS = 4
N_PTS = 16
SIDE = 4
ROWS = 16
HALF = 512
LANE = 128
TILES = HALF // LANE
SEND_TILES = REQ * TILES + 1
DENSE = PAN_DEV * TILES
LISTED = 36

sharpness_divisor = 16.0
evenness_coefficient = 1.0
prior_mass = 1.0

BF16 = jnp.bfloat16
F32 = jnp.float32
MIB = 1 << 20


def params(mib):
    return pltpu.CompilerParams(vmem_limit_bytes=mib * MIB)


def pick_kernel(ids, table, out, held, sems):
    def fetch(n):
        return pltpu.make_async_copy(table.at[ids[n]], held.at[n], sems.at[0, n])

    def put(n):
        return pltpu.make_async_copy(held.at[n], out.at[n], sems.at[1, n])

    for n in range(ids.shape[0]):
        fetch(n).start()
    for n in range(ids.shape[0]):
        fetch(n).wait()
        put(n).start()
    for n in range(ids.shape[0]):
        put(n).wait()


def pick_panels(ids, table):
    count = ids.shape[0]
    return pl.pallas_call(
        pick_kernel,
        out_shape=jax.ShapeDtypeStruct((count, PANEL, WIDTH), BF16),
        in_specs=[pl.BlockSpec(memory_space=pltpu.SMEM), pl.BlockSpec(memory_space=pltpu.HBM)],
        out_specs=pl.BlockSpec(memory_space=pltpu.HBM),
        scratch_shapes=[pltpu.VMEM((count, PANEL, WIDTH), BF16), pltpu.SemaphoreType.DMA((2, count))],
        compiler_params=params(60),
        cost_estimate=pl.CostEstimate(flops=0, bytes_accessed=4 * count * PANEL * WIDTH, transcendentals=0),
    )(ids, table)


def whole(shape):
    return pl.BlockSpec(shape, lambda *_: (0,) * len(shape))


def smem_spec():
    return pl.BlockSpec(memory_space=pltpu.SMEM)


def score_kernel(target, points, c0, c1, c2, c3, surcharge, out, centers, shares, marks):
    del target
    group = pl.program_id(0)
    for j, panel in enumerate((c0, c1, c2, c3)):
        centers[j * PANEL : (j + 1) * PANEL, :] = panel[0]
    wide = centers[...].astype(F32)
    squares = jnp.sum(wide * wide, axis=1, keepdims=True)
    bias = squares * (1.0 / sharpness_divisor) + evenness_coefficient * surcharge[0]
    step = 256
    weights = jnp.zeros((CAND * PANEL, LANE), F32)
    for s in range(GROUP // step):
        block = points[s * step : (s + 1) * step, :]
        inner = lax.dot_general(centers[...], block, (((1,), (1,)), ((), ())), preferred_element_type=F32)
        logits = inner * (2.0 / sharpness_divisor) - bias
        highest = jnp.max(logits, axis=0, keepdims=True)
        raised = jnp.exp(logits - highest)
        scale = 1.0 / jnp.sum(raised, axis=0, keepdims=True)
        share = (raised * scale).astype(BF16)
        shares[:, s * step : (s + 1) * step] = share
        rounded = share.astype(F32)
        for part in range(step // LANE):
            weights = weights + rounded[:, part * LANE : (part + 1) * LANE]
    weight = jnp.sum(weights, axis=1, keepdims=True)
    coarse = weight.astype(BF16).astype(F32)
    fine = weight - coarse
    lane = lax.broadcasted_iota(jnp.int32, (PANEL, LANE), 1)

    @pl.when(group == 0)
    def _():
        marks[...] = jnp.zeros_like(marks)

    tile = marks[...]
    for j in range(CAND):
        place = group * CAND + j
        rows = slice(j * PANEL, (j + 1) * PANEL)
        tile = jnp.where(lane == place, coarse[rows], tile)
        tile = jnp.where(lane == REQ + place, fine[rows], tile)
    marks[...] = tile

    wide_step = 256
    for s in range(WIDTH // wide_step):
        part = lax.dot_general(
            shares[...], points[:, s * wide_step : (s + 1) * wide_step], (((1,), (0,)), ((), ())),
            preferred_element_type=F32,
        ).astype(BF16)
        for t in range(wide_step // LANE):
            column = s * (wide_step // LANE) + t
            half, tile_at = divmod(column, TILES)
            for j in range(CAND):
                for block_at in range(PANEL // ROWS):
                    row = j * PANEL + block_at * ROWS
                    out[block_at * 2 + half, (group * CAND + j) * TILES + tile_at] = part[
                        row : row + ROWS, t * LANE : (t + 1) * LANE
                    ]

    @pl.when(group == GROUPS_DEV - 1)
    def _():
        last = marks[...].astype(BF16)
        for block_at in range(PANEL // ROWS):
            for half in range(2):
                out[block_at * 2 + half, REQ * TILES] = last[block_at * ROWS : (block_at + 1) * ROWS]


def score(target, points, arrived, surcharge):
    def panel(j):
        return pl.BlockSpec((1, PANEL, WIDTH), lambda g, t: (t[g * CAND + j], 0, 0))

    return pl.pallas_call(
        score_kernel,
        grid_spec=pltpu.PrefetchScalarGridSpec(
            num_scalar_prefetch=1,
            grid=(GROUPS_DEV,),
            in_specs=[
                pl.BlockSpec((GROUP, WIDTH), lambda g, t: (g, 0)),
                panel(0), panel(1), panel(2), panel(3),
                pl.BlockSpec((1, CAND * PANEL, 1), lambda g, t: (g, 0, 0)),
            ],
            out_specs=pl.BlockSpec((N_PTS, SEND_TILES, ROWS, LANE), lambda g, t: (0, 0, 0, 0)),
            scratch_shapes=[
                pltpu.VMEM((CAND * PANEL, WIDTH), BF16),
                pltpu.VMEM((CAND * PANEL, GROUP), BF16),
                pltpu.VMEM((PANEL, LANE), F32),
            ],
        ),
        out_shape=jax.ShapeDtypeStruct((N_PTS, SEND_TILES, ROWS, LANE), BF16),
        compiler_params=params(48),
        cost_estimate=pl.CostEstimate(flops=4294967296, bytes_accessed=10 * MIB, transcendentals=1 << 20),
    )(target, points, arrived, arrived, arrived, arrived, surcharge)


def spread_kernel(rows, places, mine, mate, lanes, own, own_weights, out1, out2, out3, total):
    total[...] = jnp.zeros_like(total)
    sources = (mine, mate)
    for n, source in enumerate(sources):
        def add(s, carry, n=n, source=source):
            for i in range(REQ):
                at = places[(n * N_PTS + s) * REQ + i] * TILES
                total[pl.ds(at, TILES)] += source[s, i * TILES : (i + 1) * TILES].astype(F32)
            return carry

        lax.fori_loop(0, N_PTS, add, 0)
    panel = lax.broadcasted_iota(jnp.int32, (CHIPS * PAN_DEV, LANE), 0)
    weights = jnp.zeros((ROWS, CHIPS * PAN_DEV), F32)
    for n in range(2 * N_PTS):
        chosen = jnp.where(panel == lanes[n : n + 1, :], 1.0, 0.0).astype(BF16)
        weights = weights + lax.dot_general(
            sources[n // N_PTS][n % N_PTS, REQ * TILES], chosen, (((1,), (1,)), ((), ())),
            preferred_element_type=F32,
        )
    own[...] = total[0:DENSE]
    coarse = weights.astype(BF16)
    fine = (weights - coarse.astype(F32)).astype(BF16)
    own_weights[...] = weights[:, 0:LANE]
    for d, out in ((1, out1), (2, out2), (3, out3)):
        first = DENSE + (d - 1) * rows * TILES
        out[0 : rows * TILES] = total[first : first + rows * TILES].astype(BF16)
        out[rows * TILES, :, 0:PAN_DEV] = coarse[:, d * PAN_DEV : (d + 1) * PAN_DEV]
        out[rows * TILES, :, PAN_DEV:LANE] = fine[:, d * PAN_DEV : (d + 1) * PAN_DEV]


def spread(rows, places, mine, mate, lanes):
    chunk = jax.ShapeDtypeStruct((rows * TILES + 1, ROWS, LANE), BF16)
    return pl.pallas_call(
        functools.partial(spread_kernel, rows),
        grid=(1,),
        in_specs=[smem_spec()] + [whole(mine.shape)] * 2 + [whole((2 * N_PTS, LANE))],
        out_specs=[whole((DENSE, ROWS, LANE)), whole((ROWS, LANE))] + [whole(chunk.shape)] * 3,
        out_shape=[
            jax.ShapeDtypeStruct((DENSE, ROWS, LANE), F32), jax.ShapeDtypeStruct((ROWS, LANE), F32),
            chunk, chunk, chunk,
        ],
        scratch_shapes=[pltpu.VMEM(((PAN_DEV + 3 * rows + 1) * TILES, ROWS, LANE), F32)],
        compiler_params=params(48),
        cost_estimate=pl.CostEstimate(flops=1 << 22, bytes_accessed=8 * MIB, transcendentals=0),
    )(places, mine, mate, lanes)


def finish_kernel(rows, numbers, own, own_weights, in1, in2, in3, lanes, old, out, total):
    weights = own_weights[:, 0:PAN_DEV]
    panel = lax.broadcasted_iota(jnp.int32, (PAN_DEV, LANE), 0)
    total[...] = own[...]
    for d, arrived in enumerate((in1, in2, in3)):
        chosen = jnp.where(panel == lanes[d : d + 1, :], 1.0, 0.0).astype(BF16)
        weights = weights + lax.dot_general(
            arrived[rows * TILES], chosen, (((1,), (1,)), ((), ())), preferred_element_type=F32
        )
        first = 4 + d * rows

        def add(n, carry, arrived=arrived, first=first):
            at = numbers[first + n] * TILES
            total[pl.ds(at, TILES)] += arrived[pl.ds(n * TILES, TILES)].astype(F32)
            return carry

        lax.fori_loop(0, numbers[1 + d], add, 0)
    inverse = 1.0 / (weights + prior_mass)
    for q in range(PAN_DEV):
        scale = jnp.broadcast_to(inverse[:, q : q + 1], (ROWS, LANE))
        for t in range(TILES):
            previous = old[q, :, t * LANE : (t + 1) * LANE].astype(F32)
            fresh = (total[q * TILES + t] + prior_mass * previous) * scale
            out[q // CAND, (q % CAND) * TILES + t] = fresh.astype(BF16)
    coarse = weights.astype(BF16)
    fine = (weights - coarse.astype(F32)).astype(BF16)
    for p in range(N_PTS):
        out[p, CAND * TILES, :, 0:PAN_DEV] = coarse
        out[p, CAND * TILES, :, PAN_DEV:LANE] = fine


def finish(rows, numbers, own, own_weights, arrived, lanes, table):
    chunk = whole((rows * TILES + 1, ROWS, LANE))
    fresh = (N_PTS, CAND * TILES + 1, ROWS, LANE)
    return pl.pallas_call(
        functools.partial(finish_kernel, rows),
        grid_spec=pltpu.PrefetchScalarGridSpec(
            num_scalar_prefetch=1,
            grid=(1,),
            in_specs=[
                whole((DENSE, ROWS, LANE)), whole((ROWS, LANE)), chunk, chunk, chunk, whole((CHIPS - 1, LANE)),
                pl.BlockSpec((PAN_DEV, ROWS, HALF), lambda g, n: (0, n[0] // 2, n[0] % 2)),
            ],
            out_specs=whole(fresh),
            scratch_shapes=[pltpu.VMEM((DENSE, ROWS, LANE), F32)],
        ),
        out_shape=jax.ShapeDtypeStruct(fresh, BF16),
        compiler_params=params(48),
        cost_estimate=pl.CostEstimate(flops=1 << 22, bytes_accessed=6 * MIB, transcendentals=0),
    )(numbers, own, own_weights, *arrived, lanes, table)


def place_kernel(me, pieces, out, loads):
    for block_at in range(PANEL // ROWS):
        for half in range(2):
            for q in range(CAND):
                for t in range(TILES):
                    column = half * HALF + t * LANE
                    out[q, block_at * ROWS : (block_at + 1) * ROWS, column : column + LANE] = pieces[
                        block_at * 2 + half, q * TILES + t
                    ]
    lane = lax.broadcasted_iota(jnp.int32, (ROWS, LANE), 1)
    row = lax.broadcasted_iota(jnp.int32, (ROWS, LANE), 0)
    wanted = me[0] * CAND + row
    chosen = jnp.where((row < CAND) & (lane % PAN_DEV == wanted), 1.0, 0.0).astype(BF16)
    for block_at in range(PANEL // ROWS):
        pair = pieces[block_at * 2, CAND * TILES]
        part = lax.dot_general(chosen, pair, (((1,), (1,)), ((), ())), preferred_element_type=F32)
        loads[:, block_at * ROWS : (block_at + 1) * ROWS] = part[0:8]


def place(me, pieces):
    return pl.pallas_call(
        place_kernel,
        grid=(1,),
        in_specs=[smem_spec(), whole(pieces.shape)],
        out_specs=[whole((CAND, PANEL, WIDTH)), whole((8, PANEL))],
        out_shape=[
            jax.ShapeDtypeStruct((CAND, PANEL, WIDTH), BF16),
            jax.ShapeDtypeStruct((8, PANEL), F32),
        ],
        compiler_params=params(32),
        cost_estimate=pl.CostEstimate(flops=1 << 20, bytes_accessed=2 * MIB, transcendentals=0),
    )(me, pieces)


def shift(dy, dk):
    return [(y * 2 + k, ((y + dy) % CHIPS) * 2 + (k + dk) % 2) for y in range(CHIPS) for k in range(2)]


def spread_out(x, place, dz, dx):
    held = [x]
    for d in range(1, SIDE):
        pairs = [
            (ix * SIDE + iz, (ix + d * dx) % SIDE * SIDE + (iz + d * dz) % SIDE)
            for ix in range(SIDE)
            for iz in range(SIDE)
        ]
        held.append(lax.ppermute(x, "pts", pairs))
    held = jnp.stack(held)
    at = (place - jnp.arange(SIDE, dtype=jnp.int32)) % SIDE
    return jnp.stack([jnp.sum(jnp.where((at == n).reshape((SIDE,) + (1,) * x.ndim), held, 0), axis=0) for n in range(SIDE)])


def exchange(x, axis):
    return lax.all_to_all(x, axis, split_axis=0, concat_axis=0, tiled=True)


def local(points, centroids, prev_loads, candidates, panel_home):
    me = lax.axis_index("pts")
    here = lax.axis_index("cent")
    chip, core = here // 2, here % 2
    shelf = centroids.reshape(PAN_DEV, PANEL, WIDTH)

    with jax.named_scope("requests"):
        wanted_ids = candidates.reshape(REQ)
        slots = jnp.sum(
            jnp.where(wanted_ids[:, None] == jnp.arange(panel_home.shape[0], dtype=jnp.int32), panel_home[None, :], 0),
            axis=1,
        )
        owners, local_ids = slots // PAN_DEV, slots % PAN_DEV
        target = owners * GROUPS_DEV + jnp.arange(REQ, dtype=jnp.int32) // CAND
        spots = jnp.arange(N_CENT * GROUPS_DEV, dtype=jnp.int32)
        wanted = jnp.sum(jnp.where(target[None, :] == spots[:, None], local_ids[None, :], 0), axis=1)
        ask = jnp.stack(
            [
                jnp.pad(wanted.reshape(N_CENT, GROUPS_DEV), ((0, 0), (0, LANE - GROUPS_DEV))),
                jnp.broadcast_to(jnp.pad(owners, (0, LANE - REQ)), (N_CENT, LANE)),
                jnp.broadcast_to(jnp.pad(local_ids, (0, LANE - REQ)), (N_CENT, LANE)),
            ],
            axis=1,
        ).astype(BF16)
        ask = jnp.pad(ask, ((0, 0), (0, ROWS - 3), (0, 0))).reshape(N_CENT, 1, ROWS, LANE)
        table = jnp.broadcast_to(
            prev_loads.reshape(1, PAN_DEV // ROWS, ROWS, LANE), (N_CENT, PAN_DEV // ROWS, ROWS, LANE)
        )
        answered = exchange(jnp.concatenate([table, ask], axis=1), "cent")
        asked = answered[:, PAN_DEV // ROWS, 0, 0:GROUPS_DEV].astype(jnp.int32).reshape(-1)

    with jax.named_scope("gather_panels"):
        arrived = exchange(pick_panels(asked, shelf).reshape(N_CENT, GROUPS_DEV, PANEL, WIDTH), "cent")
        arrived = arrived.reshape(N_CENT * GROUPS_DEV, PANEL, WIDTH)

    with jax.named_scope("all_requests"):
        ring = answered[:, PAN_DEV // ROWS, 1:3, 0:REQ].astype(jnp.int32)
        ring = ring[:, 0] * PAN_DEV + ring[:, 1]
        line = spread_out(ring, me % SIDE, 1, 0)
        everyone = spread_out(line, me // SIDE, 0, 1).reshape(N_PTS, N_CENT, REQ)
        numbers = jnp.arange(N_CENT * PAN_DEV, dtype=jnp.int32)
        by_chip = jnp.transpose(everyone.reshape(N_PTS, CHIPS, 2 * REQ), (1, 0, 2)).reshape(CHIPS, -1)
        asked_by = jnp.any(by_chip[:, :, None] == numbers, axis=1).reshape(CHIPS, N_CENT, PAN_DEV)
        below = jnp.arange(PAN_DEV)[:, None] < jnp.arange(PAN_DEV)[None, :]
        ranks = lax.dot_general(
            asked_by.astype(BF16), below.astype(BF16), (((2,), (0,)), ((), ())), preferred_element_type=F32
        ).astype(jnp.int32)
        lengths = jnp.sum(asked_by.astype(jnp.int32), axis=2)
        off_chip = jnp.arange(N_CENT)[None, :] // 2 != jnp.arange(CHIPS)[:, None]
        too_long = jnp.any(off_chip & (lengths > LISTED))

        pair = jnp.stack(
            [lax.dynamic_index_in_dim(everyone, at, 1, keepdims=False) for at in (here, chip * 2 + 1 - core)]
        ).reshape(2 * N_PTS, REQ)
        owner = pair // PAN_DEV
        relative = (owner // 2 - chip) % CHIPS
        my_ranks = lax.dynamic_index_in_dim(ranks, chip, 0, keepdims=False).reshape(-1)
        rank = jnp.sum(jnp.where(pair[:, :, None] == numbers, my_ranks, 0), axis=2)
        ours = owner % 2 == core

        def sender(rows, rank):
            at = jnp.where(relative == 0, pair % PAN_DEV, rank)
            known = ours & ((relative == 0) | (rank < rows))
            first = jnp.where(relative == 0, 0, PAN_DEV + (relative - 1) * rows)
            places = jnp.where(known, first + at, PAN_DEV + 3 * rows).reshape(-1)
            lane = jnp.where(known, relative * PAN_DEV + at, CHIPS * PAN_DEV)
            lanes = jnp.pad(
                jnp.concatenate([lane, lane], axis=1), ((0, 0), (0, LANE - 2 * REQ)), constant_values=CHIPS * PAN_DEV
            )
            return places, lanes

        def receiver(rows, count, panels):
            numbers = jnp.concatenate([me.reshape(1), count, panels[:, :rows].reshape(-1)])
            lane = jnp.where(jnp.arange(PAN_DEV) < jnp.minimum(count, rows)[:, None], panels, PAN_DEV)
            return numbers, jnp.concatenate([lane, lane], axis=1)

        behind = [(chip - d) % CHIPS for d in range(1, CHIPS)]
        pick = lambda x, y: lax.dynamic_index_in_dim(lax.dynamic_index_in_dim(x, y, 0, False), here, 0, False)
        named = jnp.stack([pick(asked_by, y) for y in behind])
        order = jnp.stack([pick(ranks, y) for y in behind])
        spots = jnp.arange(PAN_DEV, dtype=jnp.int32)
        listed = jnp.sum(
            jnp.where(named[:, None, :] & (order[:, None, :] == spots[None, :, None]), spots, 0), axis=2
        )
        count = jnp.minimum(jnp.sum(named.astype(jnp.int32), axis=1), LISTED)
        short = sender(LISTED, rank) + receiver(LISTED, count, listed)
        target, too_long, short = lax.optimization_barrier((target, too_long, short))

    with jax.named_scope("loads"):
        load_table = answered[:, : PAN_DEV // ROWS].reshape(N_CENT * PAN_DEV, PANEL)
        loads = jnp.take(load_table, slots, axis=0, mode="clip").astype(F32)
        surcharge = jnp.log(loads).reshape(GROUPS_DEV, CAND * PANEL, 1)

    with jax.named_scope("score"):
        pieces = score(target, points, arrived, surcharge)

    with jax.named_scope("split_pieces"):
        mine = exchange(pieces, "pts")
        mate = lax.ppermute(mine, "cent", shift(0, 1))

    def sum_over_chips(rows, places, lanes, numbers, back_lanes):
        own, own_weights, *far = spread(rows, places, mine, mate, lanes)
        back = [lax.ppermute(far[d - 1], "cent", shift(d, 0)) for d in range(1, CHIPS)]
        return finish(rows, numbers, own, own_weights, back, back_lanes, shelf)

    def send_all():
        everything = jnp.broadcast_to(spots, (CHIPS - 1, PAN_DEV))
        count = jnp.full((CHIPS - 1,), PAN_DEV, jnp.int32)
        return sum_over_chips(PAN_DEV, *sender(PAN_DEV, pair % PAN_DEV), *receiver(PAN_DEV, count, everything))

    with jax.named_scope("sum_over_chips"):
        fresh = lax.cond(too_long, send_all, lambda: sum_over_chips(LISTED, *short))

    with jax.named_scope("place"):
        new_centroids, new_loads = place(me.reshape(1), exchange(fresh, "pts"))
    return new_centroids.reshape(CAND * PANEL, WIDTH), new_loads[0:CAND].reshape(CAND * PANEL)


def solution(mesh):
    placed = (P(("pts", "cent"), None), P("cent", None), P("cent"), P(("pts", "cent"), None), P())
    return jax.shard_map(
        local,
        mesh=mesh,
        in_specs=placed,
        out_specs=(P(("cent", "pts"), None), P(("cent", "pts"))),
        check_vma=False,
    )
```

```python
import functools

import jax
import jax.numpy as jnp
from jax import lax
from jax.experimental import pallas as pl
from jax.experimental.pallas import tpu as pltpu
from jax.sharding import PartitionSpec as P

PANEL = 128
GROUP = 1024
CAND = 4
GROUPS_DEV = 2
REQ = CAND * GROUPS_DEV
PAN_DEV = 64
WIDTH = 1024
N_CENT = 8
CHIPS = 4
N_PTS = 16
SIDE = 4
ROWS = 16
HALF = 512
LANE = 128
TILES = HALF // LANE
SEND_TILES = CAND * TILES + 1
DENSE = PAN_DEV * TILES
LOAD_TILES = PAN_DEV // ROWS
LISTED = 24

sharpness_divisor = 16.0
evenness_coefficient = 1.0
prior_mass = 1.0

BF16 = jnp.bfloat16
F32 = jnp.float32
MIB = 1 << 20


def params(mib):
    return pltpu.CompilerParams(vmem_limit_bytes=mib * MIB)


def whole(shape):
    return pl.BlockSpec(shape, lambda *_: (0,) * len(shape))


def smem_spec():
    return pl.BlockSpec(memory_space=pltpu.SMEM)


def hbm_spec():
    return pl.BlockSpec(memory_space=pltpu.HBM)


def ask_kernel(candidates, home, loads, out):
    row = lax.broadcasted_iota(jnp.int32, (ROWS, LANE), 0)
    lane = lax.broadcasted_iota(jnp.int32, (ROWS, LANE), 1)
    slots = [home[candidates[n // CAND, n % CAND]] for n in range(REQ)]
    common = jnp.zeros((ROWS, LANE), F32)
    for n, slot in enumerate(slots):
        common = jnp.where((row == 1) & (lane == n), (slot // PAN_DEV).astype(F32), common)
        common = jnp.where((row == 2) & (lane == n), (slot % PAN_DEV).astype(F32), common)
    for o in range(N_CENT):
        tile = common
        for n, slot in enumerate(slots):
            here = jnp.where(slot // PAN_DEV == o, slot % PAN_DEV, 0).astype(F32)
            tile = jnp.where((row == 0) & (lane == n // CAND), tile + here, tile)
        for t in range(LOAD_TILES):
            out[o, t] = loads[t * ROWS : (t + 1) * ROWS]
        out[o, LOAD_TILES] = tile.astype(BF16)


def ask(candidates, home, loads):
    shape = (N_CENT, LOAD_TILES + 1, ROWS, LANE)
    return pl.pallas_call(
        ask_kernel,
        grid=(1,),
        in_specs=[smem_spec(), smem_spec(), whole((PAN_DEV, LANE))],
        out_specs=whole(shape),
        out_shape=jax.ShapeDtypeStruct(shape, BF16),
        compiler_params=params(8),
        cost_estimate=pl.CostEstimate(flops=1 << 16, bytes_accessed=1 << 18, transcendentals=0),
    )(candidates, home, loads)


def pick_kernel(group, ids, place, table, *refs):
    *outs, held, sems = refs

    def fetch(n):
        if len(outs) == 1:
            reader = n
        else:
            reader = (place[0] // 2 + n // 2) % CHIPS * 2 + (place[0] + n) % 2
        return pltpu.make_async_copy(table.at[ids[reader * GROUPS_DEV + group]], held.at[n], sems.at[0, n])

    def put(n):
        target = outs[0].at[n] if len(outs) == 1 else outs[n]
        return pltpu.make_async_copy(held.at[n], target, sems.at[1, n])

    depth = 4
    for n in range(depth):
        fetch(n).start()
    for n in range(N_CENT):
        fetch(n).wait()
        put(n).start()
        if n + depth < N_CENT:
            fetch(n + depth).start()
    for n in range(N_CENT):
        put(n).wait()


def pick_panels(group, apart, ids, place, table):
    one = jax.ShapeDtypeStruct((PANEL, WIDTH), BF16)
    out = [one] * N_CENT if apart else [jax.ShapeDtypeStruct((N_CENT, PANEL, WIDTH), BF16)]
    return pl.pallas_call(
        functools.partial(pick_kernel, group),
        out_shape=out,
        in_specs=[smem_spec(), smem_spec(), hbm_spec()],
        out_specs=[hbm_spec()] * len(out),
        scratch_shapes=[pltpu.VMEM((N_CENT, PANEL, WIDTH), BF16), pltpu.SemaphoreType.DMA((2, N_CENT))],
        compiler_params=params(60),
        cost_estimate=pl.CostEstimate(flops=0, bytes_accessed=4 * N_CENT * PANEL * WIDTH, transcendentals=0),
    )(ids, place, table)


def score_kernel(group, sources, owners, *refs):
    panels, (points, surcharge, out, members, centers, shares, sems) = refs[:sources], refs[sources:]
    step = 256
    steps = GROUP // step

    def bring(s):
        rows = pl.ds(s * step, step)
        return pltpu.make_async_copy(points.at[pl.ds(group * GROUP + s * step, step)], members.at[rows], sems.at[s])

    def land(j, source):
        return pltpu.make_async_copy(source, centers.at[pl.ds(j * PANEL, PANEL)], sems.at[steps + j])

    for j in range(CAND):
        if sources == 1:
            land(j, panels[0].at[owners[j]]).start()
        else:
            for o in range(N_CENT):

                @pl.when(owners[j] == o)
                def _(j=j, o=o):
                    land(j, panels[o]).start()

    for s in range(steps):
        bring(s).start()
    for j in range(CAND):
        land(j, panels[0].at[0] if sources == 1 else panels[0]).wait()
    wide = centers[...].astype(F32)
    squares = jnp.sum(wide * wide, axis=1, keepdims=True)
    bias = squares * (1.0 / sharpness_divisor) + evenness_coefficient * surcharge[0]
    weights = jnp.zeros((CAND * PANEL, LANE), F32)
    for s in range(steps):
        bring(s).wait()
        block = members[s * step : (s + 1) * step, :]
        inner = lax.dot_general(centers[...], block, (((1,), (1,)), ((), ())), preferred_element_type=F32)
        logits = inner * (2.0 / sharpness_divisor) - bias
        highest = jnp.max(logits, axis=0, keepdims=True)
        raised = jnp.exp(logits - highest)
        scale = 1.0 / jnp.sum(raised, axis=0, keepdims=True)
        share = (raised * scale).astype(BF16)
        shares[:, s * step : (s + 1) * step] = share
        rounded = share.astype(F32)
        for part in range(step // LANE):
            weights = weights + rounded[:, part * LANE : (part + 1) * LANE]
    weight = jnp.sum(weights, axis=1, keepdims=True)
    coarse = weight.astype(BF16).astype(F32)
    fine = weight - coarse
    lane = lax.broadcasted_iota(jnp.int32, (PANEL, LANE), 1)
    tile = jnp.zeros((PANEL, LANE), F32)
    for j in range(CAND):
        rows = slice(j * PANEL, (j + 1) * PANEL)
        tile = jnp.where(lane == j, coarse[rows], tile)
        tile = jnp.where(lane == CAND + j, fine[rows], tile)
    tile = tile.astype(BF16)
    for block_at in range(PANEL // ROWS):
        for half in range(2):
            out[block_at * 2 + half, CAND * TILES] = tile[block_at * ROWS : (block_at + 1) * ROWS]

    wide_step = 256
    for s in range(WIDTH // wide_step):
        part = lax.dot_general(
            shares[...], members[:, s * wide_step : (s + 1) * wide_step], (((1,), (0,)), ((), ())),
            preferred_element_type=F32,
        ).astype(BF16)
        for t in range(wide_step // LANE):
            half, tile_at = divmod(s * (wide_step // LANE) + t, TILES)
            for j in range(CAND):
                for block_at in range(PANEL // ROWS):
                    row = j * PANEL + block_at * ROWS
                    out[block_at * 2 + half, j * TILES + tile_at] = part[row : row + ROWS, t * LANE : (t + 1) * LANE]


def score(group, owners, panels, points, surcharge):
    shape = (N_PTS, SEND_TILES, ROWS, LANE)
    return pl.pallas_call(
        functools.partial(score_kernel, group, len(panels)),
        grid=(1,),
        in_specs=[smem_spec()] + [pl.BlockSpec(memory_space=pl.ANY)] * (len(panels) + 1)
        + [pl.BlockSpec((1, CAND * PANEL, 1), lambda g: (group, 0, 0))],
        out_specs=whole(shape),
        out_shape=jax.ShapeDtypeStruct(shape, BF16),
        scratch_shapes=[
            pltpu.VMEM((GROUP, WIDTH), BF16),
            pltpu.VMEM((CAND * PANEL, WIDTH), BF16),
            pltpu.VMEM((CAND * PANEL, GROUP), BF16),
            pltpu.SemaphoreType.DMA((8,)),
        ],
        compiler_params=params(32),
        cost_estimate=pl.CostEstimate(flops=2 << 30, bytes_accessed=6 * MIB, transcendentals=1 << 19),
    )(owners, *panels, points, surcharge)


def spread_kernel(rows, count, places, *refs):
    sources, (lanes, own, own_weights, out1, out2, out3, total) = refs[:count], refs[count:]
    total[...] = jnp.zeros_like(total)
    for n, source in enumerate(sources):

        def add(s, carry, n=n, source=source):
            for j in range(CAND):
                at = places[(n * N_PTS + s) * CAND + j] * TILES
                total[pl.ds(at, TILES)] += source[s, j * TILES : (j + 1) * TILES].astype(F32)
            return carry

        lax.fori_loop(0, N_PTS, add, 0, unroll=2)
    panel = lax.broadcasted_iota(jnp.int32, (CHIPS * PAN_DEV, LANE), 0)
    weights = jnp.zeros((ROWS, CHIPS * PAN_DEV), F32)
    for n in range(count * N_PTS):
        chosen = jnp.where(panel == lanes[n : n + 1, :], 1.0, 0.0).astype(BF16)
        weights = weights + lax.dot_general(
            sources[n // N_PTS][n % N_PTS, CAND * TILES], chosen, (((1,), (1,)), ((), ())),
            preferred_element_type=F32,
        )
    own[...] = total[0:DENSE]
    coarse = weights.astype(BF16)
    fine = (weights - coarse.astype(F32)).astype(BF16)
    own_weights[...] = weights[:, 0:LANE]
    for d, out in ((1, out1), (2, out2), (3, out3)):
        first = DENSE + (d - 1) * rows * TILES
        out[0 : rows * TILES] = total[first : first + rows * TILES].astype(BF16)
        out[rows * TILES, :, 0:PAN_DEV] = coarse[:, d * PAN_DEV : (d + 1) * PAN_DEV]
        out[rows * TILES, :, PAN_DEV:LANE] = fine[:, d * PAN_DEV : (d + 1) * PAN_DEV]


def spread(rows, places, lanes, sources):
    chunk = jax.ShapeDtypeStruct((rows * TILES + 1, ROWS, LANE), BF16)
    return pl.pallas_call(
        functools.partial(spread_kernel, rows, len(sources)),
        grid=(1,),
        in_specs=[smem_spec()] + [whole(x.shape) for x in sources] + [whole(lanes.shape)],
        out_specs=[whole((DENSE, ROWS, LANE)), whole((ROWS, LANE))] + [whole(chunk.shape)] * 3,
        out_shape=[
            jax.ShapeDtypeStruct((DENSE, ROWS, LANE), F32), jax.ShapeDtypeStruct((ROWS, LANE), F32),
            chunk, chunk, chunk,
        ],
        scratch_shapes=[pltpu.VMEM(((PAN_DEV + 3 * rows + 1) * TILES, ROWS, LANE), F32)],
        compiler_params=params(48),
        cost_estimate=pl.CostEstimate(flops=1 << 22, bytes_accessed=6 * MIB, transcendentals=0),
    )(places, *sources, lanes)


def finish_kernel(rows, owns, blocks, numbers, *refs):
    arrivals = owns * 3
    own, own_weights, arrived = refs[:owns], refs[owns : 2 * owns], refs[2 * owns : 2 * owns + arrivals]
    lanes, old, out, total, inverse, pair = refs[2 * owns + arrivals :]
    step = pl.program_id(0)

    @pl.when(step == 0)
    def _():
        panel = lax.broadcasted_iota(jnp.int32, (PAN_DEV, LANE), 0)
        total[...] = jnp.zeros_like(total)
        weights = own_weights[0][:, 0:PAN_DEV]
        for more in own_weights[1:]:
            weights = weights + more[:, 0:PAN_DEV]
        for d, source in enumerate(arrived):
            chosen = jnp.where(panel == lanes[d : d + 1, :], 1.0, 0.0).astype(BF16)
            weights = weights + lax.dot_general(
                source[rows * TILES], chosen, (((1,), (1,)), ((), ())), preferred_element_type=F32
            )
            first = 1 + arrivals + d * rows

            def add(n, carry, source=source, first=first):
                at = numbers[first + n] * TILES
                total[pl.ds(at, TILES)] += source[pl.ds(n * TILES, TILES)].astype(F32)
                return carry

            lax.fori_loop(0, numbers[1 + d], add, 0)
        coarse = weights.astype(BF16)
        pair[:, 0:PAN_DEV] = coarse
        pair[:, PAN_DEV:LANE] = (weights - coarse.astype(F32)).astype(BF16)
        scale = 1.0 / (weights + prior_mass)
        for q in range(PAN_DEV):
            inverse[q] = jnp.broadcast_to(scale[:, q : q + 1], (ROWS, LANE))

    here = PAN_DEV // blocks
    for q in range(here):
        for t in range(TILES):
            previous = old[q, :, t * LANE : (t + 1) * LANE].astype(F32)
            fresh = total[(step * here + q) * TILES + t] + prior_mass * previous
            for part in own:
                fresh = fresh + part[q * TILES + t]
            out[q // CAND, (q % CAND) * TILES + t] = (fresh * inverse[step * here + q]).astype(BF16)
    for p in range(here // CAND):
        out[p, CAND * TILES] = pair[...]


def finish(rows, numbers, own, own_weights, arrived, lanes, table):
    blocks = 4
    here = PAN_DEV // blocks
    chunk = whole((rows * TILES + 1, ROWS, LANE))
    last = CAND * TILES + 1
    return pl.pallas_call(
        functools.partial(finish_kernel, rows, len(own), blocks),
        grid_spec=pltpu.PrefetchScalarGridSpec(
            num_scalar_prefetch=1,
            grid=(blocks,),
            in_specs=[pl.BlockSpec((here * TILES, ROWS, LANE), lambda g, n: (g, 0, 0))] * len(own)
            + [whole((ROWS, LANE))] * len(own)
            + [chunk] * len(arrived)
            + [whole(lanes.shape), pl.BlockSpec((here, ROWS, HALF), lambda g, n: (g, n[0] // 2, n[0] % 2))],
            out_specs=pl.BlockSpec((here // CAND, last, ROWS, LANE), lambda g, n: (g, 0, 0, 0)),
            scratch_shapes=[
                pltpu.VMEM((DENSE, ROWS, LANE), F32),
                pltpu.VMEM((PAN_DEV, ROWS, LANE), F32),
                pltpu.VMEM((ROWS, LANE), BF16),
            ],
        ),
        out_shape=jax.ShapeDtypeStruct((N_PTS, last, ROWS, LANE), BF16),
        compiler_params=params(48),
        cost_estimate=pl.CostEstimate(flops=1 << 22, bytes_accessed=8 * MIB, transcendentals=0),
    )(numbers, *own, *own_weights, *arrived, lanes, table)


def place_kernel(me, pieces, out, loads):
    for block_at in range(PANEL // ROWS):
        for half in range(2):
            for q in range(CAND):
                for t in range(TILES):
                    column = half * HALF + t * LANE
                    out[q, block_at * ROWS : (block_at + 1) * ROWS, column : column + LANE] = pieces[
                        block_at * 2 + half, q * TILES + t
                    ]
    lane = lax.broadcasted_iota(jnp.int32, (ROWS, LANE), 1)
    row = lax.broadcasted_iota(jnp.int32, (ROWS, LANE), 0)
    wanted = me[0] * CAND + row
    chosen = jnp.where((row < CAND) & (lane % PAN_DEV == wanted), 1.0, 0.0).astype(BF16)
    for block_at in range(PANEL // ROWS):
        pair = pieces[block_at * 2, CAND * TILES]
        part = lax.dot_general(chosen, pair, (((1,), (1,)), ((), ())), preferred_element_type=F32)
        loads[:, block_at * ROWS : (block_at + 1) * ROWS] = part[0:CAND]


def place(me, pieces):
    return pl.pallas_call(
        place_kernel,
        grid=(1,),
        in_specs=[smem_spec(), whole(pieces.shape)],
        out_specs=[whole((CAND, PANEL, WIDTH)), whole((CAND, PANEL))],
        out_shape=[
            jax.ShapeDtypeStruct((CAND, PANEL, WIDTH), BF16),
            jax.ShapeDtypeStruct((CAND, PANEL), F32),
        ],
        compiler_params=params(32),
        cost_estimate=pl.CostEstimate(flops=1 << 20, bytes_accessed=2 * MIB, transcendentals=0),
    )(me, pieces)


def shift(dy, dk):
    return [(y * 2 + k, ((y + dy) % CHIPS) * 2 + (k + dk) % 2) for y in range(CHIPS) for k in range(2)]


def spread_out(x, place, dz, dx):
    held = [x]
    for d in range(1, SIDE):
        pairs = [
            (ix * SIDE + iz, (ix + d * dx) % SIDE * SIDE + (iz + d * dz) % SIDE)
            for ix in range(SIDE)
            for iz in range(SIDE)
        ]
        held.append(lax.ppermute(x, "pts", pairs))
    held = jnp.stack(held)
    at = (place - jnp.arange(SIDE, dtype=jnp.int32)) % SIDE
    return jnp.stack([jnp.sum(jnp.where((at == n).reshape((SIDE,) + (1,) * x.ndim), held, 0), axis=0) for n in range(SIDE)])


def exchange(x, axis):
    return lax.all_to_all(x, axis, split_axis=0, concat_axis=0, tiled=True)


def at_index(x, n, axis=0):
    return lax.dynamic_index_in_dim(x, n, axis, keepdims=False)


def local(points, centroids, prev_loads, candidates, panel_home):
    me = lax.axis_index("pts")
    here = lax.axis_index("cent")
    chip, core = here // 2, here % 2
    shelf = centroids.reshape(PAN_DEV, PANEL, WIDTH)
    tie = lax.optimization_barrier
    where = here.reshape(1)

    with jax.named_scope("requests"):
        answered = exchange(ask(candidates, panel_home, prev_loads.reshape(PAN_DEV, PANEL)), "cent")
        asked = answered[:, LOAD_TILES, 0, 0:GROUPS_DEV].astype(jnp.int32).reshape(-1)

    with jax.named_scope("gather_panels"):
        ready0, = pick_panels(0, False, asked, where, shelf)
        ready1 = pick_panels(1, True, asked, where, shelf)

    with jax.named_scope("gather_panels"):
        arrived0 = exchange(ready0, "cent")

    with jax.named_scope("loads"):
        wanted_ids, answered = tie((candidates.reshape(REQ), answered))
        slots = jnp.sum(
            jnp.where(wanted_ids[:, None] == jnp.arange(panel_home.shape[0], dtype=jnp.int32), panel_home[None, :], 0),
            axis=1,
        )
        owners = (slots // PAN_DEV).reshape(GROUPS_DEV, CAND)
        seen = (chip - owners // 2) % CHIPS * 2 + (core - owners) % 2
        load_table = answered[:, :LOAD_TILES].reshape(N_CENT * PAN_DEV, PANEL)
        loads = jnp.take(load_table, slots, axis=0, mode="clip").astype(F32)
        surcharge = jnp.log(loads).reshape(GROUPS_DEV, CAND * PANEL, 1)

    with jax.named_scope("all_requests"):
        answered, ready0 = tie((answered, ready0))
        ring = answered[:, LOAD_TILES, 1:3, 0:REQ].astype(jnp.int32)
        ring = ring[:, 0] * PAN_DEV + ring[:, 1]
        line = spread_out(ring, me % SIDE, 1, 0)
        everyone = spread_out(line, me // SIDE, 0, 1).reshape(N_PTS, N_CENT, GROUPS_DEV, CAND)

        numbers = jnp.arange(N_CENT * PAN_DEV, dtype=jnp.int32)
        by_chip = jnp.transpose(everyone.reshape(N_PTS, CHIPS, 2, GROUPS_DEV, CAND), (3, 1, 0, 2, 4))
        by_chip = by_chip.reshape(GROUPS_DEV, CHIPS, 2 * N_PTS * CAND)
        asked_by = jnp.any(by_chip[..., None] == numbers, axis=2).reshape(GROUPS_DEV, CHIPS, N_CENT, PAN_DEV)
        below = jnp.arange(PAN_DEV)[:, None] < jnp.arange(PAN_DEV)[None, :]
        ranks = lax.dot_general(
            asked_by.astype(BF16), below.astype(BF16), (((3,), (0,)), ((), ())), preferred_element_type=F32
        ).astype(jnp.int32)
        lengths = jnp.sum(asked_by.astype(jnp.int32), axis=3)
        off_chip = jnp.arange(N_CENT)[None, :] // 2 != jnp.arange(CHIPS)[:, None]
        too_long = jnp.any(off_chip & (lengths > LISTED))

        pair = jnp.stack([at_index(everyone, at, 1) for at in (here, chip * 2 + 1 - core)])
        pair = jnp.transpose(pair, (2, 0, 1, 3)).reshape(GROUPS_DEV, 2 * N_PTS, CAND)
        owner = pair // PAN_DEV
        relative = (owner // 2 - chip) % CHIPS
        my_ranks = at_index(ranks, chip, 1).reshape(GROUPS_DEV, 1, 1, -1)
        rank = jnp.sum(jnp.where(pair[..., None] == numbers, my_ranks, 0), axis=3)

        def sender(rows, rank):
            at = jnp.where(relative == 0, pair % PAN_DEV, rank)
            known = (owner % 2 == core) & ((relative == 0) | (rank < rows))
            first = jnp.where(relative == 0, 0, PAN_DEV + (relative - 1) * rows)
            places = jnp.where(known, first + at, PAN_DEV + 3 * rows)
            lane = jnp.where(known, relative * PAN_DEV + at, CHIPS * PAN_DEV)
            lanes = jnp.pad(
                jnp.concatenate([lane, lane], axis=2), ((0, 0), (0, 0), (0, LANE - 2 * CAND)),
                constant_values=CHIPS * PAN_DEV,
            )
            return places, lanes

        def receiver(rows, count, panels):
            numbers = jnp.concatenate([me.reshape(1), count, panels[:, :rows].reshape(-1)])
            lane = jnp.where(jnp.arange(PAN_DEV) < count[:, None], panels, PAN_DEV)
            return numbers, jnp.concatenate([lane, lane], axis=1)

        behind = [(chip - d) % CHIPS for d in range(1, CHIPS)]
        named = jnp.stack([at_index(at_index(asked_by[g], y), here) for g in range(GROUPS_DEV) for y in behind])
        order = jnp.stack([at_index(at_index(ranks[g], y), here) for g in range(GROUPS_DEV) for y in behind])
        spots = jnp.arange(PAN_DEV, dtype=jnp.int32)
        listed = jnp.sum(
            jnp.where(named[:, None, :] & (order[:, None, :] == spots[None, :, None]), spots, 0), axis=2
        )
        count = jnp.minimum(jnp.sum(named.astype(jnp.int32), axis=1), LISTED)
        places, lanes = sender(LISTED, rank)
        places = [places[g].reshape(-1) for g in range(GROUPS_DEV)]
        lanes = [lanes[g] for g in range(GROUPS_DEV)]
        numbers, back_lanes = receiver(LISTED, count, listed)
        owners, seen, too_long, places, lanes, numbers, back_lanes = tie(
            (owners, seen, too_long, places, lanes, numbers, back_lanes)
        )

    def to_owners(far):
        return [lax.ppermute(far[d - 1], "cent", shift(d, 0)) for d in range(1, CHIPS)]

    with jax.named_scope("group_0"):
        ready1, arrived0 = tie((ready1, arrived0))
        arrived1 = [ready1[0]] + [lax.ppermute(ready1[n], "cent", shift(n // 2, n % 2)) for n in range(1, N_CENT)]
        pieces0 = score(0, owners[0], [arrived0], points, surcharge)
        mine0 = exchange(pieces0, "pts")
        arrived1, mine0 = tie((arrived1, mine0))
        mate0 = lax.ppermute(mine0, "cent", shift(0, 1))

    with jax.named_scope("group_1"):
        pieces1 = score(1, seen[1], arrived1, points, surcharge)
        mine1 = exchange(pieces1, "pts")

    with jax.named_scope("spread_0"):
        own0, weights0, *far0 = spread(LISTED, places[0], lanes[0], [mine0, mate0])
        back0 = to_owners(far0)
        mine1, back0 = tie((mine1, back0))

    with jax.named_scope("spread_1"):
        mate1 = lax.ppermute(mine1, "cent", shift(0, 1))
        own1, weights1, *far1 = spread(LISTED, places[1], lanes[1], [mine1, mate1])
        back1 = to_owners(far1)

    def from_lists():
        return finish(LISTED, numbers, [own0, own1], [weights0, weights1], back0 + back1, back_lanes, shelf)

    def from_all():
        everything = jnp.broadcast_to(spots, (CHIPS - 1, PAN_DEV))
        count = jnp.full((CHIPS - 1,), PAN_DEV, jnp.int32)
        places, lanes = sender(PAN_DEV, pair % PAN_DEV)
        sources = [mine0, mate0, mine1, mate1]
        own, weights, *far = spread(PAN_DEV, places.reshape(-1), lanes.reshape(-1, LANE), sources)
        numbers, back_lanes = receiver(PAN_DEV, count, everything)
        return finish(PAN_DEV, numbers, [own], [weights], to_owners(far), back_lanes, shelf)

    with jax.named_scope("finish"):
        fresh = lax.cond(too_long, from_all, from_lists)

    with jax.named_scope("place"):
        new_centroids, new_loads = place(me.reshape(1), exchange(fresh, "pts"))
    return new_centroids.reshape(CAND * PANEL, WIDTH), new_loads.reshape(CAND * PANEL)


def solution(mesh):
    placed = (P(("pts", "cent"), None), P("cent", None), P("cent"), P(("pts", "cent"), None), P())
    return jax.shard_map(
        local,
        mesh=mesh,
        in_specs=placed,
        out_specs=(P(("cent", "pts"), None), P(("cent", "pts"))),
        check_vma=False,
    )
```

```python
import functools

import jax
import jax.numpy as jnp
from jax import lax
from jax.experimental import pallas as pl
from jax.experimental.pallas import tpu as pltpu
from jax.sharding import PartitionSpec as P

PANEL = 128
GROUP = 1024
CAND = 4
GROUPS_DEV = 2
REQ = CAND * GROUPS_DEV
PAN_DEV = 64
WIDTH = 1024
N_CENT = 8
CHIPS = 4
N_PTS = 16
SIDE = 4
ROWS = 16
HALF = 512
LANE = 128
TILES = HALF // LANE
SEND_TILES = REQ * TILES + 1
DENSE = PAN_DEV * TILES
LOAD_TILES = PAN_DEV // ROWS
LISTED = 36

sharpness_divisor = 16.0
evenness_coefficient = 1.0
prior_mass = 1.0

BF16 = jnp.bfloat16
F32 = jnp.float32
MIB = 1 << 20


def params(mib):
    return pltpu.CompilerParams(vmem_limit_bytes=mib * MIB)


def whole(shape):
    return pl.BlockSpec(shape, lambda *_: (0,) * len(shape))


def smem_spec():
    return pl.BlockSpec(memory_space=pltpu.SMEM)


def vmem_spec():
    return pl.BlockSpec(memory_space=pltpu.VMEM)


def hbm_spec():
    return pl.BlockSpec(memory_space=pltpu.HBM)


def ask_kernel(candidates_in, home_in, loads_in, out, candidates, home, loads, sems):
    copies = [
        pltpu.make_async_copy(source, target, sems.at[n])
        for n, (source, target) in enumerate(((candidates_in, candidates), (home_in, home), (loads_in, loads)))
    ]
    for copy in copies:
        copy.start()
    for copy in copies:
        copy.wait()
    row = lax.broadcasted_iota(jnp.int32, (ROWS, LANE), 0)
    lane = lax.broadcasted_iota(jnp.int32, (ROWS, LANE), 1)
    slots = [home[candidates[n // CAND, n % CAND]] for n in range(REQ)]
    common = jnp.zeros((ROWS, LANE), F32)
    for n, slot in enumerate(slots):
        common = jnp.where((row == 1) & (lane == n), (slot // PAN_DEV).astype(F32), common)
        common = jnp.where((row == 2) & (lane == n), (slot % PAN_DEV).astype(F32), common)
    for o in range(N_CENT):
        tile = common
        for n, slot in enumerate(slots):
            here = jnp.where(slot // PAN_DEV == o, slot % PAN_DEV, 0).astype(F32)
            tile = jnp.where((row == 0) & (lane == n // CAND), tile + here, tile)
        for t in range(LOAD_TILES):
            out[o, t] = loads[t * ROWS : (t + 1) * ROWS]
        out[o, LOAD_TILES] = tile.astype(BF16)


def ask(candidates, home, loads):
    return pl.pallas_call(
        ask_kernel,
        in_specs=[hbm_spec()] * 3,
        out_specs=vmem_spec(),
        out_shape=jax.ShapeDtypeStruct((N_CENT, LOAD_TILES + 1, ROWS, LANE), BF16),
        scratch_shapes=[
            pltpu.SMEM(candidates.shape, jnp.int32),
            pltpu.SMEM(home.shape, jnp.int32),
            pltpu.VMEM(loads.shape, BF16),
            pltpu.SemaphoreType.DMA((3,)),
        ],
        compiler_params=params(60),
        cost_estimate=pl.CostEstimate(flops=1 << 16, bytes_accessed=1 << 18, transcendentals=0),
    )(candidates, home, loads)


def pick_kernel(ids, table, out, sems):
    copies = [pltpu.make_async_copy(table.at[ids[n]], out.at[n], sems.at[n]) for n in range(out.shape[0])]
    for copy in copies:
        copy.start()
    for copy in copies:
        copy.wait()


def pick_panels(ids, table):
    count = ids.shape[0]
    return pl.pallas_call(
        pick_kernel,
        out_shape=jax.ShapeDtypeStruct((count, PANEL, WIDTH), BF16),
        in_specs=[smem_spec(), hbm_spec()],
        out_specs=vmem_spec(),
        scratch_shapes=[pltpu.SemaphoreType.DMA((count,))],
        compiler_params=params(56),
        cost_estimate=pl.CostEstimate(flops=0, bytes_accessed=4 * count * PANEL * WIDTH, transcendentals=0),
    )(ids, table)


def score_kernel(target, points, arrived, surcharge, out, members, centers, shares, sems):
    step = 256
    steps = GROUP // step

    def land(n):
        rows = pl.ds(n * PANEL, PANEL)
        return pltpu.make_async_copy(arrived.at[target[n]], centers.at[rows], sems.at[0, n])

    def bring(n):
        rows = pl.ds(n * step, step)
        return pltpu.make_async_copy(points.at[rows], members.at[rows], sems.at[1, n])

    for group in range(GROUPS_DEV):
        for j in range(CAND):
            land(group * CAND + j).start()
        for s in range(steps):
            bring(group * steps + s).start()
    lane = lax.broadcasted_iota(jnp.int32, (PANEL, LANE), 1)
    tile = jnp.zeros((PANEL, LANE), F32)
    for group in range(GROUPS_DEV):
        for j in range(CAND):
            land(group * CAND + j).wait()
        mine = centers[group * CAND * PANEL : (group + 1) * CAND * PANEL, :]
        wide = mine.astype(F32)
        squares = jnp.sum(wide * wide, axis=1, keepdims=True)
        bias = squares * (1.0 / sharpness_divisor) + evenness_coefficient * surcharge[group]
        weights = jnp.zeros((CAND * PANEL, LANE), F32)
        for s in range(steps):
            bring(group * steps + s).wait()
            block = members[group * GROUP + s * step : group * GROUP + (s + 1) * step, :]
            inner = lax.dot_general(mine, block, (((1,), (1,)), ((), ())), preferred_element_type=F32)
            logits = inner * (2.0 / sharpness_divisor) - bias
            highest = jnp.max(logits, axis=0, keepdims=True)
            raised = jnp.exp(logits - highest)
            scale = 1.0 / jnp.sum(raised, axis=0, keepdims=True)
            share = (raised * scale).astype(BF16)
            shares[:, s * step : (s + 1) * step] = share
            rounded = share.astype(F32)
            for part in range(step // LANE):
                weights = weights + rounded[:, part * LANE : (part + 1) * LANE]
        weight = jnp.sum(weights, axis=1, keepdims=True)
        coarse = weight.astype(BF16).astype(F32)
        fine = weight - coarse
        for j in range(CAND):
            rows = slice(j * PANEL, (j + 1) * PANEL)
            tile = jnp.where(lane == group * CAND + j, coarse[rows], tile)
            tile = jnp.where(lane == REQ + group * CAND + j, fine[rows], tile)
        wide_step = 256
        for s in range(WIDTH // wide_step):
            part = lax.dot_general(
                shares[...],
                members[group * GROUP : (group + 1) * GROUP, s * wide_step : (s + 1) * wide_step],
                (((1,), (0,)), ((), ())),
                preferred_element_type=F32,
            ).astype(BF16)
            for t in range(wide_step // LANE):
                half, tile_at = divmod(s * (wide_step // LANE) + t, TILES)
                for j in range(CAND):
                    for block_at in range(PANEL // ROWS):
                        row = j * PANEL + block_at * ROWS
                        out[block_at * 2 + half, (group * CAND + j) * TILES + tile_at] = part[
                            row : row + ROWS, t * LANE : (t + 1) * LANE
                        ]
    tile = tile.astype(BF16)
    for block_at in range(PANEL // ROWS):
        for half in range(2):
            out[block_at * 2 + half, REQ * TILES] = tile[block_at * ROWS : (block_at + 1) * ROWS]


def score(target, points, arrived, surcharge):
    return pl.pallas_call(
        score_kernel,
        in_specs=[smem_spec(), hbm_spec(), hbm_spec(), vmem_spec()],
        out_specs=vmem_spec(),
        out_shape=jax.ShapeDtypeStruct((N_PTS, SEND_TILES, ROWS, LANE), BF16),
        scratch_shapes=[
            pltpu.VMEM((GROUPS_DEV * GROUP, WIDTH), BF16),
            pltpu.VMEM((GROUPS_DEV * CAND * PANEL, WIDTH), BF16),
            pltpu.VMEM((CAND * PANEL, GROUP), BF16),
            pltpu.SemaphoreType.DMA((2, 8)),
        ],
        compiler_params=params(48),
        cost_estimate=pl.CostEstimate(flops=4 << 30, bytes_accessed=10 * MIB, transcendentals=1 << 20),
    )(target, points, arrived, surcharge)


def spread_kernel(rows, places, mine, mate, lanes, own, own_weights, out1, out2, out3, total):
    total[...] = jnp.zeros_like(total)
    sources = (mine, mate)
    for n, source in enumerate(sources):
        def add(s, carry, n=n, source=source):
            for i in range(REQ):
                at = places[(n * N_PTS + s) * REQ + i] * TILES
                total[pl.ds(at, TILES)] += source[s, i * TILES : (i + 1) * TILES].astype(F32)
            return carry

        lax.fori_loop(0, N_PTS, add, 0)
    panel = lax.broadcasted_iota(jnp.int32, (CHIPS * PAN_DEV, LANE), 0)
    weights = jnp.zeros((ROWS, CHIPS * PAN_DEV), F32)
    for n in range(2 * N_PTS):
        chosen = jnp.where(panel == lanes[n : n + 1, :], 1.0, 0.0).astype(BF16)
        weights = weights + lax.dot_general(
            sources[n // N_PTS][n % N_PTS, REQ * TILES], chosen, (((1,), (1,)), ((), ())),
            preferred_element_type=F32,
        )
    own[...] = total[0:DENSE]
    coarse = weights.astype(BF16)
    fine = (weights - coarse.astype(F32)).astype(BF16)
    own_weights[...] = weights[:, 0:LANE]
    for d, out in ((1, out1), (2, out2), (3, out3)):
        first = DENSE + (d - 1) * rows * TILES
        out[0 : rows * TILES] = total[first : first + rows * TILES].astype(BF16)
        out[rows * TILES, :, 0:PAN_DEV] = coarse[:, d * PAN_DEV : (d + 1) * PAN_DEV]
        out[rows * TILES, :, PAN_DEV:LANE] = fine[:, d * PAN_DEV : (d + 1) * PAN_DEV]


def spread(rows, places, mine, mate, lanes):
    chunk = jax.ShapeDtypeStruct((rows * TILES + 1, ROWS, LANE), BF16)
    return pl.pallas_call(
        functools.partial(spread_kernel, rows),
        in_specs=[smem_spec()] + [vmem_spec()] * 3,
        out_specs=[vmem_spec()] * 5,
        out_shape=[
            jax.ShapeDtypeStruct((DENSE, ROWS, LANE), F32), jax.ShapeDtypeStruct((ROWS, LANE), F32),
            chunk, chunk, chunk,
        ],
        scratch_shapes=[pltpu.VMEM(((PAN_DEV + 3 * rows + 1) * TILES, ROWS, LANE), F32)],
        compiler_params=params(16),
        cost_estimate=pl.CostEstimate(flops=1 << 22, bytes_accessed=8 * MIB, transcendentals=0),
    )(places, mine, mate, lanes)


def finish_kernel(rows, numbers, own, own_weights, in1, in2, in3, lanes, table, out, total, old, sem):
    row = pl.multiple_of(numbers[0] // 2 * ROWS, ROWS)
    column = pl.multiple_of(numbers[0] % 2 * HALF, HALF)
    fetch = pltpu.make_async_copy(table.at[:, pl.ds(row, ROWS), pl.ds(column, HALF)], old, sem)
    fetch.start()
    weights = own_weights[:, 0:PAN_DEV]
    panel = lax.broadcasted_iota(jnp.int32, (PAN_DEV, LANE), 0)
    total[...] = own[...]
    for d, arrived in enumerate((in1, in2, in3)):
        chosen = jnp.where(panel == lanes[d : d + 1, :], 1.0, 0.0).astype(BF16)
        weights = weights + lax.dot_general(
            arrived[rows * TILES], chosen, (((1,), (1,)), ((), ())), preferred_element_type=F32
        )
        first = 4 + d * rows

        def add(n, carry, arrived=arrived, first=first):
            at = numbers[first + n] * TILES
            total[pl.ds(at, TILES)] += arrived[pl.ds(n * TILES, TILES)].astype(F32)
            return carry

        lax.fori_loop(0, numbers[1 + d], add, 0)
    inverse = 1.0 / (weights + prior_mass)
    fetch.wait()
    for q in range(PAN_DEV):
        scale = jnp.broadcast_to(inverse[:, q : q + 1], (ROWS, LANE))
        for t in range(TILES):
            previous = old[q, :, t * LANE : (t + 1) * LANE].astype(F32)
            fresh = (total[q * TILES + t] + prior_mass * previous) * scale
            out[q // CAND, (q % CAND) * TILES + t] = fresh.astype(BF16)
    coarse = weights.astype(BF16)
    fine = (weights - coarse.astype(F32)).astype(BF16)
    for p in range(N_PTS):
        out[p, CAND * TILES, :, 0:PAN_DEV] = coarse
        out[p, CAND * TILES, :, PAN_DEV:LANE] = fine


def finish(rows, numbers, own, own_weights, arrived, lanes, table):
    return pl.pallas_call(
        functools.partial(finish_kernel, rows),
        in_specs=[smem_spec()] + [vmem_spec()] * 6 + [hbm_spec()],
        out_specs=vmem_spec(),
        out_shape=jax.ShapeDtypeStruct((N_PTS, CAND * TILES + 1, ROWS, LANE), BF16),
        scratch_shapes=[
            pltpu.VMEM((DENSE, ROWS, LANE), F32),
            pltpu.VMEM((PAN_DEV, ROWS, HALF), BF16),
            pltpu.SemaphoreType.DMA,
        ],
        compiler_params=params(48),
        cost_estimate=pl.CostEstimate(flops=1 << 22, bytes_accessed=6 * MIB, transcendentals=0),
    )(numbers, own, own_weights, *arrived, lanes, table)


def place_kernel(me, pieces, out, loads):
    for block_at in range(PANEL // ROWS):
        for half in range(2):
            for q in range(CAND):
                for t in range(TILES):
                    column = half * HALF + t * LANE
                    out[q, block_at * ROWS : (block_at + 1) * ROWS, column : column + LANE] = pieces[
                        block_at * 2 + half, q * TILES + t
                    ]
    lane = lax.broadcasted_iota(jnp.int32, (ROWS, LANE), 1)
    row = lax.broadcasted_iota(jnp.int32, (ROWS, LANE), 0)
    wanted = me[0] * CAND + row
    chosen = jnp.where((row < CAND) & (lane % PAN_DEV == wanted), 1.0, 0.0).astype(BF16)
    for block_at in range(PANEL // ROWS):
        pair = pieces[block_at * 2, CAND * TILES]
        part = lax.dot_general(chosen, pair, (((1,), (1,)), ((), ())), preferred_element_type=F32)
        loads[:, block_at * ROWS : (block_at + 1) * ROWS] = part[0:CAND]


def place(me, pieces):
    return pl.pallas_call(
        place_kernel,
        grid=(1,),
        in_specs=[smem_spec(), whole(pieces.shape)],
        out_specs=[whole((CAND, PANEL, WIDTH)), whole((CAND, PANEL))],
        out_shape=[
            jax.ShapeDtypeStruct((CAND, PANEL, WIDTH), BF16),
            jax.ShapeDtypeStruct((CAND, PANEL), F32),
        ],
        compiler_params=params(32),
        cost_estimate=pl.CostEstimate(flops=1 << 20, bytes_accessed=2 * MIB, transcendentals=0),
    )(me, pieces)


def shift(dy, dk):
    return [(y * 2 + k, ((y + dy) % CHIPS) * 2 + (k + dk) % 2) for y in range(CHIPS) for k in range(2)]


def spread_out(x, place, dz, dx):
    held = [x]
    for d in range(1, SIDE):
        pairs = [
            (ix * SIDE + iz, (ix + d * dx) % SIDE * SIDE + (iz + d * dz) % SIDE)
            for ix in range(SIDE)
            for iz in range(SIDE)
        ]
        held.append(lax.ppermute(x, "pts", pairs))
    held = jnp.stack(held)
    at = (place - jnp.arange(SIDE, dtype=jnp.int32)) % SIDE
    return jnp.stack([jnp.sum(jnp.where((at == n).reshape((SIDE,) + (1,) * x.ndim), held, 0), axis=0) for n in range(SIDE)])


def exchange(x, axis):
    return lax.all_to_all(x, axis, split_axis=0, concat_axis=0, tiled=True)


def local(points, centroids, prev_loads, candidates, panel_home):
    me = lax.axis_index("pts")
    here = lax.axis_index("cent")
    chip, core = here // 2, here % 2
    shelf = centroids.reshape(PAN_DEV, PANEL, WIDTH)

    with jax.named_scope("requests"):
        answered = exchange(ask(candidates, panel_home, prev_loads.reshape(PAN_DEV, PANEL)), "cent")
        asked = answered[:, LOAD_TILES, 0, 0:GROUPS_DEV].astype(jnp.int32).reshape(-1)

    with jax.named_scope("gather_panels"):
        ready = pick_panels(asked, shelf)
        arrived = exchange(ready.reshape(N_CENT, GROUPS_DEV, PANEL, WIDTH), "cent")
        arrived = arrived.reshape(N_CENT * GROUPS_DEV, PANEL, WIDTH)

    with jax.named_scope("own_requests"):
        slots = jnp.sum(
            jnp.where(candidates.reshape(REQ)[:, None] == jnp.arange(panel_home.shape[0], dtype=jnp.int32), panel_home[None, :], 0),
            axis=1,
        )
        target = slots // PAN_DEV * GROUPS_DEV + jnp.arange(REQ, dtype=jnp.int32) // CAND

    with jax.named_scope("all_requests"):
        ring = answered[:, LOAD_TILES, 1:3, 0:REQ].astype(jnp.int32)
        ring = ring[:, 0] * PAN_DEV + ring[:, 1]
        line = spread_out(ring, me % SIDE, 1, 0)
        everyone = spread_out(line, me // SIDE, 0, 1).reshape(N_PTS, N_CENT, REQ)
        numbers = jnp.arange(N_CENT * PAN_DEV, dtype=jnp.int32)
        by_chip = jnp.transpose(everyone.reshape(N_PTS, CHIPS, 2 * REQ), (1, 0, 2)).reshape(CHIPS, -1)
        asked_by = jnp.any(by_chip[:, :, None] == numbers, axis=1).reshape(CHIPS, N_CENT, PAN_DEV)
        below = jnp.arange(PAN_DEV)[:, None] < jnp.arange(PAN_DEV)[None, :]
        ranks = lax.dot_general(
            asked_by.astype(BF16), below.astype(BF16), (((2,), (0,)), ((), ())), preferred_element_type=F32
        ).astype(jnp.int32)
        lengths = jnp.sum(asked_by.astype(jnp.int32), axis=2)
        off_chip = jnp.arange(N_CENT)[None, :] // 2 != jnp.arange(CHIPS)[:, None]
        too_long = jnp.any(off_chip & (lengths > LISTED))

        pair = jnp.stack(
            [lax.dynamic_index_in_dim(everyone, at, 1, keepdims=False) for at in (here, chip * 2 + 1 - core)]
        ).reshape(2 * N_PTS, REQ)
        owner = pair // PAN_DEV
        relative = (owner // 2 - chip) % CHIPS
        my_ranks = lax.dynamic_index_in_dim(ranks, chip, 0, keepdims=False).reshape(-1)
        rank = jnp.sum(jnp.where(pair[:, :, None] == numbers, my_ranks, 0), axis=2)
        ours = owner % 2 == core

        def sender(rows, rank):
            at = jnp.where(relative == 0, pair % PAN_DEV, rank)
            known = ours & ((relative == 0) | (rank < rows))
            first = jnp.where(relative == 0, 0, PAN_DEV + (relative - 1) * rows)
            places = jnp.where(known, first + at, PAN_DEV + 3 * rows).reshape(-1)
            lane = jnp.where(known, relative * PAN_DEV + at, CHIPS * PAN_DEV)
            lanes = jnp.pad(
                jnp.concatenate([lane, lane], axis=1), ((0, 0), (0, LANE - 2 * REQ)), constant_values=CHIPS * PAN_DEV
            )
            return places, lanes

        def receiver(rows, count, panels):
            numbers = jnp.concatenate([me.reshape(1), count, panels[:, :rows].reshape(-1)])
            lane = jnp.where(jnp.arange(PAN_DEV) < jnp.minimum(count, rows)[:, None], panels, PAN_DEV)
            return numbers, jnp.concatenate([lane, lane], axis=1)

        behind = [(chip - d) % CHIPS for d in range(1, CHIPS)]
        pick = lambda x, y: lax.dynamic_index_in_dim(lax.dynamic_index_in_dim(x, y, 0, False), here, 0, False)
        named = jnp.stack([pick(asked_by, y) for y in behind])
        order = jnp.stack([pick(ranks, y) for y in behind])
        spots = jnp.arange(PAN_DEV, dtype=jnp.int32)
        listed = jnp.sum(
            jnp.where(named[:, None, :] & (order[:, None, :] == spots[None, :, None]), spots, 0), axis=2
        )
        count = jnp.minimum(jnp.sum(named.astype(jnp.int32), axis=1), LISTED)
        short = sender(LISTED, rank) + receiver(LISTED, count, listed)
        target, too_long, short = lax.optimization_barrier((target, too_long, short))

    with jax.named_scope("loads"):
        load_table = answered[:, :LOAD_TILES].reshape(N_CENT * PAN_DEV, PANEL)
        loads = jnp.take(load_table, slots, axis=0, mode="clip").astype(F32)
        surcharge = jnp.log(loads).reshape(GROUPS_DEV, CAND * PANEL, 1)

    with jax.named_scope("score"):
        pieces = score(target, points, arrived, surcharge)

    with jax.named_scope("split_pieces"):
        mine = exchange(pieces, "pts")
        mate = lax.ppermute(mine, "cent", shift(0, 1))

    def sum_over_chips(rows, places, lanes, numbers, back_lanes):
        own, own_weights, *far = spread(rows, places, mine, mate, lanes)
        back = [lax.ppermute(far[d - 1], "cent", shift(d, 0)) for d in range(1, CHIPS)]
        return finish(rows, numbers, own, own_weights, back, back_lanes, shelf)

    def send_all():
        everything = jnp.broadcast_to(spots, (CHIPS - 1, PAN_DEV))
        count = jnp.full((CHIPS - 1,), PAN_DEV, jnp.int32)
        return sum_over_chips(PAN_DEV, *sender(PAN_DEV, pair % PAN_DEV), *receiver(PAN_DEV, count, everything))

    with jax.named_scope("sum_over_chips"):
        fresh = lax.cond(too_long, send_all, lambda: sum_over_chips(LISTED, *short))

    with jax.named_scope("place"):
        new_centroids, new_loads = place(me.reshape(1), exchange(fresh, "pts"))
    return new_centroids.reshape(CAND * PANEL, WIDTH), new_loads.reshape(CAND * PANEL)


def solution(mesh):
    placed = (P(("pts", "cent"), None), P("cent", None), P("cent"), P(("pts", "cent"), None), P())
    return jax.shard_map(
        local,
        mesh=mesh,
        in_specs=placed,
        out_specs=(P(("cent", "pts"), None), P(("cent", "pts"))),
        check_vma=False,
    )
```

```python
import functools

import jax
import jax.numpy as jnp
from jax import lax
from jax.experimental import pallas as pl
from jax.experimental.pallas import tpu as pltpu
from jax.sharding import PartitionSpec as P

PANEL = 128
GROUP = 1024
CAND = 4
GROUPS_DEV = 2
REQ = CAND * GROUPS_DEV
PAN_DEV = 64
WIDTH = 1024
N_CENT = 8
CHIPS = 4
N_PTS = 16
SIDE = 4
ROWS = 16
HALF = 512
LANE = 128
TILES = HALF // LANE
SEND_TILES = REQ * TILES + 1
DENSE = PAN_DEV * TILES
LOAD_TILES = PAN_DEV // ROWS
LISTED = 36

sharpness_divisor = 16.0
evenness_coefficient = 1.0
prior_mass = 1.0

BF16 = jnp.bfloat16
F32 = jnp.float32
MIB = 1 << 20
LOG2E = 1.4426950408889634


def params(mib):
    return pltpu.CompilerParams(vmem_limit_bytes=mib * MIB)


def whole(shape):
    return pl.BlockSpec(shape, lambda *_: (0,) * len(shape))


def smem_spec():
    return pl.BlockSpec(memory_space=pltpu.SMEM)


def vmem_spec():
    return pl.BlockSpec(memory_space=pltpu.VMEM)


def hbm_spec():
    return pl.BlockSpec(memory_space=pltpu.HBM)


def ask_kernel(candidates_in, home_in, loads_in, out, candidates, home, loads, sems):
    copies = [
        pltpu.make_async_copy(source, target, sems.at[n])
        for n, (source, target) in enumerate(((candidates_in, candidates), (home_in, home), (loads_in, loads)))
    ]
    for copy in copies:
        copy.start()
    for copy in copies:
        copy.wait()
    row = lax.broadcasted_iota(jnp.int32, (ROWS, LANE), 0)
    lane = lax.broadcasted_iota(jnp.int32, (ROWS, LANE), 1)
    slots = [home[candidates[n // CAND, n % CAND]] for n in range(REQ)]
    common = jnp.zeros((ROWS, LANE), F32)
    for n, slot in enumerate(slots):
        common = jnp.where((row == 1) & (lane == n), (slot // PAN_DEV).astype(F32), common)
        common = jnp.where((row == 2) & (lane == n), (slot % PAN_DEV).astype(F32), common)
    for o in range(N_CENT):
        tile = common
        for n, slot in enumerate(slots):
            here = jnp.where(slot // PAN_DEV == o, slot % PAN_DEV, 0).astype(F32)
            tile = jnp.where((row == 0) & (lane == n // CAND), tile + here, tile)
        for t in range(LOAD_TILES):
            out[o, t] = loads[t * ROWS : (t + 1) * ROWS]
        out[o, LOAD_TILES] = tile.astype(BF16)


def ask(candidates, home, loads):
    return pl.pallas_call(
        ask_kernel,
        in_specs=[hbm_spec()] * 3,
        out_specs=vmem_spec(),
        out_shape=jax.ShapeDtypeStruct((N_CENT, LOAD_TILES + 1, ROWS, LANE), BF16),
        scratch_shapes=[
            pltpu.SMEM(candidates.shape, jnp.int32),
            pltpu.SMEM(home.shape, jnp.int32),
            pltpu.VMEM(loads.shape, BF16),
            pltpu.SemaphoreType.DMA((3,)),
        ],
        compiler_params=params(60),
        cost_estimate=pl.CostEstimate(flops=1 << 16, bytes_accessed=1 << 18, transcendentals=0),
    )(candidates, home, loads)


def pick_kernel(ids, table, out, sems):
    copies = [pltpu.make_async_copy(table.at[ids[n]], out.at[n], sems.at[n]) for n in range(out.shape[0])]
    for copy in copies:
        copy.start()
    for copy in copies:
        copy.wait()


def pick_panels(ids, table):
    count = ids.shape[0]
    return pl.pallas_call(
        pick_kernel,
        out_shape=jax.ShapeDtypeStruct((count, PANEL, WIDTH), BF16),
        in_specs=[smem_spec(), hbm_spec()],
        out_specs=vmem_spec(),
        scratch_shapes=[pltpu.SemaphoreType.DMA((count,))],
        compiler_params=params(56),
        cost_estimate=pl.CostEstimate(flops=0, bytes_accessed=4 * count * PANEL * WIDTH, transcendentals=0),
    )(ids, table)


def score_kernel(target, points, arrived, surcharge, out, members, centers, shares, sems):
    step = 256
    steps = GROUP // step

    def land(n):
        rows = pl.ds(n * PANEL, PANEL)
        return pltpu.make_async_copy(arrived.at[target[n]], centers.at[rows], sems.at[0, n])

    def bring(n):
        rows = pl.ds(n * step, step)
        return pltpu.make_async_copy(points.at[rows], members.at[rows], sems.at[1, n])

    for group in range(GROUPS_DEV):
        for j in range(CAND):
            land(group * CAND + j).start()
        for s in range(steps):
            bring(group * steps + s).start()
    lane = lax.broadcasted_iota(jnp.int32, (PANEL, LANE), 1)
    tile = jnp.zeros((PANEL, LANE), F32)
    for group in range(GROUPS_DEV):
        for j in range(CAND):
            land(group * CAND + j).wait()
        for s in range(steps):
            bring(group * steps + s).wait()
        mine = centers[group * CAND * PANEL : (group + 1) * CAND * PANEL, :]
        wide = mine.astype(F32)
        squares = jnp.sum(wide * wide, axis=1, keepdims=True)
        bias = (squares * (1.0 / sharpness_divisor) + evenness_coefficient * surcharge[group]) * LOG2E
        weights = jnp.zeros((CAND * PANEL, LANE), F32)
        for s in range(steps):
            block = members[group * GROUP + s * step : group * GROUP + (s + 1) * step, :]
            inner = lax.dot_general(mine, block, (((1,), (1,)), ((), ())), preferred_element_type=F32)
            logits = inner * (2.0 / sharpness_divisor * LOG2E) - bias
            highest = jnp.max(logits, axis=0, keepdims=True)
            raised = jnp.exp2(logits - highest)
            scale = 1.0 / jnp.sum(raised, axis=0, keepdims=True)
            share = (raised * scale).astype(BF16)
            shares[:, s * step : (s + 1) * step] = share
            rounded = share.astype(F32)
            for part in range(step // LANE):
                weights = weights + rounded[:, part * LANE : (part + 1) * LANE]
        weight = jnp.sum(weights, axis=1, keepdims=True)
        coarse = weight.astype(BF16).astype(F32)
        fine = weight - coarse
        for j in range(CAND):
            rows = slice(j * PANEL, (j + 1) * PANEL)
            tile = jnp.where(lane == group * CAND + j, coarse[rows], tile)
            tile = jnp.where(lane == REQ + group * CAND + j, fine[rows], tile)
        wide_step = 256
        for s in range(WIDTH // wide_step):
            part = lax.dot_general(
                shares[...],
                members[group * GROUP : (group + 1) * GROUP, s * wide_step : (s + 1) * wide_step],
                (((1,), (0,)), ((), ())),
                preferred_element_type=F32,
            ).astype(BF16)
            for t in range(wide_step // LANE):
                half, tile_at = divmod(s * (wide_step // LANE) + t, TILES)
                for j in range(CAND):
                    for block_at in range(PANEL // ROWS):
                        row = j * PANEL + block_at * ROWS
                        out[block_at * 2 + half, (group * CAND + j) * TILES + tile_at] = part[
                            row : row + ROWS, t * LANE : (t + 1) * LANE
                        ]
    tile = tile.astype(BF16)
    for block_at in range(PANEL // ROWS):
        for half in range(2):
            out[block_at * 2 + half, REQ * TILES] = tile[block_at * ROWS : (block_at + 1) * ROWS]


def score(target, points, arrived, surcharge):
    return pl.pallas_call(
        score_kernel,
        in_specs=[smem_spec(), hbm_spec(), hbm_spec(), vmem_spec()],
        out_specs=vmem_spec(),
        out_shape=jax.ShapeDtypeStruct((N_PTS, SEND_TILES, ROWS, LANE), BF16),
        scratch_shapes=[
            pltpu.VMEM((GROUPS_DEV * GROUP, WIDTH), BF16),
            pltpu.VMEM((GROUPS_DEV * CAND * PANEL, WIDTH), BF16),
            pltpu.VMEM((CAND * PANEL, GROUP), BF16),
            pltpu.SemaphoreType.DMA((2, 8)),
        ],
        compiler_params=params(48),
        cost_estimate=pl.CostEstimate(flops=4 << 30, bytes_accessed=10 * MIB, transcendentals=1 << 20),
    )(target, points, arrived, surcharge)


def add_pieces(places, source, total):
    def add(s, carry):
        for i in range(REQ):
            at = places[s * REQ + i] * TILES
            total[pl.ds(at, TILES)] += source[s, i * TILES : (i + 1) * TILES].astype(F32)
        return carry

    lax.fori_loop(0, N_PTS, add, 0)


def sum_weights(lanes, source):
    panel = lax.broadcasted_iota(jnp.int32, (CHIPS * PAN_DEV, LANE), 0)
    weights = jnp.zeros((ROWS, CHIPS * PAN_DEV), F32)
    for n in range(N_PTS):
        chosen = jnp.where(panel == lanes[n : n + 1, :], 1.0, 0.0).astype(BF16)
        weights = weights + lax.dot_general(
            source[n, REQ * TILES], chosen, (((1,), (1,)), ((), ())), preferred_element_type=F32
        )
    return weights


def spread_mine_kernel(places, mine, lanes, total, total_weights):
    total[...] = jnp.zeros_like(total)
    add_pieces(places, mine, total)
    total_weights[...] = sum_weights(lanes, mine)


def spread_mate_kernel(rows, places, mate, lanes, total, total_weights, total_out, own_weights, out1, out2, out3):
    del total
    add_pieces(places, mate, total_out)
    weights = total_weights[...] + sum_weights(lanes, mate)
    coarse = weights.astype(BF16)
    fine = (weights - coarse.astype(F32)).astype(BF16)
    own_weights[...] = weights[:, 0:LANE]
    for d, out in ((1, out1), (2, out2), (3, out3)):
        first = DENSE + (d - 1) * rows * TILES
        out[0 : rows * TILES] = total_out[first : first + rows * TILES].astype(BF16)
        out[rows * TILES, :, 0:PAN_DEV] = coarse[:, d * PAN_DEV : (d + 1) * PAN_DEV]
        out[rows * TILES, :, PAN_DEV:LANE] = fine[:, d * PAN_DEV : (d + 1) * PAN_DEV]


def spread_mine(rows, places, lanes, mine):
    return pl.pallas_call(
        spread_mine_kernel,
        in_specs=[smem_spec(), vmem_spec(), vmem_spec()],
        out_specs=[vmem_spec(), vmem_spec()],
        out_shape=[
            jax.ShapeDtypeStruct(((PAN_DEV + 3 * rows + 1) * TILES, ROWS, LANE), F32),
            jax.ShapeDtypeStruct((ROWS, CHIPS * PAN_DEV), F32),
        ],
        compiler_params=params(16),
        cost_estimate=pl.CostEstimate(flops=1 << 21, bytes_accessed=8 * MIB, transcendentals=0),
    )(places, mine, lanes)


def spread_mate(rows, places, lanes, mate, total, total_weights):
    chunk = jax.ShapeDtypeStruct((rows * TILES + 1, ROWS, LANE), BF16)
    return pl.pallas_call(
        functools.partial(spread_mate_kernel, rows),
        in_specs=[smem_spec()] + [vmem_spec()] * 4,
        out_specs=[vmem_spec()] * 5,
        out_shape=[
            jax.ShapeDtypeStruct(total.shape, F32), jax.ShapeDtypeStruct((ROWS, LANE), F32), chunk, chunk, chunk,
        ],
        input_output_aliases={3: 0},
        compiler_params=params(16),
        cost_estimate=pl.CostEstimate(flops=1 << 21, bytes_accessed=8 * MIB, transcendentals=0),
    )(places, mate, lanes, total, total_weights)


def finish_kernel(rows, numbers, own, own_weights, in1, in2, in3, lanes, table, out, total, old, sem):
    row = pl.multiple_of(numbers[0] // 2 * ROWS, ROWS)
    column = pl.multiple_of(numbers[0] % 2 * HALF, HALF)
    fetch = pltpu.make_async_copy(table.at[:, pl.ds(row, ROWS), pl.ds(column, HALF)], old, sem)
    fetch.start()
    weights = own_weights[:, 0:PAN_DEV]
    panel = lax.broadcasted_iota(jnp.int32, (PAN_DEV, LANE), 0)
    total[...] = own[0:DENSE]
    for d, arrived in enumerate((in1, in2, in3)):
        chosen = jnp.where(panel == lanes[d : d + 1, :], 1.0, 0.0).astype(BF16)
        weights = weights + lax.dot_general(
            arrived[rows * TILES], chosen, (((1,), (1,)), ((), ())), preferred_element_type=F32
        )
        first = 4 + d * rows

        def add(n, carry, arrived=arrived, first=first):
            at = numbers[first + n] * TILES
            total[pl.ds(at, TILES)] += arrived[pl.ds(n * TILES, TILES)].astype(F32)
            return carry

        lax.fori_loop(0, numbers[1 + d], add, 0)
    inverse = 1.0 / (weights + prior_mass)
    fetch.wait()
    for q in range(PAN_DEV):
        scale = jnp.broadcast_to(inverse[:, q : q + 1], (ROWS, LANE))
        for t in range(TILES):
            previous = old[q, :, t * LANE : (t + 1) * LANE].astype(F32)
            fresh = (total[q * TILES + t] + prior_mass * previous) * scale
            out[q // CAND, (q % CAND) * TILES + t] = fresh.astype(BF16)
    coarse = weights.astype(BF16)
    fine = (weights - coarse.astype(F32)).astype(BF16)
    for p in range(N_PTS):
        out[p, CAND * TILES, :, 0:PAN_DEV] = coarse
        out[p, CAND * TILES, :, PAN_DEV:LANE] = fine


def finish(rows, numbers, own, own_weights, arrived, lanes, table):
    return pl.pallas_call(
        functools.partial(finish_kernel, rows),
        in_specs=[smem_spec()] + [vmem_spec()] * 6 + [hbm_spec()],
        out_specs=vmem_spec(),
        out_shape=jax.ShapeDtypeStruct((N_PTS, CAND * TILES + 1, ROWS, LANE), BF16),
        scratch_shapes=[
            pltpu.VMEM((DENSE, ROWS, LANE), F32),
            pltpu.VMEM((PAN_DEV, ROWS, HALF), BF16),
            pltpu.SemaphoreType.DMA,
        ],
        compiler_params=params(48),
        cost_estimate=pl.CostEstimate(flops=1 << 22, bytes_accessed=6 * MIB, transcendentals=0),
    )(numbers, own, own_weights, *arrived, lanes, table)


def place_kernel(me, pieces, out, loads):
    for block_at in range(PANEL // ROWS):
        for half in range(2):
            for q in range(CAND):
                for t in range(TILES):
                    column = half * HALF + t * LANE
                    out[q, block_at * ROWS : (block_at + 1) * ROWS, column : column + LANE] = pieces[
                        block_at * 2 + half, q * TILES + t
                    ]
    lane = lax.broadcasted_iota(jnp.int32, (ROWS, LANE), 1)
    row = lax.broadcasted_iota(jnp.int32, (ROWS, LANE), 0)
    wanted = me[0] * CAND + row
    chosen = jnp.where((row < CAND) & (lane % PAN_DEV == wanted), 1.0, 0.0).astype(BF16)
    for block_at in range(PANEL // ROWS):
        pair = pieces[block_at * 2, CAND * TILES]
        part = lax.dot_general(chosen, pair, (((1,), (1,)), ((), ())), preferred_element_type=F32)
        loads[:, block_at * ROWS : (block_at + 1) * ROWS] = part[0:CAND]


def place(me, pieces):
    return pl.pallas_call(
        place_kernel,
        grid=(1,),
        in_specs=[smem_spec(), whole(pieces.shape)],
        out_specs=[whole((CAND, PANEL, WIDTH)), whole((CAND, PANEL))],
        out_shape=[
            jax.ShapeDtypeStruct((CAND, PANEL, WIDTH), BF16),
            jax.ShapeDtypeStruct((CAND, PANEL), F32),
        ],
        compiler_params=params(32),
        cost_estimate=pl.CostEstimate(flops=1 << 20, bytes_accessed=2 * MIB, transcendentals=0),
    )(me, pieces)


def shift(dy, dk):
    return [(y * 2 + k, ((y + dy) % CHIPS) * 2 + (k + dk) % 2) for y in range(CHIPS) for k in range(2)]


def spread_out(x, place, dz, dx):
    held = [x]
    for d in range(1, SIDE):
        pairs = [
            (ix * SIDE + iz, (ix + d * dx) % SIDE * SIDE + (iz + d * dz) % SIDE)
            for ix in range(SIDE)
            for iz in range(SIDE)
        ]
        held.append(lax.ppermute(x, "pts", pairs))
    held = jnp.stack(held)
    at = (place - jnp.arange(SIDE, dtype=jnp.int32)) % SIDE
    return jnp.stack([jnp.sum(jnp.where((at == n).reshape((SIDE,) + (1,) * x.ndim), held, 0), axis=0) for n in range(SIDE)])


def exchange(x, axis):
    return lax.all_to_all(x, axis, split_axis=0, concat_axis=0, tiled=True)


def local(points, centroids, prev_loads, candidates, panel_home):
    me = lax.axis_index("pts")
    here = lax.axis_index("cent")
    chip, core = here // 2, here % 2
    shelf = centroids.reshape(PAN_DEV, PANEL, WIDTH)

    with jax.named_scope("requests"):
        answered = exchange(ask(candidates, panel_home, prev_loads.reshape(PAN_DEV, PANEL)), "cent")
        asked = answered[:, LOAD_TILES, 0, 0:GROUPS_DEV].astype(jnp.int32).reshape(-1)

    with jax.named_scope("gather_panels"):
        ready = pick_panels(asked, shelf)
        arrived = exchange(ready.reshape(N_CENT, GROUPS_DEV, PANEL, WIDTH), "cent")
        arrived = arrived.reshape(N_CENT * GROUPS_DEV, PANEL, WIDTH)

    with jax.named_scope("own_requests"):
        slots = jnp.sum(
            jnp.where(candidates.reshape(REQ)[:, None] == jnp.arange(panel_home.shape[0], dtype=jnp.int32), panel_home[None, :], 0),
            axis=1,
        )
        target = slots // PAN_DEV * GROUPS_DEV + jnp.arange(REQ, dtype=jnp.int32) // CAND

    with jax.named_scope("all_requests"):
        ring = answered[:, LOAD_TILES, 1:3, 0:REQ].astype(jnp.int32)
        ring = ring[:, 0] * PAN_DEV + ring[:, 1]
        line = spread_out(ring, me % SIDE, 1, 0)
        everyone = spread_out(line, me // SIDE, 0, 1).reshape(N_PTS, N_CENT, REQ)
        numbers = jnp.arange(N_CENT * PAN_DEV, dtype=jnp.int32)
        by_chip = jnp.transpose(everyone.reshape(N_PTS, CHIPS, 2 * REQ), (1, 0, 2)).reshape(CHIPS, -1)
        asked_by = jnp.any(by_chip[:, :, None] == numbers, axis=1).reshape(CHIPS, N_CENT, PAN_DEV)
        below = jnp.arange(PAN_DEV)[:, None] < jnp.arange(PAN_DEV)[None, :]
        ranks = lax.dot_general(
            asked_by.astype(BF16), below.astype(BF16), (((2,), (0,)), ((), ())), preferred_element_type=F32
        ).astype(jnp.int32)
        lengths = jnp.sum(asked_by.astype(jnp.int32), axis=2)
        off_chip = jnp.arange(N_CENT)[None, :] // 2 != jnp.arange(CHIPS)[:, None]
        too_long = jnp.any(off_chip & (lengths > LISTED))

        pair = jnp.stack(
            [lax.dynamic_index_in_dim(everyone, at, 1, keepdims=False) for at in (here, chip * 2 + 1 - core)]
        ).reshape(2 * N_PTS, REQ)
        owner = pair // PAN_DEV
        relative = (owner // 2 - chip) % CHIPS
        my_ranks = lax.dynamic_index_in_dim(ranks, chip, 0, keepdims=False).reshape(-1)
        rank = jnp.sum(jnp.where(pair[:, :, None] == numbers, my_ranks, 0), axis=2)
        ours = owner % 2 == core

        def sender(rows, rank):
            at = jnp.where(relative == 0, pair % PAN_DEV, rank)
            known = ours & ((relative == 0) | (rank < rows))
            first = jnp.where(relative == 0, 0, PAN_DEV + (relative - 1) * rows)
            places = jnp.where(known, first + at, PAN_DEV + 3 * rows).reshape(-1)
            lane = jnp.where(known, relative * PAN_DEV + at, CHIPS * PAN_DEV)
            lanes = jnp.pad(
                jnp.concatenate([lane, lane], axis=1), ((0, 0), (0, LANE - 2 * REQ)), constant_values=CHIPS * PAN_DEV
            )
            return places, lanes

        def receiver(rows, count, panels):
            numbers = jnp.concatenate([me.reshape(1), count, panels[:, :rows].reshape(-1)])
            lane = jnp.where(jnp.arange(PAN_DEV) < jnp.minimum(count, rows)[:, None], panels, PAN_DEV)
            return numbers, jnp.concatenate([lane, lane], axis=1)

        behind = [(chip - d) % CHIPS for d in range(1, CHIPS)]
        pick = lambda x, y: lax.dynamic_index_in_dim(lax.dynamic_index_in_dim(x, y, 0, False), here, 0, False)
        named = jnp.stack([pick(asked_by, y) for y in behind])
        order = jnp.stack([pick(ranks, y) for y in behind])
        spots = jnp.arange(PAN_DEV, dtype=jnp.int32)
        listed = jnp.sum(
            jnp.where(named[:, None, :] & (order[:, None, :] == spots[None, :, None]), spots, 0), axis=2
        )
        count = jnp.minimum(jnp.sum(named.astype(jnp.int32), axis=1), LISTED)
        short = sender(LISTED, rank) + receiver(LISTED, count, listed)
        target, too_long, short = lax.optimization_barrier((target, too_long, short))

    with jax.named_scope("loads"):
        load_table = answered[:, :LOAD_TILES].reshape(N_CENT * PAN_DEV, PANEL)
        loads = jnp.take(load_table, slots, axis=0, mode="clip").astype(F32)
        surcharge = jnp.log(loads).reshape(GROUPS_DEV, CAND * PANEL, 1)

    with jax.named_scope("score"):
        pieces = score(target, points, arrived, surcharge)

    with jax.named_scope("split_pieces"):
        mine = exchange(pieces, "pts")
        mate = lax.ppermute(mine, "cent", shift(0, 1))

    def half(x, n):
        return x.reshape(2, -1)[n] if x.ndim == 1 else x.reshape(2, -1, LANE)[n]

    def start_sums(rows, places, lanes):
        return spread_mine(rows, half(places, 0), half(lanes, 0), mine)

    def sum_over_chips(rows, begun, places, lanes, numbers, back_lanes):
        own, own_weights, *far = spread_mate(rows, half(places, 1), half(lanes, 1), mate, *begun)
        back = [lax.ppermute(far[d - 1], "cent", shift(d, 0)) for d in range(1, CHIPS)]
        return finish(rows, numbers, own, own_weights, back, back_lanes, shelf)

    def send_all():
        everything = jnp.broadcast_to(spots, (CHIPS - 1, PAN_DEV))
        count = jnp.full((CHIPS - 1,), PAN_DEV, jnp.int32)
        to = sender(PAN_DEV, pair % PAN_DEV)
        return sum_over_chips(
            PAN_DEV, start_sums(PAN_DEV, *to), *to, *receiver(PAN_DEV, count, everything)
        )

    with jax.named_scope("sum_over_chips"):
        begun = start_sums(LISTED, *short[:2])
        begun, mate = lax.optimization_barrier((begun, mate))
        fresh = lax.cond(too_long, send_all, lambda: sum_over_chips(LISTED, begun, *short))

    with jax.named_scope("place"):
        new_centroids, new_loads = place(me.reshape(1), exchange(fresh, "pts"))
    return new_centroids.reshape(CAND * PANEL, WIDTH), new_loads.reshape(CAND * PANEL)


def solution(mesh):
    placed = (P(("pts", "cent"), None), P("cent", None), P("cent"), P(("pts", "cent"), None), P())
    return jax.shard_map(
        local,
        mesh=mesh,
        in_specs=placed,
        out_specs=(P(("cent", "pts"), None), P(("cent", "pts"))),
        check_vma=False,
    )
```

```python
import functools

import jax
import jax.numpy as jnp
from jax import lax
from jax.experimental import pallas as pl
from jax.experimental.pallas import tpu as pltpu
from jax.sharding import PartitionSpec as P

PANEL = 128
GROUP = 1024
CAND = 4
GROUPS_DEV = 2
REQ = CAND * GROUPS_DEV
PAN_DEV = 64
WIDTH = 1024
N_CENT = 8
CHIPS = 4
N_PTS = 16
ROWS = 16
HALF = 512
LANE = 128
TILES = HALF // LANE
SEND_TILES = REQ * TILES + 1
DENSE = PAN_DEV * TILES
LOAD_TILES = PAN_DEV // ROWS
LISTED = 36

sharpness_divisor = 16.0
evenness_coefficient = 1.0
prior_mass = 1.0

BF16 = jnp.bfloat16
F32 = jnp.float32
MIB = 1 << 20
LOG2E = 1.4426950408889634


def params(mib):
    return pltpu.CompilerParams(vmem_limit_bytes=mib * MIB)


def whole(shape):
    return pl.BlockSpec(shape, lambda *_: (0,) * len(shape))


def smem_spec():
    return pl.BlockSpec(memory_space=pltpu.SMEM)


def vmem_spec():
    return pl.BlockSpec(memory_space=pltpu.VMEM)


def hbm_spec():
    return pl.BlockSpec(memory_space=pltpu.HBM)


def ask_kernel(candidates_in, home_in, loads_in, out, candidates, home, loads, sems):
    copies = [
        pltpu.make_async_copy(source, target, sems.at[n])
        for n, (source, target) in enumerate(((candidates_in, candidates), (home_in, home), (loads_in, loads)))
    ]
    for copy in copies:
        copy.start()
    for copy in copies:
        copy.wait()
    row = lax.broadcasted_iota(jnp.int32, (ROWS, LANE), 0)
    lane = lax.broadcasted_iota(jnp.int32, (ROWS, LANE), 1)
    slots = [home[candidates[n // CAND, n % CAND]] for n in range(REQ)]
    common = jnp.zeros((ROWS, LANE), F32)
    for n, slot in enumerate(slots):
        common = jnp.where((row == 1) & (lane == n), (slot // PAN_DEV).astype(F32), common)
        common = jnp.where((row == 2) & (lane == n), (slot % PAN_DEV).astype(F32), common)
    for o in range(N_CENT):
        tile = common
        for n, slot in enumerate(slots):
            here = jnp.where(slot // PAN_DEV == o, slot % PAN_DEV, 0).astype(F32)
            tile = jnp.where((row == 0) & (lane == n // CAND), tile + here, tile)
        for t in range(LOAD_TILES):
            out[o, t] = loads[t * ROWS : (t + 1) * ROWS]
        out[o, LOAD_TILES] = tile.astype(BF16)


def ask(candidates, home, loads):
    return pl.pallas_call(
        ask_kernel,
        in_specs=[hbm_spec()] * 3,
        out_specs=vmem_spec(),
        out_shape=jax.ShapeDtypeStruct((N_CENT, LOAD_TILES + 1, ROWS, LANE), BF16),
        scratch_shapes=[
            pltpu.SMEM(candidates.shape, jnp.int32),
            pltpu.SMEM(home.shape, jnp.int32),
            pltpu.VMEM(loads.shape, BF16),
            pltpu.SemaphoreType.DMA((3,)),
        ],
        compiler_params=params(60),
        cost_estimate=pl.CostEstimate(flops=1 << 16, bytes_accessed=1 << 18, transcendentals=0),
    )(candidates, home, loads)


def pick_kernel(readers, ids, place, table, *refs):
    *outs, held, sems = refs

    def fetch(n, g):
        reader = (place[0] // 2 + readers[n] // 2) % CHIPS * 2 + (place[0] + readers[n]) % 2
        at = n * GROUPS_DEV + g
        return pltpu.make_async_copy(table.at[ids[reader * GROUPS_DEV + g]], held.at[at], sems.at[0, at])

    def put(n, g):
        at = n * GROUPS_DEV + g
        return pltpu.make_async_copy(held.at[at], outs[n].at[g], sems.at[1, at])

    every = [(n, g) for n in range(len(readers)) for g in range(GROUPS_DEV)]
    for at in every:
        fetch(*at).start()
    for at in every:
        fetch(*at).wait()
        put(*at).start()
    for at in every:
        put(*at).wait()


def pick_panels(readers, ids, place, table):
    count = len(readers) * GROUPS_DEV
    return pl.pallas_call(
        functools.partial(pick_kernel, readers),
        out_shape=[jax.ShapeDtypeStruct((GROUPS_DEV, PANEL, WIDTH), BF16)] * len(readers),
        in_specs=[smem_spec(), smem_spec(), hbm_spec()],
        out_specs=[hbm_spec()] * len(readers),
        scratch_shapes=[pltpu.VMEM((count, PANEL, WIDTH), BF16), pltpu.SemaphoreType.DMA((2, count))],
        compiler_params=params(60),
        cost_estimate=pl.CostEstimate(flops=0, bytes_accessed=4 * count * PANEL * WIDTH, transcendentals=0),
    )(ids, place, table)


def score_kernel(owners, *refs):
    panels, (points, surcharge, out, members, centers, shares, sems) = refs[:N_CENT], refs[N_CENT:]
    step = 256
    steps = GROUP // step

    def land(n, o):
        rows = pl.ds(n * PANEL, PANEL)
        return pltpu.make_async_copy(panels[o].at[n // CAND], centers.at[rows], sems.at[0, n])

    def bring(n):
        rows = pl.ds(n * step, step)
        return pltpu.make_async_copy(points.at[rows], members.at[rows], sems.at[1, n])

    for group in range(GROUPS_DEV):
        for j in range(CAND):
            for o in range(N_CENT):

                @pl.when(owners[group * CAND + j] == o)
                def _(n=group * CAND + j, o=o):
                    land(n, o).start()

        for s in range(steps):
            bring(group * steps + s).start()
    lane = lax.broadcasted_iota(jnp.int32, (PANEL, LANE), 1)
    tile = jnp.zeros((PANEL, LANE), F32)
    for group in range(GROUPS_DEV):
        for j in range(CAND):
            land(group * CAND + j, 0).wait()
        for s in range(steps):
            bring(group * steps + s).wait()
        mine = centers[group * CAND * PANEL : (group + 1) * CAND * PANEL, :]
        wide = mine.astype(F32)
        squares = jnp.sum(wide * wide, axis=1, keepdims=True)
        bias = (squares * (1.0 / sharpness_divisor) + evenness_coefficient * surcharge[group]) * LOG2E
        weights = jnp.zeros((CAND * PANEL, LANE), F32)
        for s in range(steps):
            block = members[group * GROUP + s * step : group * GROUP + (s + 1) * step, :]
            inner = lax.dot_general(mine, block, (((1,), (1,)), ((), ())), preferred_element_type=F32)
            logits = inner * (2.0 / sharpness_divisor * LOG2E) - bias
            highest = jnp.max(logits, axis=0, keepdims=True)
            raised = jnp.exp2(logits - highest)
            scale = 1.0 / jnp.sum(raised, axis=0, keepdims=True)
            share = (raised * scale).astype(BF16)
            shares[:, s * step : (s + 1) * step] = share
            rounded = share.astype(F32)
            for part in range(step // LANE):
                weights = weights + rounded[:, part * LANE : (part + 1) * LANE]
        weight = jnp.sum(weights, axis=1, keepdims=True)
        coarse = weight.astype(BF16).astype(F32)
        fine = weight - coarse
        for j in range(CAND):
            rows = slice(j * PANEL, (j + 1) * PANEL)
            tile = jnp.where(lane == group * CAND + j, coarse[rows], tile)
            tile = jnp.where(lane == REQ + group * CAND + j, fine[rows], tile)
        wide_step = 256
        for s in range(WIDTH // wide_step):
            part = lax.dot_general(
                shares[...],
                members[group * GROUP : (group + 1) * GROUP, s * wide_step : (s + 1) * wide_step],
                (((1,), (0,)), ((), ())),
                preferred_element_type=F32,
            ).astype(BF16)
            for t in range(wide_step // LANE):
                half, tile_at = divmod(s * (wide_step // LANE) + t, TILES)
                for j in range(CAND):
                    for block_at in range(PANEL // ROWS):
                        row = j * PANEL + block_at * ROWS
                        out[block_at * 2 + half, (group * CAND + j) * TILES + tile_at] = part[
                            row : row + ROWS, t * LANE : (t + 1) * LANE
                        ]
    tile = tile.astype(BF16)
    for block_at in range(PANEL // ROWS):
        for half in range(2):
            out[block_at * 2 + half, REQ * TILES] = tile[block_at * ROWS : (block_at + 1) * ROWS]


def score(owners, panels, points, surcharge):
    return pl.pallas_call(
        score_kernel,
        in_specs=[smem_spec()] + [hbm_spec()] * (N_CENT + 1) + [vmem_spec()],
        out_specs=vmem_spec(),
        out_shape=jax.ShapeDtypeStruct((N_PTS, SEND_TILES, ROWS, LANE), BF16),
        scratch_shapes=[
            pltpu.VMEM((GROUPS_DEV * GROUP, WIDTH), BF16),
            pltpu.VMEM((GROUPS_DEV * CAND * PANEL, WIDTH), BF16),
            pltpu.VMEM((CAND * PANEL, GROUP), BF16),
            pltpu.SemaphoreType.DMA((2, 8)),
        ],
        compiler_params=params(45),
        cost_estimate=pl.CostEstimate(flops=4 << 30, bytes_accessed=10 * MIB, transcendentals=1 << 20),
    )(owners, *panels, points, surcharge)


def add_pieces(places, source, total):
    def add(s, carry):
        for i in range(REQ):
            at = places[s * REQ + i] * TILES
            total[pl.ds(at, TILES)] += source[s, i * TILES : (i + 1) * TILES].astype(F32)
        return carry

    lax.fori_loop(0, N_PTS, add, 0)


def sum_weights(lanes, source):
    panel = lax.broadcasted_iota(jnp.int32, (CHIPS * PAN_DEV, LANE), 0)
    weights = jnp.zeros((ROWS, CHIPS * PAN_DEV), F32)
    for n in range(N_PTS):
        chosen = jnp.where(panel == lanes[n : n + 1, :], 1.0, 0.0).astype(BF16)
        weights = weights + lax.dot_general(
            source[n, REQ * TILES], chosen, (((1,), (1,)), ((), ())), preferred_element_type=F32
        )
    return weights


def spread_mine_kernel(places, mine, lanes, total, total_weights):
    total[...] = jnp.zeros_like(total)
    add_pieces(places, mine, total)
    total_weights[...] = sum_weights(lanes, mine)


def spread_mate_kernel(rows, places, mate, lanes, total, total_weights, total_out, own_weights, out1, out2, out3):
    del total
    add_pieces(places, mate, total_out)
    weights = total_weights[...] + sum_weights(lanes, mate)
    coarse = weights.astype(BF16)
    fine = (weights - coarse.astype(F32)).astype(BF16)
    own_weights[...] = weights[:, 0:LANE]
    for d, out in ((1, out1), (2, out2), (3, out3)):
        first = DENSE + (d - 1) * rows * TILES
        out[0 : rows * TILES] = total_out[first : first + rows * TILES].astype(BF16)
        out[rows * TILES, :, 0:PAN_DEV] = coarse[:, d * PAN_DEV : (d + 1) * PAN_DEV]
        out[rows * TILES, :, PAN_DEV:LANE] = fine[:, d * PAN_DEV : (d + 1) * PAN_DEV]


def spread_mine(rows, places, lanes, mine):
    return pl.pallas_call(
        spread_mine_kernel,
        in_specs=[smem_spec(), vmem_spec(), vmem_spec()],
        out_specs=[vmem_spec(), vmem_spec()],
        out_shape=[
            jax.ShapeDtypeStruct(((PAN_DEV + 3 * rows + 1) * TILES, ROWS, LANE), F32),
            jax.ShapeDtypeStruct((ROWS, CHIPS * PAN_DEV), F32),
        ],
        compiler_params=params(16),
        cost_estimate=pl.CostEstimate(flops=1 << 21, bytes_accessed=8 * MIB, transcendentals=0),
    )(places, mine, lanes)


def spread_mate(rows, places, lanes, mate, total, total_weights):
    chunk = jax.ShapeDtypeStruct((rows * TILES + 1, ROWS, LANE), BF16)
    return pl.pallas_call(
        functools.partial(spread_mate_kernel, rows),
        in_specs=[smem_spec()] + [vmem_spec()] * 4,
        out_specs=[vmem_spec()] * 5,
        out_shape=[
            jax.ShapeDtypeStruct(total.shape, F32), jax.ShapeDtypeStruct((ROWS, LANE), F32), chunk, chunk, chunk,
        ],
        input_output_aliases={3: 0},
        compiler_params=params(16),
        cost_estimate=pl.CostEstimate(flops=1 << 21, bytes_accessed=8 * MIB, transcendentals=0),
    )(places, mate, lanes, total, total_weights)


def finish_kernel(rows, numbers, own, own_weights, in1, in2, in3, lanes, table, out, total, old, sem):
    row = pl.multiple_of(numbers[0] // 2 * ROWS, ROWS)
    column = pl.multiple_of(numbers[0] % 2 * HALF, HALF)
    fetch = pltpu.make_async_copy(table.at[:, pl.ds(row, ROWS), pl.ds(column, HALF)], old, sem)
    fetch.start()
    weights = own_weights[:, 0:PAN_DEV]
    panel = lax.broadcasted_iota(jnp.int32, (PAN_DEV, LANE), 0)
    total[...] = own[0:DENSE]
    for d, arrived in enumerate((in1, in2, in3)):
        chosen = jnp.where(panel == lanes[d : d + 1, :], 1.0, 0.0).astype(BF16)
        weights = weights + lax.dot_general(
            arrived[rows * TILES], chosen, (((1,), (1,)), ((), ())), preferred_element_type=F32
        )
        first = 4 + d * rows

        def add(n, carry, arrived=arrived, first=first):
            at = numbers[first + n] * TILES
            total[pl.ds(at, TILES)] += arrived[pl.ds(n * TILES, TILES)].astype(F32)
            return carry

        lax.fori_loop(0, numbers[1 + d], add, 0)
    inverse = 1.0 / (weights + prior_mass)
    fetch.wait()
    for q in range(PAN_DEV):
        scale = jnp.broadcast_to(inverse[:, q : q + 1], (ROWS, LANE))
        for t in range(TILES):
            previous = old[q, :, t * LANE : (t + 1) * LANE].astype(F32)
            fresh = (total[q * TILES + t] + prior_mass * previous) * scale
            out[q // CAND, (q % CAND) * TILES + t] = fresh.astype(BF16)
    coarse = weights.astype(BF16)
    fine = (weights - coarse.astype(F32)).astype(BF16)
    for p in range(N_PTS):
        out[p, CAND * TILES, :, 0:PAN_DEV] = coarse
        out[p, CAND * TILES, :, PAN_DEV:LANE] = fine


def finish(rows, numbers, own, own_weights, arrived, lanes, table):
    return pl.pallas_call(
        functools.partial(finish_kernel, rows),
        in_specs=[smem_spec()] + [vmem_spec()] * 6 + [hbm_spec()],
        out_specs=vmem_spec(),
        out_shape=jax.ShapeDtypeStruct((N_PTS, CAND * TILES + 1, ROWS, LANE), BF16),
        scratch_shapes=[
            pltpu.VMEM((DENSE, ROWS, LANE), F32),
            pltpu.VMEM((PAN_DEV, ROWS, HALF), BF16),
            pltpu.SemaphoreType.DMA,
        ],
        compiler_params=params(48),
        cost_estimate=pl.CostEstimate(flops=1 << 22, bytes_accessed=6 * MIB, transcendentals=0),
    )(numbers, own, own_weights, *arrived, lanes, table)


def place_kernel(me, pieces, out, loads):
    for block_at in range(PANEL // ROWS):
        for half in range(2):
            for q in range(CAND):
                for t in range(TILES):
                    column = half * HALF + t * LANE
                    out[q, block_at * ROWS : (block_at + 1) * ROWS, column : column + LANE] = pieces[
                        block_at * 2 + half, q * TILES + t
                    ]
    lane = lax.broadcasted_iota(jnp.int32, (ROWS, LANE), 1)
    row = lax.broadcasted_iota(jnp.int32, (ROWS, LANE), 0)
    wanted = me[0] * CAND + row
    chosen = jnp.where((row < CAND) & (lane % PAN_DEV == wanted), 1.0, 0.0).astype(BF16)
    for block_at in range(PANEL // ROWS):
        pair = pieces[block_at * 2, CAND * TILES]
        part = lax.dot_general(chosen, pair, (((1,), (1,)), ((), ())), preferred_element_type=F32)
        loads[:, block_at * ROWS : (block_at + 1) * ROWS] = part[0:CAND]


def place(me, pieces):
    return pl.pallas_call(
        place_kernel,
        grid=(1,),
        in_specs=[smem_spec(), whole(pieces.shape)],
        out_specs=[whole((CAND, PANEL, WIDTH)), whole((CAND, PANEL))],
        out_shape=[
            jax.ShapeDtypeStruct((CAND, PANEL, WIDTH), BF16),
            jax.ShapeDtypeStruct((CAND, PANEL), F32),
        ],
        compiler_params=params(32),
        cost_estimate=pl.CostEstimate(flops=1 << 20, bytes_accessed=2 * MIB, transcendentals=0),
    )(me, pieces)


def shift(dy, dk):
    return [(y * 2 + k, ((y + dy) % CHIPS) * 2 + (k + dk) % 2) for y in range(CHIPS) for k in range(2)]


def exchange(x, axis):
    return lax.all_to_all(x, axis, split_axis=0, concat_axis=0, tiled=True)


def local(points, centroids, prev_loads, candidates, panel_home):
    me = lax.axis_index("pts")
    here = lax.axis_index("cent")
    chip, core = here // 2, here % 2
    shelf = centroids.reshape(PAN_DEV, PANEL, WIDTH)

    with jax.named_scope("requests"):
        answered = exchange(ask(candidates, panel_home, prev_loads.reshape(PAN_DEV, PANEL)), "cent")
        asked = answered[:, LOAD_TILES, 0, 0:GROUPS_DEV].astype(jnp.int32).reshape(-1)

    with jax.named_scope("gather_panels"):
        readers = (4, 5, 2, 6, 1, 3, 7, 0)
        ready = dict(zip(readers, pick_panels(readers, asked, here.reshape(1), shelf)))
        arrived = [ready[0]] + [lax.ppermute(ready[n], "cent", shift(n // 2, n % 2)) for n in range(1, N_CENT)]
        answered, arrived[1] = lax.optimization_barrier((answered, arrived[1]))

    with jax.named_scope("own_requests"):
        slots = jnp.sum(
            jnp.where(candidates.reshape(REQ)[:, None] == jnp.arange(panel_home.shape[0], dtype=jnp.int32), panel_home[None, :], 0),
            axis=1,
        )
        owners = slots // PAN_DEV
        seen = (chip - owners // 2) % CHIPS * 2 + (core - owners) % 2

    with jax.named_scope("all_requests"):
        ring = answered[:, LOAD_TILES, 1:3, 0:REQ].astype(jnp.int32)
        ring = ring[:, 0] * PAN_DEV + ring[:, 1]
        everyone = exchange(jnp.broadcast_to(ring, (N_PTS, N_CENT, REQ)), "pts")

        numbers = jnp.arange(N_CENT * PAN_DEV, dtype=jnp.int32)
        by_chip = jnp.transpose(everyone.reshape(N_PTS, CHIPS, 2 * REQ), (1, 0, 2)).reshape(CHIPS, -1)
        asked_by = jnp.any(by_chip[:, :, None] == numbers, axis=1).reshape(CHIPS, N_CENT, PAN_DEV)
        below = jnp.arange(PAN_DEV)[:, None] < jnp.arange(PAN_DEV)[None, :]
        ranks = lax.dot_general(
            asked_by.astype(BF16), below.astype(BF16), (((2,), (0,)), ((), ())), preferred_element_type=F32
        ).astype(jnp.int32)
        lengths = jnp.sum(asked_by.astype(jnp.int32), axis=2)
        off_chip = jnp.arange(N_CENT)[None, :] // 2 != jnp.arange(CHIPS)[:, None]
        too_long = jnp.any(off_chip & (lengths > LISTED))

        pair = jnp.stack(
            [lax.dynamic_index_in_dim(everyone, at, 1, keepdims=False) for at in (here, chip * 2 + 1 - core)]
        ).reshape(2 * N_PTS, REQ)
        owner = pair // PAN_DEV
        relative = (owner // 2 - chip) % CHIPS
        my_ranks = lax.dynamic_index_in_dim(ranks, chip, 0, keepdims=False).reshape(-1)
        rank = jnp.sum(jnp.where(pair[:, :, None] == numbers, my_ranks, 0), axis=2)
        ours = owner % 2 == core

        def sender(rows, rank):
            at = jnp.where(relative == 0, pair % PAN_DEV, rank)
            known = ours & ((relative == 0) | (rank < rows))
            first = jnp.where(relative == 0, 0, PAN_DEV + (relative - 1) * rows)
            places = jnp.where(known, first + at, PAN_DEV + 3 * rows).reshape(-1)
            lane = jnp.where(known, relative * PAN_DEV + at, CHIPS * PAN_DEV)
            lanes = jnp.pad(
                jnp.concatenate([lane, lane], axis=1), ((0, 0), (0, LANE - 2 * REQ)), constant_values=CHIPS * PAN_DEV
            )
            return places, lanes

        def receiver(rows, count, panels):
            numbers = jnp.concatenate([me.reshape(1), count, panels[:, :rows].reshape(-1)])
            lane = jnp.where(jnp.arange(PAN_DEV) < jnp.minimum(count, rows)[:, None], panels, PAN_DEV)
            return numbers, jnp.concatenate([lane, lane], axis=1)

        behind = [(chip - d) % CHIPS for d in range(1, CHIPS)]
        pick = lambda x, y: lax.dynamic_index_in_dim(lax.dynamic_index_in_dim(x, y, 0, False), here, 0, False)
        named = jnp.stack([pick(asked_by, y) for y in behind])
        order = jnp.stack([pick(ranks, y) for y in behind])
        spots = jnp.arange(PAN_DEV, dtype=jnp.int32)
        listed = jnp.sum(
            jnp.where(named[:, None, :] & (order[:, None, :] == spots[None, :, None]), spots, 0), axis=2
        )
        count = jnp.minimum(jnp.sum(named.astype(jnp.int32), axis=1), LISTED)
        short = sender(LISTED, rank) + receiver(LISTED, count, listed)
        seen, too_long, short = lax.optimization_barrier((seen, too_long, short))

    with jax.named_scope("loads"):
        load_table = answered[:, :LOAD_TILES].reshape(N_CENT * PAN_DEV, PANEL)
        loads = jnp.take(load_table, slots, axis=0, mode="clip").astype(F32)
        surcharge = jnp.log(loads).reshape(GROUPS_DEV, CAND * PANEL, 1)

    with jax.named_scope("score"):
        pieces = score(seen, arrived, points, surcharge)

    with jax.named_scope("split_pieces"):
        mine = exchange(pieces, "pts")
        mate = lax.ppermute(mine, "cent", shift(0, 1))

    def half(x, n):
        return x.reshape(2, -1)[n] if x.ndim == 1 else x.reshape(2, -1, LANE)[n]

    def start_sums(rows, places, lanes):
        return spread_mine(rows, half(places, 0), half(lanes, 0), mine)

    def sum_over_chips(rows, begun, places, lanes, numbers, back_lanes):
        own, own_weights, *far = spread_mate(rows, half(places, 1), half(lanes, 1), mate, *begun)
        back = [lax.ppermute(far[d - 1], "cent", shift(d, 0)) for d in range(1, CHIPS)]
        return finish(rows, numbers, own, own_weights, back, back_lanes, shelf)

    def send_all():
        everything = jnp.broadcast_to(spots, (CHIPS - 1, PAN_DEV))
        count = jnp.full((CHIPS - 1,), PAN_DEV, jnp.int32)
        to = sender(PAN_DEV, pair % PAN_DEV)
        return sum_over_chips(
            PAN_DEV, start_sums(PAN_DEV, *to), *to, *receiver(PAN_DEV, count, everything)
        )

    with jax.named_scope("sum_over_chips"):
        begun = start_sums(LISTED, *short[:2])
        begun, mate = lax.optimization_barrier((begun, mate))
        fresh = lax.cond(too_long, send_all, lambda: sum_over_chips(LISTED, begun, *short))

    with jax.named_scope("place"):
        new_centroids, new_loads = place(me.reshape(1), exchange(fresh, "pts"))
    return new_centroids.reshape(CAND * PANEL, WIDTH), new_loads.reshape(CAND * PANEL)


def solution(mesh):
    placed = (P(("pts", "cent"), None), P("cent", None), P("cent"), P(("pts", "cent"), None), P())
    return jax.shard_map(
        local,
        mesh=mesh,
        in_specs=placed,
        out_specs=(P(("cent", "pts"), None), P(("cent", "pts"))),
        check_vma=False,
    )
```

```python
import functools

import jax
import jax.numpy as jnp
from jax import lax
from jax.experimental import pallas as pl
from jax.experimental.pallas import tpu as pltpu
from jax.sharding import PartitionSpec as P

PANEL = 128
GROUP = 1024
CAND = 4
GROUPS_DEV = 2
REQ = CAND * GROUPS_DEV
PAN_DEV = 64
WIDTH = 1024
N_CENT = 8
CHIPS = 4
N_PTS = 16
ROWS = 16
HALF = 512
LANE = 128
TILES = HALF // LANE
SEND_TILES = REQ * TILES + 1
DENSE = PAN_DEV * TILES
LOAD_TILES = PAN_DEV // ROWS
LISTED = 34

sharpness_divisor = 16.0
evenness_coefficient = 1.0
prior_mass = 1.0

BF16 = jnp.bfloat16
F32 = jnp.float32
MIB = 1 << 20
LOG2E = 1.4426950408889634


def params(mib):
    return pltpu.CompilerParams(vmem_limit_bytes=mib * MIB)


def whole(shape):
    return pl.BlockSpec(shape, lambda *_: (0,) * len(shape))


def smem_spec():
    return pl.BlockSpec(memory_space=pltpu.SMEM)


def vmem_spec():
    return pl.BlockSpec(memory_space=pltpu.VMEM)


def hbm_spec():
    return pl.BlockSpec(memory_space=pltpu.HBM)


def ask_kernel(candidates_in, home_in, loads_in, out, candidates, home, loads, sems):
    copies = [
        pltpu.make_async_copy(source, target, sems.at[n])
        for n, (source, target) in enumerate(((candidates_in, candidates), (home_in, home), (loads_in, loads)))
    ]
    for copy in copies:
        copy.start()
    for copy in copies:
        copy.wait()
    row = lax.broadcasted_iota(jnp.int32, (ROWS, LANE), 0)
    lane = lax.broadcasted_iota(jnp.int32, (ROWS, LANE), 1)
    slots = [home[candidates[n // CAND, n % CAND]] for n in range(REQ)]
    common = jnp.zeros((ROWS, LANE), F32)
    for n, slot in enumerate(slots):
        common = jnp.where((row == 1) & (lane == n), (slot // PAN_DEV).astype(F32), common)
        common = jnp.where((row == 2) & (lane == n), (slot % PAN_DEV).astype(F32), common)
    for o in range(N_CENT):
        tile = common
        for n, slot in enumerate(slots):
            here = jnp.where(slot // PAN_DEV == o, slot % PAN_DEV + 1, 0).astype(F32)
            tile = jnp.where((row == 0) & (lane == n // CAND), tile + here, tile)
        for t in range(LOAD_TILES):
            out[o, t] = loads[t * ROWS : (t + 1) * ROWS]
        out[o, LOAD_TILES] = tile.astype(BF16)


def ask(candidates, home, loads):
    return pl.pallas_call(
        ask_kernel,
        in_specs=[hbm_spec()] * 3,
        out_specs=vmem_spec(),
        out_shape=jax.ShapeDtypeStruct((N_CENT, LOAD_TILES + 1, ROWS, LANE), BF16),
        scratch_shapes=[
            pltpu.SMEM(candidates.shape, jnp.int32),
            pltpu.SMEM(home.shape, jnp.int32),
            pltpu.VMEM(loads.shape, BF16),
            pltpu.SemaphoreType.DMA((3,)),
        ],
        compiler_params=params(60),
        cost_estimate=pl.CostEstimate(flops=1 << 16, bytes_accessed=1 << 18, transcendentals=0),
    )(candidates, home, loads)


def pick_kernel(readers, ids, place, table, *refs):
    *outs, held, sems = refs

    def fetch(n, g):
        reader = (place[0] // 2 + readers[n] // 2) % CHIPS * 2 + (place[0] + readers[n]) % 2
        at = n * GROUPS_DEV + g
        return pltpu.make_async_copy(table.at[ids[reader * GROUPS_DEV + g]], held.at[at], sems.at[0, at])

    def put(n, g):
        at = n * GROUPS_DEV + g
        return pltpu.make_async_copy(held.at[at], outs[n].at[g], sems.at[1, at])

    def each(work):
        for n, reader in enumerate(readers):
            at = (place[0] // 2 + reader // 2) % CHIPS * 2 + (place[0] + reader) % 2
            for g in range(GROUPS_DEV):

                @pl.when(ids[at * GROUPS_DEV + g] >= 0)
                def _(n=n, g=g):
                    work(n, g)

    def pass_on(n, g):
        fetch(n, g).wait()
        put(n, g).start()

    each(lambda n, g: fetch(n, g).start())
    each(pass_on)
    each(lambda n, g: put(n, g).wait())


def pick_panels(readers, ids, place, table):
    count = len(readers) * GROUPS_DEV
    return pl.pallas_call(
        functools.partial(pick_kernel, readers),
        out_shape=[jax.ShapeDtypeStruct((GROUPS_DEV, PANEL, WIDTH), BF16)] * len(readers),
        in_specs=[smem_spec(), smem_spec(), hbm_spec()],
        out_specs=[hbm_spec()] * len(readers),
        scratch_shapes=[pltpu.VMEM((count, PANEL, WIDTH), BF16), pltpu.SemaphoreType.DMA((2, count))],
        compiler_params=params(60),
        cost_estimate=pl.CostEstimate(flops=0, bytes_accessed=4 * count * PANEL * WIDTH, transcendentals=0),
    )(ids, place, table)


def score_kernel(owners, *refs):
    panels, (points, surcharge, out, members, centers, shares, sems) = refs[:N_CENT], refs[N_CENT:]
    step = 256
    steps = GROUP // step

    def land(n, o):
        rows = pl.ds(n * PANEL, PANEL)
        return pltpu.make_async_copy(panels[o].at[n // CAND], centers.at[rows], sems.at[0, n])

    def bring(n):
        rows = pl.ds(n * step, step)
        return pltpu.make_async_copy(points.at[rows], members.at[rows], sems.at[1, n])

    for group in range(GROUPS_DEV):
        for j in range(CAND):
            for o in range(N_CENT):

                @pl.when(owners[group * CAND + j] == o)
                def _(n=group * CAND + j, o=o):
                    land(n, o).start()

        for s in range(steps):
            bring(group * steps + s).start()
    lane = lax.broadcasted_iota(jnp.int32, (PANEL, LANE), 1)
    tile = jnp.zeros((PANEL, LANE), F32)
    for group in range(GROUPS_DEV):
        for j in range(CAND):
            land(group * CAND + j, 0).wait()
        for s in range(steps):
            bring(group * steps + s).wait()
        mine = centers[group * CAND * PANEL : (group + 1) * CAND * PANEL, :]
        wide = mine.astype(F32)
        squares = jnp.sum(wide * wide, axis=1, keepdims=True)
        bias = (squares * (1.0 / sharpness_divisor) + evenness_coefficient * surcharge[group]) * LOG2E
        weights = jnp.zeros((CAND * PANEL, LANE), F32)
        for s in range(steps):
            block = members[group * GROUP + s * step : group * GROUP + (s + 1) * step, :]
            inner = lax.dot_general(mine, block, (((1,), (1,)), ((), ())), preferred_element_type=F32)
            logits = inner * (2.0 / sharpness_divisor * LOG2E) - bias
            highest = jnp.max(logits, axis=0, keepdims=True)
            raised = jnp.exp2(logits - highest)
            scale = 1.0 / jnp.sum(raised, axis=0, keepdims=True)
            share = (raised * scale).astype(BF16)
            shares[:, s * step : (s + 1) * step] = share
            rounded = share.astype(F32)
            for part in range(step // LANE):
                weights = weights + rounded[:, part * LANE : (part + 1) * LANE]
        weight = jnp.sum(weights, axis=1, keepdims=True)
        coarse = weight.astype(BF16).astype(F32)
        fine = weight - coarse
        for j in range(CAND):
            rows = slice(j * PANEL, (j + 1) * PANEL)
            tile = jnp.where(lane == group * CAND + j, coarse[rows], tile)
            tile = jnp.where(lane == REQ + group * CAND + j, fine[rows], tile)
        wide_step = 256
        for s in range(WIDTH // wide_step):
            part = lax.dot_general(
                shares[...],
                members[group * GROUP : (group + 1) * GROUP, s * wide_step : (s + 1) * wide_step],
                (((1,), (0,)), ((), ())),
                preferred_element_type=F32,
            ).astype(BF16)
            for t in range(wide_step // LANE):
                half, tile_at = divmod(s * (wide_step // LANE) + t, TILES)
                for j in range(CAND):
                    for block_at in range(PANEL // ROWS):
                        row = j * PANEL + block_at * ROWS
                        out[block_at * 2 + half, (group * CAND + j) * TILES + tile_at] = part[
                            row : row + ROWS, t * LANE : (t + 1) * LANE
                        ]
    tile = tile.astype(BF16)
    for block_at in range(PANEL // ROWS):
        for half in range(2):
            out[block_at * 2 + half, REQ * TILES] = tile[block_at * ROWS : (block_at + 1) * ROWS]


def score(owners, panels, points, surcharge):
    return pl.pallas_call(
        score_kernel,
        in_specs=[smem_spec()] + [hbm_spec()] * (N_CENT + 1) + [vmem_spec()],
        out_specs=vmem_spec(),
        out_shape=jax.ShapeDtypeStruct((N_PTS, SEND_TILES, ROWS, LANE), BF16),
        scratch_shapes=[
            pltpu.VMEM((GROUPS_DEV * GROUP, WIDTH), BF16),
            pltpu.VMEM((GROUPS_DEV * CAND * PANEL, WIDTH), BF16),
            pltpu.VMEM((CAND * PANEL, GROUP), BF16),
            pltpu.SemaphoreType.DMA((2, 8)),
        ],
        compiler_params=params(45),
        cost_estimate=pl.CostEstimate(flops=4 << 30, bytes_accessed=10 * MIB, transcendentals=1 << 20),
    )(owners, *panels, points, surcharge)


def add_pieces(places, source, total):
    def add(s, carry):
        for i in range(REQ):
            at = places[s * REQ + i] * TILES
            total[pl.ds(at, TILES)] += source[s, i * TILES : (i + 1) * TILES].astype(F32)
        return carry

    lax.fori_loop(0, N_PTS, add, 0)


def sum_weights(lanes, source):
    panel = lax.broadcasted_iota(jnp.int32, (CHIPS * PAN_DEV, LANE), 0)
    weights = jnp.zeros((ROWS, CHIPS * PAN_DEV), F32)
    for n in range(N_PTS):
        chosen = jnp.where(panel == lanes[n : n + 1, :], 1.0, 0.0).astype(BF16)
        weights = weights + lax.dot_general(
            source[n, REQ * TILES], chosen, (((1,), (1,)), ((), ())), preferred_element_type=F32
        )
    return weights


def spread_mine_kernel(places, mine, lanes, total, total_weights):
    total[...] = jnp.zeros_like(total)
    add_pieces(places, mine, total)
    total_weights[...] = sum_weights(lanes, mine)


def spread_mate_kernel(rows, places, mate, lanes, total, total_weights, total_out, own_weights, out1, out2, out3):
    del total
    add_pieces(places, mate, total_out)
    weights = total_weights[...] + sum_weights(lanes, mate)
    coarse = weights.astype(BF16)
    fine = (weights - coarse.astype(F32)).astype(BF16)
    own_weights[...] = weights[:, 0:LANE]
    for d, out in ((1, out1), (2, out2), (3, out3)):
        first = DENSE + (d - 1) * rows * TILES
        out[0 : rows * TILES] = total_out[first : first + rows * TILES].astype(BF16)
        out[rows * TILES, :, 0:PAN_DEV] = coarse[:, d * PAN_DEV : (d + 1) * PAN_DEV]
        out[rows * TILES, :, PAN_DEV:LANE] = fine[:, d * PAN_DEV : (d + 1) * PAN_DEV]


def spread_mine(rows, places, lanes, mine):
    return pl.pallas_call(
        spread_mine_kernel,
        in_specs=[smem_spec(), vmem_spec(), vmem_spec()],
        out_specs=[vmem_spec(), vmem_spec()],
        out_shape=[
            jax.ShapeDtypeStruct(((PAN_DEV + 3 * rows + 1) * TILES, ROWS, LANE), F32),
            jax.ShapeDtypeStruct((ROWS, CHIPS * PAN_DEV), F32),
        ],
        compiler_params=params(16),
        cost_estimate=pl.CostEstimate(flops=1 << 21, bytes_accessed=8 * MIB, transcendentals=0),
    )(places, mine, lanes)


def spread_mate(rows, places, lanes, mate, total, total_weights):
    chunk = jax.ShapeDtypeStruct((rows * TILES + 1, ROWS, LANE), BF16)
    return pl.pallas_call(
        functools.partial(spread_mate_kernel, rows),
        in_specs=[smem_spec()] + [vmem_spec()] * 4,
        out_specs=[vmem_spec()] * 5,
        out_shape=[
            jax.ShapeDtypeStruct(total.shape, F32), jax.ShapeDtypeStruct((ROWS, LANE), F32), chunk, chunk, chunk,
        ],
        input_output_aliases={3: 0},
        compiler_params=params(16),
        cost_estimate=pl.CostEstimate(flops=1 << 21, bytes_accessed=8 * MIB, transcendentals=0),
    )(places, mate, lanes, total, total_weights)


def begin_kernel(me, own, table, out, old, sem):
    row = pl.multiple_of(me[0] // 2 * ROWS, ROWS)
    column = pl.multiple_of(me[0] % 2 * HALF, HALF)
    fetch = pltpu.make_async_copy(table.at[:, pl.ds(row, ROWS), pl.ds(column, HALF)], old, sem)
    fetch.start()
    fetch.wait()
    for q in range(PAN_DEV):
        for t in range(TILES):
            previous = old[q, :, t * LANE : (t + 1) * LANE].astype(F32)
            out[q * TILES + t] = own[q * TILES + t] + prior_mass * previous


def begin(me, own, table):
    return pl.pallas_call(
        begin_kernel,
        in_specs=[smem_spec(), vmem_spec(), hbm_spec()],
        out_specs=vmem_spec(),
        out_shape=jax.ShapeDtypeStruct((DENSE, ROWS, LANE), F32),
        scratch_shapes=[pltpu.VMEM((PAN_DEV, ROWS, HALF), BF16), pltpu.SemaphoreType.DMA],
        compiler_params=params(48),
        cost_estimate=pl.CostEstimate(flops=1 << 22, bytes_accessed=5 * MIB, transcendentals=0),
    )(me, own, table)


def finish_kernel(rows, numbers, begun, own_weights, in1, in2, in3, lanes, out, total):
    del begun
    weights = own_weights[:, 0:PAN_DEV]
    panel = lax.broadcasted_iota(jnp.int32, (PAN_DEV, LANE), 0)
    for d, arrived in enumerate((in1, in2, in3)):
        chosen = jnp.where(panel == lanes[d : d + 1, :], 1.0, 0.0).astype(BF16)
        weights = weights + lax.dot_general(
            arrived[rows * TILES], chosen, (((1,), (1,)), ((), ())), preferred_element_type=F32
        )
        first = 3 + d * rows

        def add(n, carry, arrived=arrived, first=first):
            at = numbers[first + n] * TILES
            total[pl.ds(at, TILES)] += arrived[pl.ds(n * TILES, TILES)].astype(F32)
            return carry

        lax.fori_loop(0, numbers[d], add, 0)
    inverse = 1.0 / (weights + prior_mass)
    for q in range(PAN_DEV):
        scale = jnp.broadcast_to(inverse[:, q : q + 1], (ROWS, LANE))
        for t in range(TILES):
            out[q // CAND, (q % CAND) * TILES + t] = (total[q * TILES + t] * scale).astype(BF16)
    coarse = weights.astype(BF16)
    fine = (weights - coarse.astype(F32)).astype(BF16)
    for p in range(N_PTS):
        out[p, CAND * TILES, :, 0:PAN_DEV] = coarse
        out[p, CAND * TILES, :, PAN_DEV:LANE] = fine


def finish(rows, numbers, begun, own_weights, arrived, lanes):
    return pl.pallas_call(
        functools.partial(finish_kernel, rows),
        in_specs=[smem_spec()] + [vmem_spec()] * 6,
        out_specs=[vmem_spec(), vmem_spec()],
        out_shape=[
            jax.ShapeDtypeStruct((N_PTS, CAND * TILES + 1, ROWS, LANE), BF16),
            jax.ShapeDtypeStruct(begun.shape, F32),
        ],
        input_output_aliases={1: 1},
        compiler_params=params(32),
        cost_estimate=pl.CostEstimate(flops=1 << 22, bytes_accessed=6 * MIB, transcendentals=0),
    )(numbers, begun, own_weights, *arrived, lanes)[0]


def place_kernel(me, pieces, out, loads):
    for block_at in range(PANEL // ROWS):
        for half in range(2):
            for q in range(CAND):
                for t in range(TILES):
                    column = half * HALF + t * LANE
                    out[q, block_at * ROWS : (block_at + 1) * ROWS, column : column + LANE] = pieces[
                        block_at * 2 + half, q * TILES + t
                    ]
    lane = lax.broadcasted_iota(jnp.int32, (ROWS, LANE), 1)
    row = lax.broadcasted_iota(jnp.int32, (ROWS, LANE), 0)
    wanted = me[0] * CAND + row
    chosen = jnp.where((row < CAND) & (lane % PAN_DEV == wanted), 1.0, 0.0).astype(BF16)
    for block_at in range(PANEL // ROWS):
        pair = pieces[block_at * 2, CAND * TILES]
        part = lax.dot_general(chosen, pair, (((1,), (1,)), ((), ())), preferred_element_type=F32)
        loads[:, block_at * ROWS : (block_at + 1) * ROWS] = part[0:CAND]


def place(me, pieces):
    return pl.pallas_call(
        place_kernel,
        grid=(1,),
        in_specs=[smem_spec(), whole(pieces.shape)],
        out_specs=[whole((CAND, PANEL, WIDTH)), whole((CAND, PANEL))],
        out_shape=[
            jax.ShapeDtypeStruct((CAND, PANEL, WIDTH), BF16),
            jax.ShapeDtypeStruct((CAND, PANEL), F32),
        ],
        compiler_params=params(32),
        cost_estimate=pl.CostEstimate(flops=1 << 20, bytes_accessed=2 * MIB, transcendentals=0),
    )(me, pieces)


def shift(dy, dk):
    return [(y * 2 + k, ((y + dy) % CHIPS) * 2 + (k + dk) % 2) for y in range(CHIPS) for k in range(2)]


def exchange(x, axis):
    return lax.all_to_all(x, axis, split_axis=0, concat_axis=0, tiled=True)


def local(points, centroids, prev_loads, candidates, panel_home):
    me = lax.axis_index("pts")
    here = lax.axis_index("cent")
    chip, core = here // 2, here % 2
    shelf = centroids.reshape(PAN_DEV, PANEL, WIDTH)

    with jax.named_scope("requests"):
        answered = exchange(ask(candidates, panel_home, prev_loads.reshape(PAN_DEV, PANEL)), "cent")
        asked = answered[:, LOAD_TILES, 0, 0:GROUPS_DEV].astype(jnp.int32).reshape(-1) - 1

    with jax.named_scope("gather_panels"):
        arrived = {}
        for readers in ((1, 2, 6, 4), (3, 7, 5, 0)):
            for n, panels in zip(readers, pick_panels(readers, asked, here.reshape(1), shelf)):
                arrived[n] = lax.ppermute(panels, "cent", shift(n // 2, n % 2)) if n else panels
            asked, arrived[1] = lax.optimization_barrier((asked, arrived[1]))
        answered, arrived[0] = lax.optimization_barrier((answered, arrived[0]))
        arrived = [arrived[n] for n in range(N_CENT)]

    with jax.named_scope("own_requests"):
        slots = jnp.sum(
            jnp.where(candidates.reshape(REQ)[:, None] == jnp.arange(panel_home.shape[0], dtype=jnp.int32), panel_home[None, :], 0),
            axis=1,
        )
        owners = slots // PAN_DEV
        seen = (chip - owners // 2) % CHIPS * 2 + (core - owners) % 2

    with jax.named_scope("all_requests"):
        ring = answered[:, LOAD_TILES, 1:3, 0:REQ].astype(jnp.int32)
        ring = ring[:, 0] * PAN_DEV + ring[:, 1]
        everyone = exchange(jnp.broadcast_to(ring, (N_PTS, N_CENT, REQ)), "pts")

        numbers = jnp.arange(N_CENT * PAN_DEV, dtype=jnp.int32)
        by_chip = jnp.transpose(everyone.reshape(N_PTS, CHIPS, 2 * REQ), (1, 0, 2)).reshape(CHIPS, -1)
        asked_by = jnp.any(by_chip[:, :, None] == numbers, axis=1).reshape(CHIPS, N_CENT, PAN_DEV)
        below = jnp.arange(PAN_DEV)[:, None] < jnp.arange(PAN_DEV)[None, :]
        ranks = lax.dot_general(
            asked_by.astype(BF16), below.astype(BF16), (((2,), (0,)), ((), ())), preferred_element_type=F32
        ).astype(jnp.int32)
        lengths = jnp.sum(asked_by.astype(jnp.int32), axis=2)
        off_chip = jnp.arange(N_CENT)[None, :] // 2 != jnp.arange(CHIPS)[:, None]
        too_long = jnp.any(off_chip & (lengths > LISTED))

        pair = jnp.stack(
            [lax.dynamic_index_in_dim(everyone, at, 1, keepdims=False) for at in (here, chip * 2 + 1 - core)]
        ).reshape(2 * N_PTS, REQ)
        owner = pair // PAN_DEV
        relative = (owner // 2 - chip) % CHIPS
        my_ranks = lax.dynamic_index_in_dim(ranks, chip, 0, keepdims=False).reshape(-1)
        rank = jnp.sum(jnp.where(pair[:, :, None] == numbers, my_ranks, 0), axis=2)
        ours = owner % 2 == core

        def sender(rows, rank):
            at = jnp.where(relative == 0, pair % PAN_DEV, rank)
            known = ours & ((relative == 0) | (rank < rows))
            first = jnp.where(relative == 0, 0, PAN_DEV + (relative - 1) * rows)
            places = jnp.where(known, first + at, PAN_DEV + 3 * rows).reshape(-1)
            lane = jnp.where(known, relative * PAN_DEV + at, CHIPS * PAN_DEV)
            lanes = jnp.pad(
                jnp.concatenate([lane, lane], axis=1), ((0, 0), (0, LANE - 2 * REQ)), constant_values=CHIPS * PAN_DEV
            )
            return places, lanes

        def receiver(rows, count, panels):
            numbers = jnp.concatenate([count, panels[:, :rows].reshape(-1)])
            lane = jnp.where(jnp.arange(PAN_DEV) < jnp.minimum(count, rows)[:, None], panels, PAN_DEV)
            return numbers, jnp.concatenate([lane, lane], axis=1)

        behind = [(chip - d) % CHIPS for d in range(1, CHIPS)]
        pick = lambda x, y: lax.dynamic_index_in_dim(lax.dynamic_index_in_dim(x, y, 0, False), here, 0, False)
        named = jnp.stack([pick(asked_by, y) for y in behind])
        order = jnp.stack([pick(ranks, y) for y in behind])
        spots = jnp.arange(PAN_DEV, dtype=jnp.int32)
        listed = jnp.sum(
            jnp.where(named[:, None, :] & (order[:, None, :] == spots[None, :, None]), spots, 0), axis=2
        )
        count = jnp.minimum(jnp.sum(named.astype(jnp.int32), axis=1), LISTED)
        short = sender(LISTED, rank) + receiver(LISTED, count, listed)
        seen, too_long, short = lax.optimization_barrier((seen, too_long, short))

    with jax.named_scope("loads"):
        load_table = answered[:, :LOAD_TILES].reshape(N_CENT * PAN_DEV, PANEL)
        loads = jnp.take(load_table, slots, axis=0, mode="clip").astype(F32)
        surcharge = jnp.log(loads).reshape(GROUPS_DEV, CAND * PANEL, 1)

    with jax.named_scope("score"):
        pieces = score(seen, arrived, points, surcharge)

    with jax.named_scope("split_pieces"):
        mine = exchange(pieces, "pts")
        mate = lax.ppermute(mine, "cent", shift(0, 1))

    def half(x, n):
        return x.reshape(2, -1)[n] if x.ndim == 1 else x.reshape(2, -1, LANE)[n]

    def start_sums(rows, places, lanes):
        return spread_mine(rows, half(places, 0), half(lanes, 0), mine)

    def sum_over_chips(rows, begun, places, lanes, numbers, back_lanes):
        own, own_weights, *far = spread_mate(rows, half(places, 1), half(lanes, 1), mate, *begun)
        back = [lax.ppermute(far[d - 1], "cent", shift(d, 0)) for d in range(1, CHIPS)]
        return finish(rows, numbers, begin(me.reshape(1), own, shelf), own_weights, back, back_lanes)

    def send_all():
        everything = jnp.broadcast_to(spots, (CHIPS - 1, PAN_DEV))
        count = jnp.full((CHIPS - 1,), PAN_DEV, jnp.int32)
        to = sender(PAN_DEV, pair % PAN_DEV)
        return sum_over_chips(
            PAN_DEV, start_sums(PAN_DEV, *to), *to, *receiver(PAN_DEV, count, everything)
        )

    with jax.named_scope("sum_over_chips"):
        begun = start_sums(LISTED, *short[:2])
        begun, mate = lax.optimization_barrier((begun, mate))
        fresh = lax.cond(too_long, send_all, lambda: sum_over_chips(LISTED, begun, *short))

    with jax.named_scope("place"):
        new_centroids, new_loads = place(me.reshape(1), exchange(fresh, "pts"))
    return new_centroids.reshape(CAND * PANEL, WIDTH), new_loads.reshape(CAND * PANEL)


def solution(mesh):
    placed = (P(("pts", "cent"), None), P("cent", None), P("cent"), P(("pts", "cent"), None), P())
    return jax.shard_map(
        local,
        mesh=mesh,
        in_specs=placed,
        out_specs=(P(("cent", "pts"), None), P(("cent", "pts"))),
        check_vma=False,
    )
```

```python
import functools

import jax
import jax.numpy as jnp
from jax import lax
from jax.experimental import pallas as pl
from jax.experimental.pallas import tpu as pltpu
from jax.sharding import PartitionSpec as P

PANEL = 128
GROUP = 1024
CAND = 4
GROUPS_DEV = 2
REQ = CAND * GROUPS_DEV
PAN_DEV = 64
WIDTH = 1024
N_CENT = 8
CHIPS = 4
N_PTS = 16
ROWS = 16
HALF = 512
LANE = 128
TILES = HALF // LANE
SEND_TILES = CAND * TILES + 1
DENSE = PAN_DEV * TILES
LOAD_TILES = PAN_DEV // ROWS
LISTED = 34

sharpness_divisor = 16.0
evenness_coefficient = 1.0
prior_mass = 1.0

BF16 = jnp.bfloat16
F32 = jnp.float32
MIB = 1 << 20
LOG2E = 1.4426950408889634


def params(mib):
    return pltpu.CompilerParams(vmem_limit_bytes=mib * MIB)


def whole(shape):
    return pl.BlockSpec(shape, lambda *_: (0,) * len(shape))


def smem_spec():
    return pl.BlockSpec(memory_space=pltpu.SMEM)


def vmem_spec():
    return pl.BlockSpec(memory_space=pltpu.VMEM)


def hbm_spec():
    return pl.BlockSpec(memory_space=pltpu.HBM)


def ask_kernel(candidates_in, home_in, loads_in, out, candidates, home, loads, sems):
    copies = [
        pltpu.make_async_copy(source, target, sems.at[n])
        for n, (source, target) in enumerate(((candidates_in, candidates), (home_in, home), (loads_in, loads)))
    ]
    for copy in copies:
        copy.start()
    for copy in copies:
        copy.wait()
    row = lax.broadcasted_iota(jnp.int32, (ROWS, LANE), 0)
    lane = lax.broadcasted_iota(jnp.int32, (ROWS, LANE), 1)
    slots = [home[candidates[n // CAND, n % CAND]] for n in range(REQ)]
    common = jnp.zeros((ROWS, LANE), F32)
    for n, slot in enumerate(slots):
        common = jnp.where((row == 1) & (lane == n), (slot // PAN_DEV).astype(F32), common)
        common = jnp.where((row == 2) & (lane == n), (slot % PAN_DEV).astype(F32), common)
    for o in range(N_CENT):
        tile = common
        for n, slot in enumerate(slots):
            here = jnp.where(slot // PAN_DEV == o, slot % PAN_DEV + 1, 0).astype(F32)
            tile = jnp.where((row == 0) & (lane == n // CAND), tile + here, tile)
        for t in range(LOAD_TILES):
            out[o, t] = loads[t * ROWS : (t + 1) * ROWS]
        out[o, LOAD_TILES] = tile.astype(BF16)


def ask(candidates, home, loads):
    return pl.pallas_call(
        ask_kernel,
        in_specs=[hbm_spec()] * 3,
        out_specs=vmem_spec(),
        out_shape=jax.ShapeDtypeStruct((N_CENT, LOAD_TILES + 1, ROWS, LANE), BF16),
        scratch_shapes=[
            pltpu.SMEM(candidates.shape, jnp.int32),
            pltpu.SMEM(home.shape, jnp.int32),
            pltpu.VMEM(loads.shape, BF16),
            pltpu.SemaphoreType.DMA((3,)),
        ],
        compiler_params=params(60),
        cost_estimate=pl.CostEstimate(flops=1 << 16, bytes_accessed=1 << 18, transcendentals=0),
    )(candidates, home, loads)


def pick_kernel(group, ids, place, table, *refs):
    *outs, held, sems = refs

    def fetch(n, at):
        return pltpu.make_async_copy(table.at[ids[at]], held.at[n], sems.at[0, n])

    def put(n):
        return pltpu.make_async_copy(held.at[n], outs[n], sems.at[1, n])

    def each(work):
        for n in range(N_CENT - 1):
            reader = n + 1
            at = (place[0] // 2 + reader // 2) % CHIPS * 2 + (place[0] + reader) % 2

            @pl.when(ids[at * GROUPS_DEV + group] >= 0)
            def _(n=n, at=at):
                work(n, at * GROUPS_DEV + group)

    def pass_on(n, at):
        fetch(n, at).wait()
        put(n).start()

    each(lambda n, at: fetch(n, at).start())
    each(pass_on)
    each(lambda n, at: put(n).wait())


def pick_panels(group, ids, place, table):
    count = N_CENT - 1
    return pl.pallas_call(
        functools.partial(pick_kernel, group),
        out_shape=[jax.ShapeDtypeStruct((PANEL, WIDTH), BF16)] * count,
        in_specs=[smem_spec(), smem_spec(), hbm_spec()],
        out_specs=[hbm_spec()] * count,
        scratch_shapes=[pltpu.VMEM((count, PANEL, WIDTH), BF16), pltpu.SemaphoreType.DMA((2, count))],
        compiler_params=params(60),
        cost_estimate=pl.CostEstimate(flops=0, bytes_accessed=4 * count * PANEL * WIDTH, transcendentals=0),
    )(ids, place, table)


def score_kernel(group, owners, *refs):
    panels, (table, points, surcharge, out, members, centers, shares, sems) = refs[: N_CENT - 1], refs[N_CENT - 1 :]
    step = 256
    steps = GROUP // step

    def land(j, source):
        rows = pl.ds(j * PANEL, PANEL)
        return pltpu.make_async_copy(source, centers.at[rows], sems.at[0, j])

    def bring(n):
        rows = pl.ds(n * step, step)
        return pltpu.make_async_copy(points.at[pl.ds(group * GROUP + n * step, step)], members.at[rows], sems.at[1, n])

    for j in range(CAND):

        @pl.when(owners[j] == 0)
        def _(j=j):
            land(j, table.at[owners[CAND + j]]).start()

        for o in range(1, N_CENT):

            @pl.when(owners[j] == o)
            def _(j=j, o=o):
                land(j, panels[o - 1]).start()

    for s in range(steps):
        bring(s).start()
    for j in range(CAND):
        land(j, panels[0]).wait()
    for s in range(steps):
        bring(s).wait()
    wide = centers[...].astype(F32)
    squares = jnp.sum(wide * wide, axis=1, keepdims=True)
    bias = (squares * (1.0 / sharpness_divisor) + evenness_coefficient * surcharge[group]) * LOG2E
    weights = jnp.zeros((CAND * PANEL, LANE), F32)
    for s in range(steps):
        block = members[s * step : (s + 1) * step, :]
        inner = lax.dot_general(centers[...], block, (((1,), (1,)), ((), ())), preferred_element_type=F32)
        logits = inner * (2.0 / sharpness_divisor * LOG2E) - bias
        highest = jnp.max(logits, axis=0, keepdims=True)
        raised = jnp.exp2(logits - highest)
        scale = 1.0 / jnp.sum(raised, axis=0, keepdims=True)
        share = (raised * scale).astype(BF16)
        shares[:, s * step : (s + 1) * step] = share
        rounded = share.astype(F32)
        for part in range(step // LANE):
            weights = weights + rounded[:, part * LANE : (part + 1) * LANE]
    weight = jnp.sum(weights, axis=1, keepdims=True)
    coarse = weight.astype(BF16).astype(F32)
    fine = weight - coarse
    lane = lax.broadcasted_iota(jnp.int32, (PANEL, LANE), 1)
    tile = jnp.zeros((PANEL, LANE), F32)
    for j in range(CAND):
        rows = slice(j * PANEL, (j + 1) * PANEL)
        tile = jnp.where(lane == j, coarse[rows], tile)
        tile = jnp.where(lane == CAND + j, fine[rows], tile)
    wide_step = 256
    for s in range(WIDTH // wide_step):
        part = lax.dot_general(
            shares[...], members[:, s * wide_step : (s + 1) * wide_step], (((1,), (0,)), ((), ())),
            preferred_element_type=F32,
        ).astype(BF16)
        for t in range(wide_step // LANE):
            half, tile_at = divmod(s * (wide_step // LANE) + t, TILES)
            for j in range(CAND):
                for block_at in range(PANEL // ROWS):
                    row = j * PANEL + block_at * ROWS
                    out[block_at * 2 + half, j * TILES + tile_at] = part[row : row + ROWS, t * LANE : (t + 1) * LANE]
    tile = tile.astype(BF16)
    for block_at in range(PANEL // ROWS):
        for half in range(2):
            out[block_at * 2 + half, CAND * TILES] = tile[block_at * ROWS : (block_at + 1) * ROWS]


def score(group, owners, panels, table, points, surcharge):
    return pl.pallas_call(
        functools.partial(score_kernel, group),
        in_specs=[smem_spec()] + [hbm_spec()] * (N_CENT + 1) + [vmem_spec()],
        out_specs=vmem_spec(),
        out_shape=jax.ShapeDtypeStruct((N_PTS, SEND_TILES, ROWS, LANE), BF16),
        scratch_shapes=[
            pltpu.VMEM((GROUP, WIDTH), BF16),
            pltpu.VMEM((CAND * PANEL, WIDTH), BF16),
            pltpu.VMEM((CAND * PANEL, GROUP), BF16),
            pltpu.SemaphoreType.DMA((2, 4)),
        ],
        compiler_params=params(50),
        cost_estimate=pl.CostEstimate(flops=2 << 30, bytes_accessed=5 * MIB, transcendentals=1 << 19),
    )(owners, *panels, table, points, surcharge)


def add_pieces(places, source, total):
    def add(s, carry):
        for j in range(CAND):
            at = places[s * CAND + j] * TILES
            total[pl.ds(at, TILES)] += source[s, j * TILES : (j + 1) * TILES].astype(F32)
        return carry

    lax.fori_loop(0, N_PTS, add, 0, unroll=2)


def sum_weights(lanes, source):
    panel = lax.broadcasted_iota(jnp.int32, (CHIPS * PAN_DEV, LANE), 0)
    weights = jnp.zeros((ROWS, CHIPS * PAN_DEV), F32)
    for n in range(N_PTS):
        chosen = jnp.where(panel == lanes[n : n + 1, :], 1.0, 0.0).astype(BF16)
        weights = weights + lax.dot_general(
            source[n, CAND * TILES], chosen, (((1,), (1,)), ((), ())), preferred_element_type=F32
        )
    return weights


def spread_first_kernel(places, source, lanes, total, total_weights):
    total[...] = jnp.zeros_like(total)
    add_pieces(places, source, total)
    total_weights[...] = sum_weights(lanes, source)


def spread_more_kernel(places, source, lanes, total_in, weights_in, total, total_weights):
    del total_in
    add_pieces(places, source, total)
    total_weights[...] = weights_in[...] + sum_weights(lanes, source)


def spread_join_kernel(places, source, lanes, total_in, weights_in, total, total_weights):
    total[...] = total_in[...]
    total_weights[...] = weights_in[...] + sum_weights(lanes, source)
    add_pieces(places, source, total)


def spread_last_kernel(rows, places, source, lanes, total_in, weights_in, total, own_weights, out1, out2, out3):
    del total_in
    add_pieces(places, source, total)
    weights = weights_in[...] + sum_weights(lanes, source)
    coarse = weights.astype(BF16)
    fine = (weights - coarse.astype(F32)).astype(BF16)
    own_weights[...] = weights[:, 0:LANE]
    for d, out in ((1, out1), (2, out2), (3, out3)):
        first = DENSE + (d - 1) * rows * TILES
        out[0 : rows * TILES] = total[first : first + rows * TILES].astype(BF16)
        out[rows * TILES, :, 0:PAN_DEV] = coarse[:, d * PAN_DEV : (d + 1) * PAN_DEV]
        out[rows * TILES, :, PAN_DEV:LANE] = fine[:, d * PAN_DEV : (d + 1) * PAN_DEV]


def spread(rows, places, lanes, source, before=None, last=False, join=False):
    totals = [
        jax.ShapeDtypeStruct(((PAN_DEV + 3 * rows + 1) * TILES, ROWS, LANE), F32),
        jax.ShapeDtypeStruct((ROWS, CHIPS * PAN_DEV), F32),
    ]
    if last:
        chunk = jax.ShapeDtypeStruct((rows * TILES + 1, ROWS, LANE), BF16)
        kernel = functools.partial(spread_last_kernel, rows)
        out = [totals[0], jax.ShapeDtypeStruct((ROWS, LANE), F32), chunk, chunk, chunk]
    else:
        kernel = spread_join_kernel if join else spread_first_kernel if before is None else spread_more_kernel
        out = totals
    before = before or []
    return pl.pallas_call(
        kernel,
        in_specs=[smem_spec()] + [vmem_spec()] * (2 + len(before)),
        out_specs=[vmem_spec()] * len(out),
        out_shape=out,
        input_output_aliases={3: 0} if before and not join else {},
        compiler_params=params(16),
        cost_estimate=pl.CostEstimate(flops=1 << 21, bytes_accessed=4 * MIB, transcendentals=0),
    )(places, source, lanes, *before)


def begin_kernel(me, own, table, out, old, sem):
    row = pl.multiple_of(me[0] // 2 * ROWS, ROWS)
    column = pl.multiple_of(me[0] % 2 * HALF, HALF)
    fetch = pltpu.make_async_copy(table.at[:, pl.ds(row, ROWS), pl.ds(column, HALF)], old, sem)
    fetch.start()
    fetch.wait()
    for q in range(PAN_DEV):
        for t in range(TILES):
            previous = old[q, :, t * LANE : (t + 1) * LANE].astype(F32)
            out[q * TILES + t] = own[q * TILES + t] + prior_mass * previous


def begin(me, own, table):
    return pl.pallas_call(
        begin_kernel,
        in_specs=[smem_spec(), vmem_spec(), hbm_spec()],
        out_specs=vmem_spec(),
        out_shape=jax.ShapeDtypeStruct((DENSE, ROWS, LANE), F32),
        scratch_shapes=[pltpu.VMEM((PAN_DEV, ROWS, HALF), BF16), pltpu.SemaphoreType.DMA],
        compiler_params=params(48),
        cost_estimate=pl.CostEstimate(flops=1 << 22, bytes_accessed=5 * MIB, transcendentals=0),
    )(me, own, table)


def finish_kernel(rows, numbers, begun, own_weights, in1, in2, in3, lanes, out, total):
    del begun
    weights = own_weights[:, 0:PAN_DEV]
    panel = lax.broadcasted_iota(jnp.int32, (PAN_DEV, LANE), 0)
    for d, arrived in enumerate((in1, in2, in3)):
        chosen = jnp.where(panel == lanes[d : d + 1, :], 1.0, 0.0).astype(BF16)
        weights = weights + lax.dot_general(
            arrived[rows * TILES], chosen, (((1,), (1,)), ((), ())), preferred_element_type=F32
        )
        first = 3 + d * rows

        def add(n, carry, arrived=arrived, first=first):
            at = numbers[first + n] * TILES
            total[pl.ds(at, TILES)] += arrived[pl.ds(n * TILES, TILES)].astype(F32)
            return carry

        lax.fori_loop(0, numbers[d], add, 0)
    inverse = 1.0 / (weights + prior_mass)
    for q in range(PAN_DEV):
        scale = jnp.broadcast_to(inverse[:, q : q + 1], (ROWS, LANE))
        for t in range(TILES):
            out[q // CAND, (q % CAND) * TILES + t] = (total[q * TILES + t] * scale).astype(BF16)
    coarse = weights.astype(BF16)
    fine = (weights - coarse.astype(F32)).astype(BF16)
    for p in range(N_PTS):
        out[p, CAND * TILES, :, 0:PAN_DEV] = coarse
        out[p, CAND * TILES, :, PAN_DEV:LANE] = fine


def finish(rows, numbers, begun, own_weights, arrived, lanes):
    return pl.pallas_call(
        functools.partial(finish_kernel, rows),
        in_specs=[smem_spec()] + [vmem_spec()] * 6,
        out_specs=[vmem_spec(), vmem_spec()],
        out_shape=[
            jax.ShapeDtypeStruct((N_PTS, CAND * TILES + 1, ROWS, LANE), BF16),
            jax.ShapeDtypeStruct(begun.shape, F32),
        ],
        input_output_aliases={1: 1},
        compiler_params=params(32),
        cost_estimate=pl.CostEstimate(flops=1 << 22, bytes_accessed=6 * MIB, transcendentals=0),
    )(numbers, begun, own_weights, *arrived, lanes)[0]


def place_kernel(me, pieces, out, loads):
    for block_at in range(PANEL // ROWS):
        for half in range(2):
            for q in range(CAND):
                for t in range(TILES):
                    column = half * HALF + t * LANE
                    out[q, block_at * ROWS : (block_at + 1) * ROWS, column : column + LANE] = pieces[
                        block_at * 2 + half, q * TILES + t
                    ]
    lane = lax.broadcasted_iota(jnp.int32, (ROWS, LANE), 1)
    row = lax.broadcasted_iota(jnp.int32, (ROWS, LANE), 0)
    wanted = me[0] * CAND + row
    chosen = jnp.where((row < CAND) & (lane % PAN_DEV == wanted), 1.0, 0.0).astype(BF16)
    for block_at in range(PANEL // ROWS):
        pair = pieces[block_at * 2, CAND * TILES]
        part = lax.dot_general(chosen, pair, (((1,), (1,)), ((), ())), preferred_element_type=F32)
        loads[:, block_at * ROWS : (block_at + 1) * ROWS] = part[0:CAND]


def place(me, pieces):
    return pl.pallas_call(
        place_kernel,
        grid=(1,),
        in_specs=[smem_spec(), whole(pieces.shape)],
        out_specs=[whole((CAND, PANEL, WIDTH)), whole((CAND, PANEL))],
        out_shape=[
            jax.ShapeDtypeStruct((CAND, PANEL, WIDTH), BF16),
            jax.ShapeDtypeStruct((CAND, PANEL), F32),
        ],
        compiler_params=params(32),
        cost_estimate=pl.CostEstimate(flops=1 << 20, bytes_accessed=2 * MIB, transcendentals=0),
    )(me, pieces)


def shift(dy, dk):
    return [(y * 2 + k, ((y + dy) % CHIPS) * 2 + (k + dk) % 2) for y in range(CHIPS) for k in range(2)]


def exchange(x, axis):
    return lax.all_to_all(x, axis, split_axis=0, concat_axis=0, tiled=True)


def local(points, centroids, prev_loads, candidates, panel_home):
    me = lax.axis_index("pts")
    here = lax.axis_index("cent")
    chip, core = here // 2, here % 2
    shelf = centroids.reshape(PAN_DEV, PANEL, WIDTH)

    with jax.named_scope("requests"):
        answered = exchange(ask(candidates, panel_home, prev_loads.reshape(PAN_DEV, PANEL)), "cent")
        asked = answered[:, LOAD_TILES, 0, 0:GROUPS_DEV].astype(jnp.int32).reshape(-1) - 1

    tie = lax.optimization_barrier
    with jax.named_scope("gather_panels"):
        arrived = []
        for g in range(GROUPS_DEV):
            ready = pick_panels(g, asked, here.reshape(1), shelf)
            arrived.append([lax.ppermute(x, "cent", shift((n + 1) // 2, (n + 1) % 2)) for n, x in enumerate(ready)])
            asked, arrived[g][0] = tie((asked, arrived[g][0]))
        answered, arrived[1][0] = tie((answered, arrived[1][0]))

    with jax.named_scope("own_requests"):
        slots = jnp.sum(
            jnp.where(candidates.reshape(REQ)[:, None] == jnp.arange(panel_home.shape[0], dtype=jnp.int32), panel_home[None, :], 0),
            axis=1,
        )
        owners = slots // PAN_DEV
        seen = (chip - owners // 2) % CHIPS * 2 + (core - owners) % 2
        seen = jnp.stack([seen.reshape(GROUPS_DEV, CAND), (slots % PAN_DEV).reshape(GROUPS_DEV, CAND)], axis=1)
        seen = [seen[g].reshape(-1) for g in range(GROUPS_DEV)]

    with jax.named_scope("all_requests"):
        ring = answered[:, LOAD_TILES, 1:3, 0:REQ].astype(jnp.int32)
        ring = ring[:, 0] * PAN_DEV + ring[:, 1]
        everyone = exchange(jnp.broadcast_to(ring, (N_PTS, N_CENT, REQ)), "pts")

        numbers = jnp.arange(N_CENT * PAN_DEV, dtype=jnp.int32)
        by_chip = jnp.transpose(everyone.reshape(N_PTS, CHIPS, 2 * REQ), (1, 0, 2)).reshape(CHIPS, -1)
        asked_by = jnp.any(by_chip[:, :, None] == numbers, axis=1).reshape(CHIPS, N_CENT, PAN_DEV)
        below = jnp.arange(PAN_DEV)[:, None] < jnp.arange(PAN_DEV)[None, :]
        ranks = lax.dot_general(
            asked_by.astype(BF16), below.astype(BF16), (((2,), (0,)), ((), ())), preferred_element_type=F32
        ).astype(jnp.int32)
        lengths = jnp.sum(asked_by.astype(jnp.int32), axis=2)
        off_chip = jnp.arange(N_CENT)[None, :] // 2 != jnp.arange(CHIPS)[:, None]
        too_long = jnp.any(off_chip & (lengths > LISTED))

        pair = jnp.stack(
            [lax.dynamic_index_in_dim(everyone, at, 1, keepdims=False) for at in (here, chip * 2 + 1 - core)]
        )
        pair = jnp.transpose(pair.reshape(2, N_PTS, GROUPS_DEV, CAND), (2, 0, 1, 3))
        owner = pair // PAN_DEV
        relative = (owner // 2 - chip) % CHIPS
        my_ranks = lax.dynamic_index_in_dim(ranks, chip, 0, keepdims=False).reshape(-1)
        rank = jnp.sum(jnp.where(pair[..., None] == numbers, my_ranks, 0), axis=4)
        ours = owner % 2 == core

        def sender(rows, rank):
            at = jnp.where(relative == 0, pair % PAN_DEV, rank)
            known = ours & ((relative == 0) | (rank < rows))
            first = jnp.where(relative == 0, 0, PAN_DEV + (relative - 1) * rows)
            places = jnp.where(known, first + at, PAN_DEV + 3 * rows)
            lane = jnp.where(known, relative * PAN_DEV + at, CHIPS * PAN_DEV)
            lanes = jnp.pad(
                jnp.concatenate([lane, lane], axis=3), ((0, 0), (0, 0), (0, 0), (0, LANE - 2 * CAND)),
                constant_values=CHIPS * PAN_DEV,
            )
            return [
                (places[g, n].reshape(-1), lanes[g, n]) for g in range(GROUPS_DEV) for n in range(2)
            ]

        def receiver(rows, count, panels):
            numbers = jnp.concatenate([count, panels[:, :rows].reshape(-1)])
            lane = jnp.where(jnp.arange(PAN_DEV) < jnp.minimum(count, rows)[:, None], panels, PAN_DEV)
            return numbers, jnp.concatenate([lane, lane], axis=1)

        behind = [(chip - d) % CHIPS for d in range(1, CHIPS)]
        pick = lambda x, y: lax.dynamic_index_in_dim(lax.dynamic_index_in_dim(x, y, 0, False), here, 0, False)
        named = jnp.stack([pick(asked_by, y) for y in behind])
        order = jnp.stack([pick(ranks, y) for y in behind])
        spots = jnp.arange(PAN_DEV, dtype=jnp.int32)
        listed = jnp.sum(
            jnp.where(named[:, None, :] & (order[:, None, :] == spots[None, :, None]), spots, 0), axis=2
        )
        count = jnp.minimum(jnp.sum(named.astype(jnp.int32), axis=1), LISTED)
        short = sender(LISTED, rank)
        short_back = receiver(LISTED, count, listed)
        seen[1], too_long, short, short_back = tie((seen[1], too_long, short, short_back))

    with jax.named_scope("loads"):
        load_table = answered[:, :LOAD_TILES].reshape(N_CENT * PAN_DEV, PANEL)
        loads = jnp.take(load_table, slots, axis=0, mode="clip").astype(F32)
        surcharge = jnp.log(loads).reshape(GROUPS_DEV, CAND * PANEL, 1)

    sources = []
    for g in range(GROUPS_DEV):
        with jax.named_scope("score"):
            pieces = score(g, seen[g], arrived[g], shelf, points, surcharge)
        with jax.named_scope("split_pieces"):
            mine = exchange(pieces, "pts")
            if g == 1:
                with jax.named_scope("sum_over_chips"):
                    begun = spread(LISTED, *short[0], sources[0])
                    begun = spread(LISTED, *short[1], sources[1], before=begun)
                mine, begun = tie((mine, begun))
            sources += [mine, lax.ppermute(mine, "cent", shift(0, 1))]
        if g == 0:
            arrived[1][0], sources[0] = tie((arrived[1][0], sources[0]))

    def sum_over_chips(rows, to, begun, numbers, back_lanes):
        own, own_weights, *far = spread(rows, *to[3], sources[3], before=begun, last=True)
        back = [lax.ppermute(far[d - 1], "cent", shift(d, 0)) for d in range(1, CHIPS)]
        return finish(rows, numbers, begin(me.reshape(1), own, shelf), own_weights, back, back_lanes)

    def send_all():
        everything = jnp.broadcast_to(spots, (CHIPS - 1, PAN_DEV))
        count = jnp.full((CHIPS - 1,), PAN_DEV, jnp.int32)
        to = sender(PAN_DEV, pair % PAN_DEV)
        begun = None
        for n in range(3):
            begun = spread(PAN_DEV, *to[n], sources[n], before=begun)
        return sum_over_chips(PAN_DEV, to, begun, *receiver(PAN_DEV, count, everything))

    with jax.named_scope("sum_over_chips"):
        begun = spread(LISTED, *short[2], sources[2], before=begun, join=True)
        begun, sources[3] = tie((begun, sources[3]))
        fresh = lax.cond(too_long, send_all, lambda: sum_over_chips(LISTED, short, begun, *short_back))

    with jax.named_scope("place"):
        new_centroids, new_loads = place(me.reshape(1), exchange(fresh, "pts"))
    return new_centroids.reshape(CAND * PANEL, WIDTH), new_loads.reshape(CAND * PANEL)


def solution(mesh):
    placed = (P(("pts", "cent"), None), P("cent", None), P("cent"), P(("pts", "cent"), None), P())
    return jax.shard_map(
        local,
        mesh=mesh,
        in_specs=placed,
        out_specs=(P(("cent", "pts"), None), P(("cent", "pts"))),
        check_vma=False,
    )
```

```python
import functools

import jax
import jax.numpy as jnp
from jax import lax
from jax.experimental import pallas as pl
from jax.experimental.pallas import tpu as pltpu
from jax.sharding import PartitionSpec as P

PANEL = 128
GROUP = 1024
CAND = 4
GROUPS_DEV = 2
REQ = CAND * GROUPS_DEV
PAN_DEV = 64
WIDTH = 1024
N_CENT = 8
CHIPS = 4
N_PTS = 16
ROWS = 16
HALF = 512
LANE = 128
TILES = HALF // LANE
SEND_TILES = CAND * TILES + 1
DENSE = PAN_DEV * TILES
LOAD_TILES = PAN_DEV // ROWS
LISTED = 34

sharpness_divisor = 16.0
evenness_coefficient = 1.0
prior_mass = 1.0

BF16 = jnp.bfloat16
F32 = jnp.float32
MIB = 1 << 20
LOG2E = 1.4426950408889634


def params(mib):
    return pltpu.CompilerParams(vmem_limit_bytes=mib * MIB)


def whole(shape):
    return pl.BlockSpec(shape, lambda *_: (0,) * len(shape))


def smem_spec():
    return pl.BlockSpec(memory_space=pltpu.SMEM)


def vmem_spec():
    return pl.BlockSpec(memory_space=pltpu.VMEM)


def hbm_spec():
    return pl.BlockSpec(memory_space=pltpu.HBM)


def ask_kernel(candidates_in, home_in, loads_in, out, candidates, home, loads, sems):
    copies = [
        pltpu.make_async_copy(source, target, sems.at[n])
        for n, (source, target) in enumerate(((candidates_in, candidates), (home_in, home), (loads_in, loads)))
    ]
    for copy in copies:
        copy.start()
    for copy in copies:
        copy.wait()
    row = lax.broadcasted_iota(jnp.int32, (ROWS, LANE), 0)
    lane = lax.broadcasted_iota(jnp.int32, (ROWS, LANE), 1)
    slots = [home[candidates[n // CAND, n % CAND]] for n in range(REQ)]
    common = jnp.zeros((ROWS, LANE), F32)
    for n, slot in enumerate(slots):
        common = jnp.where((row == 1) & (lane == n), (slot // PAN_DEV).astype(F32), common)
        common = jnp.where((row == 2) & (lane == n), (slot % PAN_DEV).astype(F32), common)
    for o in range(N_CENT):
        tile = common
        for n, slot in enumerate(slots):
            here = jnp.where(slot // PAN_DEV == o, slot % PAN_DEV + 1, 0).astype(F32)
            tile = jnp.where((row == 0) & (lane == n // CAND), tile + here, tile)
        for t in range(LOAD_TILES):
            out[o, t] = loads[t * ROWS : (t + 1) * ROWS]
        out[o, LOAD_TILES] = tile.astype(BF16)


def ask(candidates, home, loads):
    return pl.pallas_call(
        ask_kernel,
        in_specs=[hbm_spec()] * 3,
        out_specs=vmem_spec(),
        out_shape=jax.ShapeDtypeStruct((N_CENT, LOAD_TILES + 1, ROWS, LANE), BF16),
        scratch_shapes=[
            pltpu.SMEM(candidates.shape, jnp.int32),
            pltpu.SMEM(home.shape, jnp.int32),
            pltpu.VMEM(loads.shape, BF16),
            pltpu.SemaphoreType.DMA((3,)),
        ],
        compiler_params=params(60),
        cost_estimate=pl.CostEstimate(flops=1 << 16, bytes_accessed=1 << 18, transcendentals=0),
    )(candidates, home, loads)


def pick_kernel(group, ids, place, table, *refs):
    *outs, held, sems = refs

    def fetch(n, at):
        return pltpu.make_async_copy(table.at[ids[at]], held.at[n], sems.at[0, n])

    def put(n):
        return pltpu.make_async_copy(held.at[n], outs[n], sems.at[1, n])

    def each(work):
        for n in range(N_CENT - 1):
            reader = n + 1
            at = (place[0] // 2 + reader // 2) % CHIPS * 2 + (place[0] + reader) % 2

            @pl.when(ids[at * GROUPS_DEV + group] >= 0)
            def _(n=n, at=at):
                work(n, at * GROUPS_DEV + group)

    def pass_on(n, at):
        fetch(n, at).wait()
        put(n).start()

    each(lambda n, at: fetch(n, at).start())
    each(pass_on)
    each(lambda n, at: put(n).wait())


def pick_panels(group, ids, place, table):
    count = N_CENT - 1
    return pl.pallas_call(
        functools.partial(pick_kernel, group),
        out_shape=[jax.ShapeDtypeStruct((PANEL, WIDTH), BF16)] * count,
        in_specs=[smem_spec(), smem_spec(), hbm_spec()],
        out_specs=[hbm_spec()] * count,
        scratch_shapes=[pltpu.VMEM((count, PANEL, WIDTH), BF16), pltpu.SemaphoreType.DMA((2, count))],
        compiler_params=params(60),
        cost_estimate=pl.CostEstimate(flops=0, bytes_accessed=4 * count * PANEL * WIDTH, transcendentals=0),
    )(ids, place, table)


def score_kernel(group, owners, *refs):
    panels, (table, points, surcharge, out, members, centers, shares, sems) = refs[: N_CENT - 1], refs[N_CENT - 1 :]
    step = 256
    steps = GROUP // step

    def land(j, source):
        rows = pl.ds(j * PANEL, PANEL)
        return pltpu.make_async_copy(source, centers.at[rows], sems.at[0, j])

    def bring(n):
        rows = pl.ds(n * step, step)
        return pltpu.make_async_copy(points.at[pl.ds(group * GROUP + n * step, step)], members.at[rows], sems.at[1, n])

    for j in range(CAND):

        @pl.when(owners[j] == 0)
        def _(j=j):
            land(j, table.at[owners[CAND + j]]).start()

        for o in range(1, N_CENT):

            @pl.when(owners[j] == o)
            def _(j=j, o=o):
                land(j, panels[o - 1]).start()

    for s in range(steps):
        bring(s).start()
    for j in range(CAND):
        land(j, panels[0]).wait()
    for s in range(steps):
        bring(s).wait()
    wide = centers[...].astype(F32)
    squares = jnp.sum(wide * wide, axis=1, keepdims=True)
    bias = (squares * (1.0 / sharpness_divisor) + evenness_coefficient * surcharge[group]) * LOG2E
    weights = jnp.zeros((CAND * PANEL, LANE), F32)
    for s in range(steps):
        block = members[s * step : (s + 1) * step, :]
        inner = lax.dot_general(centers[...], block, (((1,), (1,)), ((), ())), preferred_element_type=F32)
        logits = inner * (2.0 / sharpness_divisor * LOG2E) - bias
        highest = jnp.max(logits, axis=0, keepdims=True)
        raised = jnp.exp2(logits - highest)
        scale = 1.0 / jnp.sum(raised, axis=0, keepdims=True)
        share = (raised * scale).astype(BF16)
        shares[:, s * step : (s + 1) * step] = share
        rounded = share.astype(F32)
        for part in range(step // LANE):
            weights = weights + rounded[:, part * LANE : (part + 1) * LANE]
    weight = jnp.sum(weights, axis=1, keepdims=True)
    coarse = weight.astype(BF16).astype(F32)
    fine = weight - coarse
    lane = lax.broadcasted_iota(jnp.int32, (PANEL, LANE), 1)
    tile = jnp.zeros((PANEL, LANE), F32)
    for j in range(CAND):
        rows = slice(j * PANEL, (j + 1) * PANEL)
        tile = jnp.where(lane == j, coarse[rows], tile)
        tile = jnp.where(lane == CAND + j, fine[rows], tile)
    wide_step = 256
    for s in range(WIDTH // wide_step):
        part = lax.dot_general(
            shares[...], members[:, s * wide_step : (s + 1) * wide_step], (((1,), (0,)), ((), ())),
            preferred_element_type=F32,
        ).astype(BF16)
        for t in range(wide_step // LANE):
            half, tile_at = divmod(s * (wide_step // LANE) + t, TILES)
            for j in range(CAND):
                for block_at in range(PANEL // ROWS):
                    row = j * PANEL + block_at * ROWS
                    out[block_at * 2 + half, j * TILES + tile_at] = part[row : row + ROWS, t * LANE : (t + 1) * LANE]
    tile = tile.astype(BF16)
    for block_at in range(PANEL // ROWS):
        for half in range(2):
            out[block_at * 2 + half, CAND * TILES] = tile[block_at * ROWS : (block_at + 1) * ROWS]


def score(group, owners, panels, table, points, surcharge):
    return pl.pallas_call(
        functools.partial(score_kernel, group),
        in_specs=[smem_spec()] + [hbm_spec()] * (N_CENT + 1) + [vmem_spec()],
        out_specs=vmem_spec(),
        out_shape=jax.ShapeDtypeStruct((N_PTS, SEND_TILES, ROWS, LANE), BF16),
        scratch_shapes=[
            pltpu.VMEM((GROUP, WIDTH), BF16),
            pltpu.VMEM((CAND * PANEL, WIDTH), BF16),
            pltpu.VMEM((CAND * PANEL, GROUP), BF16),
            pltpu.SemaphoreType.DMA((2, 4)),
        ],
        compiler_params=params(50),
        cost_estimate=pl.CostEstimate(flops=2 << 30, bytes_accessed=5 * MIB, transcendentals=1 << 19),
    )(owners, *panels, table, points, surcharge)


def add_pieces(places, source, total):
    def add(s, carry):
        for j in range(CAND):
            at = places[s * CAND + j] * TILES
            total[pl.ds(at, TILES)] += source[s, j * TILES : (j + 1) * TILES].astype(F32)
        return carry

    lax.fori_loop(0, N_PTS, add, 0, unroll=2)


def sum_weights(lanes, source):
    panel = lax.broadcasted_iota(jnp.int32, (CHIPS * PAN_DEV, LANE), 0)
    weights = jnp.zeros((ROWS, CHIPS * PAN_DEV), F32)
    for n in range(N_PTS):
        chosen = jnp.where(panel == lanes[n : n + 1, :], 1.0, 0.0).astype(BF16)
        weights = weights + lax.dot_general(
            source[n, CAND * TILES], chosen, (((1,), (1,)), ((), ())), preferred_element_type=F32
        )
    return weights


def spread_first_kernel(places, source, lanes, total, total_weights):
    total[...] = jnp.zeros_like(total)
    add_pieces(places, source, total)
    total_weights[...] = sum_weights(lanes, source)


def spread_more_kernel(places, source, lanes, total_in, weights_in, total, total_weights):
    del total_in
    add_pieces(places, source, total)
    total_weights[...] = weights_in[...] + sum_weights(lanes, source)


def spread_join_kernel(places, source, lanes, total_in, weights_in, total, total_weights):
    total[...] = total_in[...]
    total_weights[...] = weights_in[...] + sum_weights(lanes, source)
    add_pieces(places, source, total)


def spread_last_kernel(rows, places, source, lanes, total_in, weights_in, total, own_weights, out1, out2, out3):
    del total_in
    add_pieces(places, source, total)
    weights = weights_in[...] + sum_weights(lanes, source)
    coarse = weights.astype(BF16)
    fine = (weights - coarse.astype(F32)).astype(BF16)
    own_weights[...] = weights[:, 0:LANE]
    for d, out in ((1, out1), (2, out2), (3, out3)):
        first = DENSE + (d - 1) * rows * TILES
        out[0 : rows * TILES] = total[first : first + rows * TILES].astype(BF16)
        out[rows * TILES, :, 0:PAN_DEV] = coarse[:, d * PAN_DEV : (d + 1) * PAN_DEV]
        out[rows * TILES, :, PAN_DEV:LANE] = fine[:, d * PAN_DEV : (d + 1) * PAN_DEV]


def spread(rows, places, lanes, source, before=None, last=False, join=False):
    totals = [
        jax.ShapeDtypeStruct(((PAN_DEV + 3 * rows + 1) * TILES, ROWS, LANE), F32),
        jax.ShapeDtypeStruct((ROWS, CHIPS * PAN_DEV), F32),
    ]
    if last:
        chunk = jax.ShapeDtypeStruct((rows * TILES + 1, ROWS, LANE), BF16)
        kernel = functools.partial(spread_last_kernel, rows)
        out = [totals[0], jax.ShapeDtypeStruct((ROWS, LANE), F32), chunk, chunk, chunk]
    else:
        kernel = spread_join_kernel if join else spread_first_kernel if before is None else spread_more_kernel
        out = totals
    before = before or []
    return pl.pallas_call(
        kernel,
        in_specs=[smem_spec()] + [vmem_spec()] * (2 + len(before)),
        out_specs=[vmem_spec()] * len(out),
        out_shape=out,
        input_output_aliases={3: 0} if before and not join else {},
        compiler_params=params(16),
        cost_estimate=pl.CostEstimate(flops=1 << 21, bytes_accessed=4 * MIB, transcendentals=0),
    )(places, source, lanes, *before)


def begin_kernel(me, own, table, out, old, sem):
    row = pl.multiple_of(me[0] // 2 * ROWS, ROWS)
    column = pl.multiple_of(me[0] % 2 * HALF, HALF)
    fetch = pltpu.make_async_copy(table.at[:, pl.ds(row, ROWS), pl.ds(column, HALF)], old, sem)
    fetch.start()
    fetch.wait()
    for q in range(PAN_DEV):
        for t in range(TILES):
            previous = old[q, :, t * LANE : (t + 1) * LANE].astype(F32)
            out[q * TILES + t] = own[q * TILES + t] + prior_mass * previous


def begin(me, own, table):
    return pl.pallas_call(
        begin_kernel,
        in_specs=[smem_spec(), vmem_spec(), hbm_spec()],
        out_specs=vmem_spec(),
        out_shape=jax.ShapeDtypeStruct((DENSE, ROWS, LANE), F32),
        scratch_shapes=[pltpu.VMEM((PAN_DEV, ROWS, HALF), BF16), pltpu.SemaphoreType.DMA],
        compiler_params=params(48),
        cost_estimate=pl.CostEstimate(flops=1 << 22, bytes_accessed=5 * MIB, transcendentals=0),
    )(me, own, table)


def finish_kernel(rows, numbers, begun, own_weights, in1, in2, in3, lanes, out, total):
    del begun
    weights = own_weights[:, 0:PAN_DEV]
    panel = lax.broadcasted_iota(jnp.int32, (PAN_DEV, LANE), 0)
    for d, arrived in enumerate((in1, in2, in3)):
        chosen = jnp.where(panel == lanes[d : d + 1, :], 1.0, 0.0).astype(BF16)
        weights = weights + lax.dot_general(
            arrived[rows * TILES], chosen, (((1,), (1,)), ((), ())), preferred_element_type=F32
        )
        first = 3 + d * rows

        def add(n, carry, arrived=arrived, first=first):
            at = numbers[first + n] * TILES
            total[pl.ds(at, TILES)] += arrived[pl.ds(n * TILES, TILES)].astype(F32)
            return carry

        lax.fori_loop(0, numbers[d], add, 0)
    inverse = 1.0 / (weights + prior_mass)
    for q in range(PAN_DEV):
        scale = jnp.broadcast_to(inverse[:, q : q + 1], (ROWS, LANE))
        for t in range(TILES):
            out[q // CAND, (q % CAND) * TILES + t] = (total[q * TILES + t] * scale).astype(BF16)
    coarse = weights.astype(BF16)
    fine = (weights - coarse.astype(F32)).astype(BF16)
    for p in range(N_PTS):
        out[p, CAND * TILES, :, 0:PAN_DEV] = coarse
        out[p, CAND * TILES, :, PAN_DEV:LANE] = fine


def finish(rows, numbers, begun, own_weights, arrived, lanes):
    return pl.pallas_call(
        functools.partial(finish_kernel, rows),
        in_specs=[smem_spec()] + [vmem_spec()] * 6,
        out_specs=[vmem_spec(), vmem_spec()],
        out_shape=[
            jax.ShapeDtypeStruct((N_PTS, CAND * TILES + 1, ROWS, LANE), BF16),
            jax.ShapeDtypeStruct(begun.shape, F32),
        ],
        input_output_aliases={1: 1},
        compiler_params=params(32),
        cost_estimate=pl.CostEstimate(flops=1 << 22, bytes_accessed=6 * MIB, transcendentals=0),
    )(numbers, begun, own_weights, *arrived, lanes)[0]


def place_kernel(me, pieces, out, loads):
    for block_at in range(PANEL // ROWS):
        for half in range(2):
            for q in range(CAND):
                for t in range(TILES):
                    column = half * HALF + t * LANE
                    out[q, block_at * ROWS : (block_at + 1) * ROWS, column : column + LANE] = pieces[
                        block_at * 2 + half, q * TILES + t
                    ]
    lane = lax.broadcasted_iota(jnp.int32, (ROWS, LANE), 1)
    row = lax.broadcasted_iota(jnp.int32, (ROWS, LANE), 0)
    wanted = me[0] * CAND + row
    chosen = jnp.where((row < CAND) & (lane % PAN_DEV == wanted), 1.0, 0.0).astype(BF16)
    for block_at in range(PANEL // ROWS):
        pair = pieces[block_at * 2, CAND * TILES]
        part = lax.dot_general(chosen, pair, (((1,), (1,)), ((), ())), preferred_element_type=F32)
        loads[:, block_at * ROWS : (block_at + 1) * ROWS] = part[0:CAND]


def place(me, pieces):
    return pl.pallas_call(
        place_kernel,
        grid=(1,),
        in_specs=[smem_spec(), whole(pieces.shape)],
        out_specs=[whole((CAND, PANEL, WIDTH)), whole((CAND, PANEL))],
        out_shape=[
            jax.ShapeDtypeStruct((CAND, PANEL, WIDTH), BF16),
            jax.ShapeDtypeStruct((CAND, PANEL), F32),
        ],
        compiler_params=params(32),
        cost_estimate=pl.CostEstimate(flops=1 << 20, bytes_accessed=2 * MIB, transcendentals=0),
    )(me, pieces)


def shift(dy, dk):
    return [(y * 2 + k, ((y + dy) % CHIPS) * 2 + (k + dk) % 2) for y in range(CHIPS) for k in range(2)]


def exchange(x, axis):
    return lax.all_to_all(x, axis, split_axis=0, concat_axis=0, tiled=True)


def local(points, centroids, prev_loads, candidates, panel_home):
    me = lax.axis_index("pts")
    here = lax.axis_index("cent")
    chip, core = here // 2, here % 2
    shelf = centroids.reshape(PAN_DEV, PANEL, WIDTH)

    with jax.named_scope("requests"):
        answered = exchange(ask(candidates, panel_home, prev_loads.reshape(PAN_DEV, PANEL)), "cent")
        asked = answered[:, LOAD_TILES, 0, 0:GROUPS_DEV].astype(jnp.int32).reshape(-1) - 1

    tie = lax.optimization_barrier
    with jax.named_scope("gather_panels"):
        arrived = []
        for g in range(GROUPS_DEV):
            ready = pick_panels(g, asked, here.reshape(1), shelf)
            arrived.append([lax.ppermute(x, "cent", shift((n + 1) // 2, (n + 1) % 2)) for n, x in enumerate(ready)])
            if g == 0:
                answered, arrived[g][0] = tie((answered, arrived[g][0]))
                asked, arrived[g][1] = tie((asked, arrived[g][1]))

    with jax.named_scope("own_requests"):
        slots = jnp.sum(
            jnp.where(candidates.reshape(REQ)[:, None] == jnp.arange(panel_home.shape[0], dtype=jnp.int32), panel_home[None, :], 0),
            axis=1,
        )
        owners = slots // PAN_DEV
        seen = (chip - owners // 2) % CHIPS * 2 + (core - owners) % 2
        seen = jnp.stack([seen.reshape(GROUPS_DEV, CAND), (slots % PAN_DEV).reshape(GROUPS_DEV, CAND)], axis=1)
        seen = [seen[g].reshape(-1) for g in range(GROUPS_DEV)]

    with jax.named_scope("all_requests"):
        ring = answered[:, LOAD_TILES, 1:3, 0:REQ].astype(jnp.int32)
        ring = ring[:, 0] * PAN_DEV + ring[:, 1]
        everyone = exchange(jnp.broadcast_to(ring, (N_PTS, N_CENT, REQ)), "pts")

        numbers = jnp.arange(N_CENT * PAN_DEV, dtype=jnp.int32)
        by_chip = jnp.transpose(everyone.reshape(N_PTS, CHIPS, 2 * REQ), (1, 0, 2)).reshape(CHIPS, -1)
        asked_by = jnp.any(by_chip[:, :, None] == numbers, axis=1).reshape(CHIPS, N_CENT, PAN_DEV)
        below = jnp.arange(PAN_DEV)[:, None] < jnp.arange(PAN_DEV)[None, :]
        ranks = lax.dot_general(
            asked_by.astype(BF16), below.astype(BF16), (((2,), (0,)), ((), ())), preferred_element_type=F32
        ).astype(jnp.int32)
        lengths = jnp.sum(asked_by.astype(jnp.int32), axis=2)
        off_chip = jnp.arange(N_CENT)[None, :] // 2 != jnp.arange(CHIPS)[:, None]
        too_long = jnp.any(off_chip & (lengths > LISTED))

        pair = jnp.stack(
            [lax.dynamic_index_in_dim(everyone, at, 1, keepdims=False) for at in (here, chip * 2 + 1 - core)]
        )
        pair = jnp.transpose(pair.reshape(2, N_PTS, GROUPS_DEV, CAND), (2, 0, 1, 3))
        owner = pair // PAN_DEV
        relative = (owner // 2 - chip) % CHIPS
        my_ranks = lax.dynamic_index_in_dim(ranks, chip, 0, keepdims=False).reshape(-1)
        rank = jnp.sum(jnp.where(pair[..., None] == numbers, my_ranks, 0), axis=4)
        ours = owner % 2 == core

        def sender(rows, rank):
            at = jnp.where(relative == 0, pair % PAN_DEV, rank)
            known = ours & ((relative == 0) | (rank < rows))
            first = jnp.where(relative == 0, 0, PAN_DEV + (relative - 1) * rows)
            places = jnp.where(known, first + at, PAN_DEV + 3 * rows)
            lane = jnp.where(known, relative * PAN_DEV + at, CHIPS * PAN_DEV)
            lanes = jnp.pad(
                jnp.concatenate([lane, lane], axis=3), ((0, 0), (0, 0), (0, 0), (0, LANE - 2 * CAND)),
                constant_values=CHIPS * PAN_DEV,
            )
            return [
                (places[g, n].reshape(-1), lanes[g, n]) for g in range(GROUPS_DEV) for n in range(2)
            ]

        def receiver(rows, count, panels):
            numbers = jnp.concatenate([count, panels[:, :rows].reshape(-1)])
            lane = jnp.where(jnp.arange(PAN_DEV) < jnp.minimum(count, rows)[:, None], panels, PAN_DEV)
            return numbers, jnp.concatenate([lane, lane], axis=1)

        behind = [(chip - d) % CHIPS for d in range(1, CHIPS)]
        pick = lambda x, y: lax.dynamic_index_in_dim(lax.dynamic_index_in_dim(x, y, 0, False), here, 0, False)
        named = jnp.stack([pick(asked_by, y) for y in behind])
        order = jnp.stack([pick(ranks, y) for y in behind])
        spots = jnp.arange(PAN_DEV, dtype=jnp.int32)
        listed = jnp.sum(
            jnp.where(named[:, None, :] & (order[:, None, :] == spots[None, :, None]), spots, 0), axis=2
        )
        count = jnp.minimum(jnp.sum(named.astype(jnp.int32), axis=1), LISTED)
        short = sender(LISTED, rank)
        short_back = receiver(LISTED, count, listed)
        seen[1], too_long, short, short_back = tie((seen[1], too_long, short, short_back))

    with jax.named_scope("loads"):
        load_table = answered[:, :LOAD_TILES].reshape(N_CENT * PAN_DEV, PANEL)
        loads = jnp.take(load_table, slots, axis=0, mode="clip").astype(F32)
        surcharge = jnp.log(loads).reshape(GROUPS_DEV, CAND * PANEL, 1)

    sources = []
    for g in range(GROUPS_DEV):
        with jax.named_scope("score"):
            pieces = score(g, seen[g], arrived[g], shelf, points, surcharge)
        with jax.named_scope("split_pieces"):
            mine = exchange(pieces, "pts")
            if g == 1:
                with jax.named_scope("sum_over_chips"):
                    begun = spread(LISTED, *short[0], sources[0])
                    begun = spread(LISTED, *short[1], sources[1], before=begun)
                mine, begun = tie((mine, begun))
            sources += [mine, lax.ppermute(mine, "cent", shift(0, 1))]

    def sum_over_chips(rows, to, begun, numbers, back_lanes):
        own, own_weights, *far = spread(rows, *to[3], sources[3], before=begun, last=True)
        back = [lax.ppermute(far[d - 1], "cent", shift(d, 0)) for d in range(1, CHIPS)]
        return finish(rows, numbers, begin(me.reshape(1), own, shelf), own_weights, back, back_lanes)

    def send_all():
        everything = jnp.broadcast_to(spots, (CHIPS - 1, PAN_DEV))
        count = jnp.full((CHIPS - 1,), PAN_DEV, jnp.int32)
        to = sender(PAN_DEV, pair % PAN_DEV)
        begun = None
        for n in range(3):
            begun = spread(PAN_DEV, *to[n], sources[n], before=begun)
        return sum_over_chips(PAN_DEV, to, begun, *receiver(PAN_DEV, count, everything))

    with jax.named_scope("sum_over_chips"):
        begun = spread(LISTED, *short[2], sources[2], before=begun, join=True)
        begun, sources[3] = tie((begun, sources[3]))
        fresh = lax.cond(too_long, send_all, lambda: sum_over_chips(LISTED, short, begun, *short_back))

    with jax.named_scope("place"):
        new_centroids, new_loads = place(me.reshape(1), exchange(fresh, "pts"))
    return new_centroids.reshape(CAND * PANEL, WIDTH), new_loads.reshape(CAND * PANEL)


def solution(mesh):
    placed = (P(("pts", "cent"), None), P("cent", None), P("cent"), P(("pts", "cent"), None), P())
    return jax.shard_map(
        local,
        mesh=mesh,
        in_specs=placed,
        out_specs=(P(("cent", "pts"), None), P(("cent", "pts"))),
        check_vma=False,
    )
```

```python
import functools

import jax
import jax.numpy as jnp
from jax import lax
from jax.experimental import pallas as pl
from jax.experimental.pallas import tpu as pltpu
from jax.sharding import PartitionSpec as P

PANEL = 128
GROUP = 1024
CAND = 4
GROUPS_DEV = 2
REQ = CAND * GROUPS_DEV
PAN_DEV = 64
WIDTH = 1024
N_CENT = 8
CHIPS = 4
N_PTS = 16
ROWS = 16
HALF = 512
LANE = 128
TILES = HALF // LANE
SEND_TILES = CAND * TILES + 1
DENSE = PAN_DEV * TILES
LOAD_TILES = PAN_DEV // ROWS
LISTED = 34

sharpness_divisor = 16.0
evenness_coefficient = 1.0
prior_mass = 1.0

BF16 = jnp.bfloat16
F32 = jnp.float32
MIB = 1 << 20
LOG2E = 1.4426950408889634


def params(mib):
    return pltpu.CompilerParams(vmem_limit_bytes=mib * MIB)


def whole(shape):
    return pl.BlockSpec(shape, lambda *_: (0,) * len(shape))


def smem_spec():
    return pl.BlockSpec(memory_space=pltpu.SMEM)


def vmem_spec():
    return pl.BlockSpec(memory_space=pltpu.VMEM)


def hbm_spec():
    return pl.BlockSpec(memory_space=pltpu.HBM)


def ask_kernel(candidates_in, home_in, loads_in, out, candidates, home, loads, sems):
    copies = [
        pltpu.make_async_copy(source, target, sems.at[n])
        for n, (source, target) in enumerate(((candidates_in, candidates), (home_in, home), (loads_in, loads)))
    ]
    for copy in copies:
        copy.start()
    for copy in copies:
        copy.wait()
    row = lax.broadcasted_iota(jnp.int32, (ROWS, LANE), 0)
    lane = lax.broadcasted_iota(jnp.int32, (ROWS, LANE), 1)
    slots = [home[candidates[n // CAND, n % CAND]] for n in range(REQ)]
    common = jnp.zeros((ROWS, LANE), F32)
    for n, slot in enumerate(slots):
        common = jnp.where((row == 1) & (lane == n), (slot // PAN_DEV).astype(F32), common)
        common = jnp.where((row == 2) & (lane == n), (slot % PAN_DEV).astype(F32), common)
    for o in range(N_CENT):
        tile = common
        for n, slot in enumerate(slots):
            here = jnp.where(slot // PAN_DEV == o, slot % PAN_DEV + 1, 0).astype(F32)
            tile = jnp.where((row == 0) & (lane == n // CAND), tile + here, tile)
        for t in range(LOAD_TILES):
            out[o, t] = loads[t * ROWS : (t + 1) * ROWS]
        out[o, LOAD_TILES] = tile.astype(BF16)


def ask(candidates, home, loads):
    return pl.pallas_call(
        ask_kernel,
        in_specs=[hbm_spec()] * 3,
        out_specs=vmem_spec(),
        out_shape=jax.ShapeDtypeStruct((N_CENT, LOAD_TILES + 1, ROWS, LANE), BF16),
        scratch_shapes=[
            pltpu.SMEM(candidates.shape, jnp.int32),
            pltpu.SMEM(home.shape, jnp.int32),
            pltpu.VMEM(loads.shape, BF16),
            pltpu.SemaphoreType.DMA((3,)),
        ],
        compiler_params=params(60),
        cost_estimate=pl.CostEstimate(flops=1 << 16, bytes_accessed=1 << 18, transcendentals=0),
    )(candidates, home, loads)


def pick_kernel(group, paired, ids, place, table, *refs):
    *outs, held, sems = refs

    def fetch(n, at):
        return pltpu.make_async_copy(table.at[ids[at]], held.at[n], sems.at[0, n])

    def put(n):
        target = outs[(n + 1) // 2].at[n and (n + 1) % 2] if paired else outs[n]
        return pltpu.make_async_copy(held.at[n], target, sems.at[1, n])

    def each(work):
        for n in range(N_CENT - 1):
            reader = n + 1
            at = (place[0] // 2 + reader // 2) % CHIPS * 2 + (place[0] + reader) % 2

            @pl.when(ids[at * GROUPS_DEV + group] >= 0)
            def _(n=n, at=at):
                work(n, at * GROUPS_DEV + group)

    def pass_on(n, at):
        fetch(n, at).wait()
        put(n).start()

    each(lambda n, at: fetch(n, at).start())
    each(pass_on)
    each(lambda n, at: put(n).wait())


def pick_panels(group, paired, ids, place, table):
    count = N_CENT - 1
    one = jax.ShapeDtypeStruct((PANEL, WIDTH), BF16)
    pair = jax.ShapeDtypeStruct((2, PANEL, WIDTH), BF16)
    out = [jax.ShapeDtypeStruct((1, PANEL, WIDTH), BF16), pair, pair, pair] if paired else [one] * count
    return pl.pallas_call(
        functools.partial(pick_kernel, group, paired),
        out_shape=out,
        in_specs=[smem_spec(), smem_spec(), hbm_spec()],
        out_specs=[hbm_spec()] * len(out),
        scratch_shapes=[pltpu.VMEM((count, PANEL, WIDTH), BF16), pltpu.SemaphoreType.DMA((2, count))],
        compiler_params=params(60),
        cost_estimate=pl.CostEstimate(flops=0, bytes_accessed=4 * count * PANEL * WIDTH, transcendentals=0),
    )(ids, place, table)


def score_kernel(group, owners, *refs):
    *panels, table, points, surcharge, out, members, centers, shares, sems = refs
    if len(panels) == CHIPS:
        panels = [panels[o // 2 - 1].at[0] if o % 2 == 0 else panels[-1].at[o // 2] for o in range(1, N_CENT)]
    step = 256
    steps = GROUP // step

    def land(j, source):
        rows = pl.ds(j * PANEL, PANEL)
        return pltpu.make_async_copy(source, centers.at[rows], sems.at[0, j])

    def bring(n):
        rows = pl.ds(n * step, step)
        return pltpu.make_async_copy(points.at[pl.ds(group * GROUP + n * step, step)], members.at[rows], sems.at[1, n])

    for j in range(CAND):

        @pl.when(owners[j] == 0)
        def _(j=j):
            land(j, table.at[owners[CAND + j]]).start()

        for o in range(1, N_CENT):

            @pl.when(owners[j] == o)
            def _(j=j, o=o):
                land(j, panels[o - 1]).start()

    for s in range(steps):
        bring(s).start()
    for j in range(CAND):
        land(j, panels[0]).wait()
    for s in range(steps):
        bring(s).wait()
    wide = centers[...].astype(F32)
    squares = jnp.sum(wide * wide, axis=1, keepdims=True)
    bias = (squares * (1.0 / sharpness_divisor) + evenness_coefficient * surcharge[group]) * LOG2E
    weights = jnp.zeros((CAND * PANEL, LANE), F32)
    for s in range(steps):
        block = members[s * step : (s + 1) * step, :]
        inner = lax.dot_general(centers[...], block, (((1,), (1,)), ((), ())), preferred_element_type=F32)
        logits = inner * (2.0 / sharpness_divisor * LOG2E) - bias
        highest = jnp.max(logits, axis=0, keepdims=True)
        raised = jnp.exp2(logits - highest)
        scale = 1.0 / jnp.sum(raised, axis=0, keepdims=True)
        share = (raised * scale).astype(BF16)
        shares[:, s * step : (s + 1) * step] = share
        rounded = share.astype(F32)
        for part in range(step // LANE):
            weights = weights + rounded[:, part * LANE : (part + 1) * LANE]
    weight = jnp.sum(weights, axis=1, keepdims=True)
    coarse = weight.astype(BF16).astype(F32)
    fine = weight - coarse
    lane = lax.broadcasted_iota(jnp.int32, (PANEL, LANE), 1)
    tile = jnp.zeros((PANEL, LANE), F32)
    for j in range(CAND):
        rows = slice(j * PANEL, (j + 1) * PANEL)
        tile = jnp.where(lane == j, coarse[rows], tile)
        tile = jnp.where(lane == CAND + j, fine[rows], tile)
    wide_step = 256
    for s in range(WIDTH // wide_step):
        part = lax.dot_general(
            shares[...], members[:, s * wide_step : (s + 1) * wide_step], (((1,), (0,)), ((), ())),
            preferred_element_type=F32,
        ).astype(BF16)
        for t in range(wide_step // LANE):
            half, tile_at = divmod(s * (wide_step // LANE) + t, TILES)
            for j in range(CAND):
                for block_at in range(PANEL // ROWS):
                    row = j * PANEL + block_at * ROWS
                    out[block_at * 2 + half, j * TILES + tile_at] = part[row : row + ROWS, t * LANE : (t + 1) * LANE]
    tile = tile.astype(BF16)
    for block_at in range(PANEL // ROWS):
        for half in range(2):
            out[block_at * 2 + half, CAND * TILES] = tile[block_at * ROWS : (block_at + 1) * ROWS]


def score(group, owners, panels, table, points, surcharge):
    return pl.pallas_call(
        functools.partial(score_kernel, group),
        in_specs=[smem_spec()] + [hbm_spec()] * (len(panels) + 2) + [vmem_spec()],
        out_specs=vmem_spec(),
        out_shape=jax.ShapeDtypeStruct((N_PTS, SEND_TILES, ROWS, LANE), BF16),
        scratch_shapes=[
            pltpu.VMEM((GROUP, WIDTH), BF16),
            pltpu.VMEM((CAND * PANEL, WIDTH), BF16),
            pltpu.VMEM((CAND * PANEL, GROUP), BF16),
            pltpu.SemaphoreType.DMA((2, 4)),
        ],
        compiler_params=params(50),
        cost_estimate=pl.CostEstimate(flops=2 << 30, bytes_accessed=5 * MIB, transcendentals=1 << 19),
    )(owners, *panels, table, points, surcharge)


def add_pieces(places, source, total):
    def add(s, carry):
        for j in range(CAND):
            at = places[s * CAND + j] * TILES
            total[pl.ds(at, TILES)] += source[s, j * TILES : (j + 1) * TILES].astype(F32)
        return carry

    lax.fori_loop(0, N_PTS, add, 0, unroll=2)


def sum_weights(lanes, source):
    panel = lax.broadcasted_iota(jnp.int32, (CHIPS * PAN_DEV, LANE), 0)
    weights = jnp.zeros((ROWS, CHIPS * PAN_DEV), F32)
    for n in range(N_PTS):
        chosen = jnp.where(panel == lanes[n : n + 1, :], 1.0, 0.0).astype(BF16)
        weights = weights + lax.dot_general(
            source[n, CAND * TILES], chosen, (((1,), (1,)), ((), ())), preferred_element_type=F32
        )
    return weights


def spread_first_kernel(places, source, lanes, total, total_weights):
    total[...] = jnp.zeros_like(total)
    add_pieces(places, source, total)
    total_weights[...] = sum_weights(lanes, source)


def spread_more_kernel(places, source, lanes, total_in, weights_in, total, total_weights):
    del total_in
    add_pieces(places, source, total)
    total_weights[...] = weights_in[...] + sum_weights(lanes, source)


def spread_join_kernel(places, source, lanes, total_in, weights_in, total, total_weights):
    total[...] = total_in[...]
    total_weights[...] = weights_in[...] + sum_weights(lanes, source)
    add_pieces(places, source, total)


def spread_last_kernel(rows, places, source, lanes, total_in, weights_in, total, own_weights, out1, out2, out3):
    del total_in
    add_pieces(places, source, total)
    weights = weights_in[...] + sum_weights(lanes, source)
    coarse = weights.astype(BF16)
    fine = (weights - coarse.astype(F32)).astype(BF16)
    own_weights[...] = weights[:, 0:LANE]
    for d, out in ((1, out1), (2, out2), (3, out3)):
        first = DENSE + (d - 1) * rows * TILES
        out[0 : rows * TILES] = total[first : first + rows * TILES].astype(BF16)
        out[rows * TILES, :, 0:PAN_DEV] = coarse[:, d * PAN_DEV : (d + 1) * PAN_DEV]
        out[rows * TILES, :, PAN_DEV:LANE] = fine[:, d * PAN_DEV : (d + 1) * PAN_DEV]


def spread(rows, places, lanes, source, before=None, last=False, join=False):
    totals = [
        jax.ShapeDtypeStruct(((PAN_DEV + 3 * rows + 1) * TILES, ROWS, LANE), F32),
        jax.ShapeDtypeStruct((ROWS, CHIPS * PAN_DEV), F32),
    ]
    if last:
        chunk = jax.ShapeDtypeStruct((rows * TILES + 1, ROWS, LANE), BF16)
        kernel = functools.partial(spread_last_kernel, rows)
        out = [totals[0], jax.ShapeDtypeStruct((ROWS, LANE), F32), chunk, chunk, chunk]
    else:
        kernel = spread_join_kernel if join else spread_first_kernel if before is None else spread_more_kernel
        out = totals
    before = before or []
    return pl.pallas_call(
        kernel,
        in_specs=[smem_spec()] + [vmem_spec()] * (2 + len(before)),
        out_specs=[vmem_spec()] * len(out),
        out_shape=out,
        input_output_aliases={3: 0} if before and not join else {},
        compiler_params=params(16),
        cost_estimate=pl.CostEstimate(flops=1 << 21, bytes_accessed=4 * MIB, transcendentals=0),
    )(places, source, lanes, *before)


def begin_kernel(me, own, table, out, old, sem):
    row = pl.multiple_of(me[0] // 2 * ROWS, ROWS)
    column = pl.multiple_of(me[0] % 2 * HALF, HALF)
    fetch = pltpu.make_async_copy(table.at[:, pl.ds(row, ROWS), pl.ds(column, HALF)], old, sem)
    fetch.start()
    fetch.wait()
    for q in range(PAN_DEV):
        for t in range(TILES):
            previous = old[q, :, t * LANE : (t + 1) * LANE].astype(F32)
            out[q * TILES + t] = own[q * TILES + t] + prior_mass * previous


def begin(me, own, table):
    return pl.pallas_call(
        begin_kernel,
        in_specs=[smem_spec(), vmem_spec(), hbm_spec()],
        out_specs=vmem_spec(),
        out_shape=jax.ShapeDtypeStruct((DENSE, ROWS, LANE), F32),
        scratch_shapes=[pltpu.VMEM((PAN_DEV, ROWS, HALF), BF16), pltpu.SemaphoreType.DMA],
        compiler_params=params(48),
        cost_estimate=pl.CostEstimate(flops=1 << 22, bytes_accessed=5 * MIB, transcendentals=0),
    )(me, own, table)


def finish_kernel(rows, numbers, begun, own_weights, in1, in2, in3, lanes, out, total):
    del begun
    weights = own_weights[:, 0:PAN_DEV]
    panel = lax.broadcasted_iota(jnp.int32, (PAN_DEV, LANE), 0)
    for d, arrived in enumerate((in1, in2, in3)):
        chosen = jnp.where(panel == lanes[d : d + 1, :], 1.0, 0.0).astype(BF16)
        weights = weights + lax.dot_general(
            arrived[rows * TILES], chosen, (((1,), (1,)), ((), ())), preferred_element_type=F32
        )
        first = 3 + d * rows

        def add(n, carry, arrived=arrived, first=first):
            at = numbers[first + n] * TILES
            total[pl.ds(at, TILES)] += arrived[pl.ds(n * TILES, TILES)].astype(F32)
            return carry

        lax.fori_loop(0, numbers[d], add, 0)
    inverse = 1.0 / (weights + prior_mass)
    for q in range(PAN_DEV):
        scale = jnp.broadcast_to(inverse[:, q : q + 1], (ROWS, LANE))
        for t in range(TILES):
            out[q // CAND, (q % CAND) * TILES + t] = (total[q * TILES + t] * scale).astype(BF16)
    coarse = weights.astype(BF16)
    fine = (weights - coarse.astype(F32)).astype(BF16)
    for p in range(N_PTS):
        out[p, CAND * TILES, :, 0:PAN_DEV] = coarse
        out[p, CAND * TILES, :, PAN_DEV:LANE] = fine


def finish(rows, numbers, begun, own_weights, arrived, lanes):
    return pl.pallas_call(
        functools.partial(finish_kernel, rows),
        in_specs=[smem_spec()] + [vmem_spec()] * 6,
        out_specs=[vmem_spec(), vmem_spec()],
        out_shape=[
            jax.ShapeDtypeStruct((N_PTS, CAND * TILES + 1, ROWS, LANE), BF16),
            jax.ShapeDtypeStruct(begun.shape, F32),
        ],
        input_output_aliases={1: 1},
        compiler_params=params(32),
        cost_estimate=pl.CostEstimate(flops=1 << 22, bytes_accessed=6 * MIB, transcendentals=0),
    )(numbers, begun, own_weights, *arrived, lanes)[0]


def place_kernel(me, pieces, out, loads):
    for block_at in range(PANEL // ROWS):
        for half in range(2):
            for q in range(CAND):
                for t in range(TILES):
                    column = half * HALF + t * LANE
                    out[q, block_at * ROWS : (block_at + 1) * ROWS, column : column + LANE] = pieces[
                        block_at * 2 + half, q * TILES + t
                    ]
    lane = lax.broadcasted_iota(jnp.int32, (ROWS, LANE), 1)
    row = lax.broadcasted_iota(jnp.int32, (ROWS, LANE), 0)
    wanted = me[0] * CAND + row
    chosen = jnp.where((row < CAND) & (lane % PAN_DEV == wanted), 1.0, 0.0).astype(BF16)
    for block_at in range(PANEL // ROWS):
        pair = pieces[block_at * 2, CAND * TILES]
        part = lax.dot_general(chosen, pair, (((1,), (1,)), ((), ())), preferred_element_type=F32)
        loads[:, block_at * ROWS : (block_at + 1) * ROWS] = part[0:CAND]


def place(me, pieces):
    return pl.pallas_call(
        place_kernel,
        grid=(1,),
        in_specs=[smem_spec(), whole(pieces.shape)],
        out_specs=[whole((CAND, PANEL, WIDTH)), whole((CAND, PANEL))],
        out_shape=[
            jax.ShapeDtypeStruct((CAND, PANEL, WIDTH), BF16),
            jax.ShapeDtypeStruct((CAND, PANEL), F32),
        ],
        compiler_params=params(32),
        cost_estimate=pl.CostEstimate(flops=1 << 20, bytes_accessed=2 * MIB, transcendentals=0),
    )(me, pieces)


def shift(dy, dk):
    return [(y * 2 + k, ((y + dy) % CHIPS) * 2 + (k + dk) % 2) for y in range(CHIPS) for k in range(2)]


def exchange(x, axis):
    return lax.all_to_all(x, axis, split_axis=0, concat_axis=0, tiled=True)


def local(points, centroids, prev_loads, candidates, panel_home):
    me = lax.axis_index("pts")
    here = lax.axis_index("cent")
    chip, core = here // 2, here % 2
    shelf = centroids.reshape(PAN_DEV, PANEL, WIDTH)

    with jax.named_scope("requests"):
        answered = exchange(ask(candidates, panel_home, prev_loads.reshape(PAN_DEV, PANEL)), "cent")
        asked = answered[:, LOAD_TILES, 0, 0:GROUPS_DEV].astype(jnp.int32).reshape(-1) - 1

    tie = lax.optimization_barrier
    with jax.named_scope("gather_panels"):
        arrived = []
        for g in range(GROUPS_DEV):
            ready = pick_panels(g, g == 1, asked, here.reshape(1), shelf)
            if g == 0:
                arrived.append([lax.ppermute(x, "cent", shift((n + 1) // 2, (n + 1) % 2)) for n, x in enumerate(ready)])
            else:
                direct = [lax.ppermute(ready[d], "cent", shift(d, 0)) for d in range(1, CHIPS)]
                passed = jnp.concatenate([ready[0]] + [x[1:2] for x in direct])
                arrived.append(direct + [lax.ppermute(passed, "cent", shift(0, 1))])
            if g == 0:
                answered, arrived[g][0] = tie((answered, arrived[g][0]))
                asked, arrived[g][1] = tie((asked, arrived[g][1]))

    with jax.named_scope("own_requests"):
        slots = jnp.sum(
            jnp.where(candidates.reshape(REQ)[:, None] == jnp.arange(panel_home.shape[0], dtype=jnp.int32), panel_home[None, :], 0),
            axis=1,
        )
        owners = slots // PAN_DEV
        seen = (chip - owners // 2) % CHIPS * 2 + (core - owners) % 2
        seen = jnp.stack([seen.reshape(GROUPS_DEV, CAND), (slots % PAN_DEV).reshape(GROUPS_DEV, CAND)], axis=1)
        seen = [seen[g].reshape(-1) for g in range(GROUPS_DEV)]

    with jax.named_scope("all_requests"):
        ring = answered[:, LOAD_TILES, 1:3, 0:REQ].astype(jnp.int32)
        ring = ring[:, 0] * PAN_DEV + ring[:, 1]
        everyone = exchange(jnp.broadcast_to(ring, (N_PTS, N_CENT, REQ)), "pts")

        numbers = jnp.arange(N_CENT * PAN_DEV, dtype=jnp.int32)
        by_chip = jnp.transpose(everyone.reshape(N_PTS, CHIPS, 2 * REQ), (1, 0, 2)).reshape(CHIPS, -1)
        asked_by = jnp.any(by_chip[:, :, None] == numbers, axis=1).reshape(CHIPS, N_CENT, PAN_DEV)
        below = jnp.arange(PAN_DEV)[:, None] < jnp.arange(PAN_DEV)[None, :]
        ranks = lax.dot_general(
            asked_by.astype(BF16), below.astype(BF16), (((2,), (0,)), ((), ())), preferred_element_type=F32
        ).astype(jnp.int32)
        lengths = jnp.sum(asked_by.astype(jnp.int32), axis=2)
        off_chip = jnp.arange(N_CENT)[None, :] // 2 != jnp.arange(CHIPS)[:, None]
        too_long = jnp.any(off_chip & (lengths > LISTED))

        pair = jnp.stack(
            [lax.dynamic_index_in_dim(everyone, at, 1, keepdims=False) for at in (here, chip * 2 + 1 - core)]
        )
        pair = jnp.transpose(pair.reshape(2, N_PTS, GROUPS_DEV, CAND), (2, 0, 1, 3))
        owner = pair // PAN_DEV
        relative = (owner // 2 - chip) % CHIPS
        my_ranks = lax.dynamic_index_in_dim(ranks, chip, 0, keepdims=False).reshape(-1)
        rank = jnp.sum(jnp.where(pair[..., None] == numbers, my_ranks, 0), axis=4)
        ours = owner % 2 == core

        def sender(rows, rank):
            at = jnp.where(relative == 0, pair % PAN_DEV, rank)
            known = ours & ((relative == 0) | (rank < rows))
            first = jnp.where(relative == 0, 0, PAN_DEV + (relative - 1) * rows)
            places = jnp.where(known, first + at, PAN_DEV + 3 * rows)
            lane = jnp.where(known, relative * PAN_DEV + at, CHIPS * PAN_DEV)
            lanes = jnp.pad(
                jnp.concatenate([lane, lane], axis=3), ((0, 0), (0, 0), (0, 0), (0, LANE - 2 * CAND)),
                constant_values=CHIPS * PAN_DEV,
            )
            return [
                (places[g, n].reshape(-1), lanes[g, n]) for g in range(GROUPS_DEV) for n in range(2)
            ]

        def receiver(rows, count, panels):
            numbers = jnp.concatenate([count, panels[:, :rows].reshape(-1)])
            lane = jnp.where(jnp.arange(PAN_DEV) < jnp.minimum(count, rows)[:, None], panels, PAN_DEV)
            return numbers, jnp.concatenate([lane, lane], axis=1)

        behind = [(chip - d) % CHIPS for d in range(1, CHIPS)]
        pick = lambda x, y: lax.dynamic_index_in_dim(lax.dynamic_index_in_dim(x, y, 0, False), here, 0, False)
        named = jnp.stack([pick(asked_by, y) for y in behind])
        order = jnp.stack([pick(ranks, y) for y in behind])
        spots = jnp.arange(PAN_DEV, dtype=jnp.int32)
        listed = jnp.sum(
            jnp.where(named[:, None, :] & (order[:, None, :] == spots[None, :, None]), spots, 0), axis=2
        )
        count = jnp.minimum(jnp.sum(named.astype(jnp.int32), axis=1), LISTED)
        short = sender(LISTED, rank)
        short_back = receiver(LISTED, count, listed)
        seen[1], too_long, short, short_back = tie((seen[1], too_long, short, short_back))

    with jax.named_scope("loads"):
        load_table = answered[:, :LOAD_TILES].reshape(N_CENT * PAN_DEV, PANEL)
        loads = jnp.take(load_table, slots, axis=0, mode="clip").astype(F32)
        surcharge = jnp.log(loads).reshape(GROUPS_DEV, CAND * PANEL, 1)

    sources = []
    for g in range(GROUPS_DEV):
        with jax.named_scope("score"):
            pieces = score(g, seen[g], arrived[g], shelf, points, surcharge)
        with jax.named_scope("split_pieces"):
            if g == 0:
                sources.append(exchange(pieces, "pts"))
            else:
                with jax.named_scope("sum_over_chips"):
                    sources[0], pieces = tie((sources[0], pieces))
                    sources.append(lax.ppermute(sources[0], "cent", shift(0, 1)))
                    begun = spread(LISTED, *short[0], sources[0])
                    begun = spread(LISTED, *short[1], sources[1], before=begun)
                mine, begun = tie((exchange(pieces, "pts"), begun))
                sources += [mine, lax.ppermute(mine, "cent", shift(0, 1))]

    def sum_over_chips(rows, to, begun, numbers, back_lanes):
        own, own_weights, *far = spread(rows, *to[3], sources[3], before=begun, last=True)
        back = [lax.ppermute(far[d - 1], "cent", shift(d, 0)) for d in range(1, CHIPS)]
        return finish(rows, numbers, begin(me.reshape(1), own, shelf), own_weights, back, back_lanes)

    def send_all():
        everything = jnp.broadcast_to(spots, (CHIPS - 1, PAN_DEV))
        count = jnp.full((CHIPS - 1,), PAN_DEV, jnp.int32)
        to = sender(PAN_DEV, pair % PAN_DEV)
        begun = None
        for n in range(3):
            begun = spread(PAN_DEV, *to[n], sources[n], before=begun)
        return sum_over_chips(PAN_DEV, to, begun, *receiver(PAN_DEV, count, everything))

    with jax.named_scope("sum_over_chips"):
        begun = spread(LISTED, *short[2], sources[2], before=begun, join=True)
        begun, sources[3] = tie((begun, sources[3]))
        fresh = lax.cond(too_long, send_all, lambda: sum_over_chips(LISTED, short, begun, *short_back))

    with jax.named_scope("place"):
        new_centroids, new_loads = place(me.reshape(1), exchange(fresh, "pts"))
    return new_centroids.reshape(CAND * PANEL, WIDTH), new_loads.reshape(CAND * PANEL)


def solution(mesh):
    placed = (P(("pts", "cent"), None), P("cent", None), P("cent"), P(("pts", "cent"), None), P())
    return jax.shard_map(
        local,
        mesh=mesh,
        in_specs=placed,
        out_specs=(P(("cent", "pts"), None), P(("cent", "pts"))),
        check_vma=False,
    )
```

```python
import functools

import jax
import jax.numpy as jnp
from jax import lax
from jax.experimental import pallas as pl
from jax.experimental.pallas import tpu as pltpu
from jax.sharding import PartitionSpec as P

PANEL = 128
GROUP = 1024
CAND = 4
GROUPS_DEV = 2
REQ = CAND * GROUPS_DEV
PAN_DEV = 64
WIDTH = 1024
N_CENT = 8
CHIPS = 4
N_PTS = 16
ROWS = 16
HALF = 512
LANE = 128
TILES = HALF // LANE
SEND_TILES = CAND * TILES + 1
DENSE = PAN_DEV * TILES
LOAD_TILES = PAN_DEV // ROWS
LISTED = 34

sharpness_divisor = 16.0
evenness_coefficient = 1.0
prior_mass = 1.0

BF16 = jnp.bfloat16
F32 = jnp.float32
MIB = 1 << 20
LOG2E = 1.4426950408889634


def params(mib):
    return pltpu.CompilerParams(vmem_limit_bytes=mib * MIB)


def whole(shape):
    return pl.BlockSpec(shape, lambda *_: (0,) * len(shape))


def smem_spec():
    return pl.BlockSpec(memory_space=pltpu.SMEM)


def vmem_spec():
    return pl.BlockSpec(memory_space=pltpu.VMEM)


def hbm_spec():
    return pl.BlockSpec(memory_space=pltpu.HBM)


def ask_kernel(candidates_in, home_in, loads_in, out, candidates, home, loads, sems):
    copies = [
        pltpu.make_async_copy(source, target, sems.at[n])
        for n, (source, target) in enumerate(((candidates_in, candidates), (home_in, home), (loads_in, loads)))
    ]
    for copy in copies:
        copy.start()
    for copy in copies:
        copy.wait()
    row = lax.broadcasted_iota(jnp.int32, (ROWS, LANE), 0)
    lane = lax.broadcasted_iota(jnp.int32, (ROWS, LANE), 1)
    slots = [home[candidates[n // CAND, n % CAND]] for n in range(REQ)]
    common = jnp.zeros((ROWS, LANE), F32)
    for n, slot in enumerate(slots):
        common = jnp.where((row == 1) & (lane == n), (slot // PAN_DEV).astype(F32), common)
        common = jnp.where((row == 2) & (lane == n), (slot % PAN_DEV).astype(F32), common)
    for o in range(N_CENT):
        tile = common
        for n, slot in enumerate(slots):
            here = jnp.where(slot // PAN_DEV == o, slot % PAN_DEV + 1, 0).astype(F32)
            tile = jnp.where((row == 0) & (lane == n // CAND), tile + here, tile)
        for t in range(LOAD_TILES):
            out[o, t] = loads[t * ROWS : (t + 1) * ROWS]
        out[o, LOAD_TILES] = tile.astype(BF16)


def ask(candidates, home, loads):
    return pl.pallas_call(
        ask_kernel,
        in_specs=[hbm_spec()] * 3,
        out_specs=vmem_spec(),
        out_shape=jax.ShapeDtypeStruct((N_CENT, LOAD_TILES + 1, ROWS, LANE), BF16),
        scratch_shapes=[
            pltpu.SMEM(candidates.shape, jnp.int32),
            pltpu.SMEM(home.shape, jnp.int32),
            pltpu.VMEM(loads.shape, BF16),
            pltpu.SemaphoreType.DMA((3,)),
        ],
        compiler_params=params(60),
        cost_estimate=pl.CostEstimate(flops=1 << 16, bytes_accessed=1 << 18, transcendentals=0),
    )(candidates, home, loads)


def pick_kernel(group, paired, ids, place, table, *refs):
    *outs, held, sems = refs

    def fetch(n, at):
        return pltpu.make_async_copy(table.at[ids[at]], held.at[n], sems.at[0, n])

    def put(n):
        target = outs[(n + 1) // 2].at[n and (n + 1) % 2] if paired else outs[n]
        return pltpu.make_async_copy(held.at[n], target, sems.at[1, n])

    def each(work):
        for n in range(N_CENT - 1):
            reader = n + 1
            at = (place[0] // 2 + reader // 2) % CHIPS * 2 + (place[0] + reader) % 2

            @pl.when(ids[at * GROUPS_DEV + group] >= 0)
            def _(n=n, at=at):
                work(n, at * GROUPS_DEV + group)

    def pass_on(n, at):
        fetch(n, at).wait()
        put(n).start()

    each(lambda n, at: fetch(n, at).start())
    each(pass_on)
    each(lambda n, at: put(n).wait())


def pick_panels(group, paired, ids, place, table):
    count = N_CENT - 1
    one = jax.ShapeDtypeStruct((PANEL, WIDTH), BF16)
    pair = jax.ShapeDtypeStruct((2, PANEL, WIDTH), BF16)
    out = [jax.ShapeDtypeStruct((1, PANEL, WIDTH), BF16), pair, pair, pair] if paired else [one] * count
    return pl.pallas_call(
        functools.partial(pick_kernel, group, paired),
        out_shape=out,
        in_specs=[smem_spec(), smem_spec(), hbm_spec()],
        out_specs=[hbm_spec()] * len(out),
        scratch_shapes=[pltpu.VMEM((count, PANEL, WIDTH), BF16), pltpu.SemaphoreType.DMA((2, count))],
        compiler_params=params(60),
        cost_estimate=pl.CostEstimate(flops=0, bytes_accessed=4 * count * PANEL * WIDTH, transcendentals=0),
    )(ids, place, table)


def score_kernel(group, owners, *refs):
    *panels, table, points, surcharge, out, members, centers, shares, sems = refs
    if len(panels) == CHIPS:
        panels = [panels[o // 2 - 1].at[0] if o % 2 == 0 else panels[-1].at[o // 2] for o in range(1, N_CENT)]
    step = 256
    steps = GROUP // step

    def land(j, source):
        rows = pl.ds(j * PANEL, PANEL)
        return pltpu.make_async_copy(source, centers.at[rows], sems.at[0, j])

    def bring(n):
        rows = pl.ds(n * step, step)
        return pltpu.make_async_copy(points.at[pl.ds(group * GROUP + n * step, step)], members.at[rows], sems.at[1, n])

    for j in range(CAND):

        @pl.when(owners[j] == 0)
        def _(j=j):
            land(j, table.at[owners[CAND + j]]).start()

        for o in range(1, N_CENT):

            @pl.when(owners[j] == o)
            def _(j=j, o=o):
                land(j, panels[o - 1]).start()

    for s in range(steps):
        bring(s).start()
    for j in range(CAND):
        land(j, panels[0]).wait()
    for s in range(steps):
        bring(s).wait()
    wide = centers[...].astype(F32)
    squares = jnp.sum(wide * wide, axis=1, keepdims=True)
    bias = (squares * (1.0 / sharpness_divisor) + evenness_coefficient * surcharge[group]) * LOG2E
    weights = jnp.zeros((CAND * PANEL, LANE), F32)
    for s in range(steps):
        block = members[s * step : (s + 1) * step, :]
        inner = lax.dot_general(centers[...], block, (((1,), (1,)), ((), ())), preferred_element_type=F32)
        logits = inner * (2.0 / sharpness_divisor * LOG2E) - bias
        highest = jnp.max(logits, axis=0, keepdims=True)
        raised = jnp.exp2(logits - highest)
        scale = 1.0 / jnp.sum(raised, axis=0, keepdims=True)
        share = (raised * scale).astype(BF16)
        shares[:, s * step : (s + 1) * step] = share
        rounded = share.astype(F32)
        for part in range(step // LANE):
            weights = weights + rounded[:, part * LANE : (part + 1) * LANE]
    weight = jnp.sum(weights, axis=1, keepdims=True)
    coarse = weight.astype(BF16).astype(F32)
    fine = weight - coarse
    lane = lax.broadcasted_iota(jnp.int32, (PANEL, LANE), 1)
    tile = jnp.zeros((PANEL, LANE), F32)
    for j in range(CAND):
        rows = slice(j * PANEL, (j + 1) * PANEL)
        tile = jnp.where(lane == j, coarse[rows], tile)
        tile = jnp.where(lane == CAND + j, fine[rows], tile)
    wide_step = 256
    for s in range(WIDTH // wide_step):
        part = lax.dot_general(
            shares[...], members[:, s * wide_step : (s + 1) * wide_step], (((1,), (0,)), ((), ())),
            preferred_element_type=F32,
        ).astype(BF16)
        for t in range(wide_step // LANE):
            half, tile_at = divmod(s * (wide_step // LANE) + t, TILES)
            for j in range(CAND):
                for block_at in range(PANEL // ROWS):
                    row = j * PANEL + block_at * ROWS
                    out[block_at * 2 + half, j * TILES + tile_at] = part[row : row + ROWS, t * LANE : (t + 1) * LANE]
    tile = tile.astype(BF16)
    for block_at in range(PANEL // ROWS):
        for half in range(2):
            out[block_at * 2 + half, CAND * TILES] = tile[block_at * ROWS : (block_at + 1) * ROWS]


def score(group, owners, panels, table, points, surcharge):
    return pl.pallas_call(
        functools.partial(score_kernel, group),
        in_specs=[smem_spec()] + [hbm_spec()] * (len(panels) + 2) + [vmem_spec()],
        out_specs=vmem_spec(),
        out_shape=jax.ShapeDtypeStruct((N_PTS, SEND_TILES, ROWS, LANE), BF16),
        scratch_shapes=[
            pltpu.VMEM((GROUP, WIDTH), BF16),
            pltpu.VMEM((CAND * PANEL, WIDTH), BF16),
            pltpu.VMEM((CAND * PANEL, GROUP), BF16),
            pltpu.SemaphoreType.DMA((2, 4)),
        ],
        compiler_params=params(50),
        cost_estimate=pl.CostEstimate(flops=2 << 30, bytes_accessed=5 * MIB, transcendentals=1 << 19),
    )(owners, *panels, table, points, surcharge)


def add_pieces(places, source, total):
    def add(s, carry):
        for j in range(CAND):
            at = places[s * CAND + j] * TILES
            total[pl.ds(at, TILES)] += source[s, j * TILES : (j + 1) * TILES].astype(F32)
        return carry

    lax.fori_loop(0, N_PTS, add, 0, unroll=2)


def sum_weights(lanes, source):
    panel = lax.broadcasted_iota(jnp.int32, (CHIPS * PAN_DEV, LANE), 0)
    weights = jnp.zeros((ROWS, CHIPS * PAN_DEV), F32)
    for n in range(N_PTS):
        chosen = jnp.where(panel == lanes[n : n + 1, :], 1.0, 0.0).astype(BF16)
        weights = weights + lax.dot_general(
            source[n, CAND * TILES], chosen, (((1,), (1,)), ((), ())), preferred_element_type=F32
        )
    return weights


def spread_first_kernel(places, source, lanes, total, total_weights):
    total[...] = jnp.zeros_like(total)
    add_pieces(places, source, total)
    total_weights[...] = sum_weights(lanes, source)


def spread_more_kernel(places, source, lanes, total_in, weights_in, total, total_weights):
    del total_in
    add_pieces(places, source, total)
    total_weights[...] = weights_in[...] + sum_weights(lanes, source)


def spread_join_kernel(places, source, lanes, total_in, weights_in, total, total_weights):
    total[...] = total_in[...]
    total_weights[...] = weights_in[...] + sum_weights(lanes, source)
    add_pieces(places, source, total)


def spread_last_kernel(rows, places, source, lanes, total_in, weights_in, total, own_weights, out1, out2, out3):
    del total_in
    add_pieces(places, source, total)
    weights = weights_in[...] + sum_weights(lanes, source)
    coarse = weights.astype(BF16)
    fine = (weights - coarse.astype(F32)).astype(BF16)
    own_weights[...] = weights[:, 0:LANE]
    for d, out in ((1, out1), (2, out2), (3, out3)):
        first = DENSE + (d - 1) * rows * TILES
        out[0 : rows * TILES] = total[first : first + rows * TILES].astype(BF16)
        out[rows * TILES, :, 0:PAN_DEV] = coarse[:, d * PAN_DEV : (d + 1) * PAN_DEV]
        out[rows * TILES, :, PAN_DEV:LANE] = fine[:, d * PAN_DEV : (d + 1) * PAN_DEV]


def spread(rows, places, lanes, source, before=None, last=False, join=False):
    totals = [
        jax.ShapeDtypeStruct(((PAN_DEV + 3 * rows + 1) * TILES, ROWS, LANE), F32),
        jax.ShapeDtypeStruct((ROWS, CHIPS * PAN_DEV), F32),
    ]
    if last:
        chunk = jax.ShapeDtypeStruct((rows * TILES + 1, ROWS, LANE), BF16)
        kernel = functools.partial(spread_last_kernel, rows)
        out = [totals[0], jax.ShapeDtypeStruct((ROWS, LANE), F32), chunk, chunk, chunk]
    else:
        kernel = spread_join_kernel if join else spread_first_kernel if before is None else spread_more_kernel
        out = totals
    before = before or []
    return pl.pallas_call(
        kernel,
        in_specs=[smem_spec()] + [vmem_spec()] * (2 + len(before)),
        out_specs=[vmem_spec()] * len(out),
        out_shape=out,
        input_output_aliases={3: 0} if before and not join else {},
        compiler_params=params(16),
        cost_estimate=pl.CostEstimate(flops=1 << 21, bytes_accessed=4 * MIB, transcendentals=0),
    )(places, source, lanes, *before)


def begin_kernel(me, own, table, out, old, sem):
    row = pl.multiple_of(me[0] // 2 * ROWS, ROWS)
    column = pl.multiple_of(me[0] % 2 * HALF, HALF)
    fetch = pltpu.make_async_copy(table.at[:, pl.ds(row, ROWS), pl.ds(column, HALF)], old, sem)
    fetch.start()
    fetch.wait()
    for q in range(PAN_DEV):
        for t in range(TILES):
            previous = old[q, :, t * LANE : (t + 1) * LANE].astype(F32)
            out[q * TILES + t] = own[q * TILES + t] + prior_mass * previous


def begin(me, own, table):
    return pl.pallas_call(
        begin_kernel,
        in_specs=[smem_spec(), vmem_spec(), hbm_spec()],
        out_specs=vmem_spec(),
        out_shape=jax.ShapeDtypeStruct((DENSE, ROWS, LANE), F32),
        scratch_shapes=[pltpu.VMEM((PAN_DEV, ROWS, HALF), BF16), pltpu.SemaphoreType.DMA],
        compiler_params=params(48),
        cost_estimate=pl.CostEstimate(flops=1 << 22, bytes_accessed=5 * MIB, transcendentals=0),
    )(me, own, table)


def finish_kernel(rows, numbers, begun, own_weights, in1, in2, in3, lanes, out, total):
    del begun
    weights = own_weights[:, 0:PAN_DEV]
    panel = lax.broadcasted_iota(jnp.int32, (PAN_DEV, LANE), 0)
    for d, arrived in enumerate((in1, in2, in3)):
        chosen = jnp.where(panel == lanes[d : d + 1, :], 1.0, 0.0).astype(BF16)
        weights = weights + lax.dot_general(
            arrived[rows * TILES], chosen, (((1,), (1,)), ((), ())), preferred_element_type=F32
        )
        first = 3 + d * rows

        def add(n, carry, arrived=arrived, first=first):
            at = numbers[first + n] * TILES
            total[pl.ds(at, TILES)] += arrived[pl.ds(n * TILES, TILES)].astype(F32)
            return carry

        lax.fori_loop(0, numbers[d], add, 0)
    inverse = 1.0 / (weights + prior_mass)
    for q in range(PAN_DEV):
        scale = jnp.broadcast_to(inverse[:, q : q + 1], (ROWS, LANE))
        for t in range(TILES):
            out[q // CAND, (q % CAND) * TILES + t] = (total[q * TILES + t] * scale).astype(BF16)
    coarse = weights.astype(BF16)
    fine = (weights - coarse.astype(F32)).astype(BF16)
    for p in range(N_PTS):
        out[p, CAND * TILES, :, 0:PAN_DEV] = coarse
        out[p, CAND * TILES, :, PAN_DEV:LANE] = fine


def finish(rows, numbers, begun, own_weights, arrived, lanes):
    return pl.pallas_call(
        functools.partial(finish_kernel, rows),
        in_specs=[smem_spec()] + [vmem_spec()] * 6,
        out_specs=[vmem_spec(), vmem_spec()],
        out_shape=[
            jax.ShapeDtypeStruct((N_PTS, CAND * TILES + 1, ROWS, LANE), BF16),
            jax.ShapeDtypeStruct(begun.shape, F32),
        ],
        input_output_aliases={1: 1},
        compiler_params=params(32),
        cost_estimate=pl.CostEstimate(flops=1 << 22, bytes_accessed=6 * MIB, transcendentals=0),
    )(numbers, begun, own_weights, *arrived, lanes)[0]


def place_kernel(me, pieces, out, loads):
    for block_at in range(PANEL // ROWS):
        for half in range(2):
            for q in range(CAND):
                for t in range(TILES):
                    column = half * HALF + t * LANE
                    out[q, block_at * ROWS : (block_at + 1) * ROWS, column : column + LANE] = pieces[
                        block_at * 2 + half, q * TILES + t
                    ]
    lane = lax.broadcasted_iota(jnp.int32, (ROWS, LANE), 1)
    row = lax.broadcasted_iota(jnp.int32, (ROWS, LANE), 0)
    wanted = me[0] * CAND + row
    chosen = jnp.where((row < CAND) & (lane % PAN_DEV == wanted), 1.0, 0.0).astype(BF16)
    for block_at in range(PANEL // ROWS):
        pair = pieces[block_at * 2, CAND * TILES]
        part = lax.dot_general(chosen, pair, (((1,), (1,)), ((), ())), preferred_element_type=F32)
        loads[:, block_at * ROWS : (block_at + 1) * ROWS] = part[0:CAND]


def place(me, pieces):
    return pl.pallas_call(
        place_kernel,
        grid=(1,),
        in_specs=[smem_spec(), whole(pieces.shape)],
        out_specs=[whole((CAND, PANEL, WIDTH)), whole((CAND, PANEL))],
        out_shape=[
            jax.ShapeDtypeStruct((CAND, PANEL, WIDTH), BF16),
            jax.ShapeDtypeStruct((CAND, PANEL), F32),
        ],
        compiler_params=params(32),
        cost_estimate=pl.CostEstimate(flops=1 << 20, bytes_accessed=2 * MIB, transcendentals=0),
    )(me, pieces)


def shift(dy, dk):
    return [(y * 2 + k, ((y + dy) % CHIPS) * 2 + (k + dk) % 2) for y in range(CHIPS) for k in range(2)]


def exchange(x, axis):
    return lax.all_to_all(x, axis, split_axis=0, concat_axis=0, tiled=True)


def local(points, centroids, prev_loads, candidates, panel_home):
    me = lax.axis_index("pts")
    here = lax.axis_index("cent")
    chip, core = here // 2, here % 2
    shelf = centroids.reshape(PAN_DEV, PANEL, WIDTH)

    with jax.named_scope("requests"):
        answered = exchange(ask(candidates, panel_home, prev_loads.reshape(PAN_DEV, PANEL)), "cent")
        asked = answered[:, LOAD_TILES, 0, 0:GROUPS_DEV].astype(jnp.int32).reshape(-1) - 1

    tie = lax.optimization_barrier
    with jax.named_scope("gather_panels"):
        arrived = []
        for g in range(GROUPS_DEV):
            ready = pick_panels(g, g == 1, asked, here.reshape(1), shelf)
            if g == 0:
                arrived.append([lax.ppermute(x, "cent", shift((n + 1) // 2, (n + 1) % 2)) for n, x in enumerate(ready)])
            else:
                direct = [lax.ppermute(ready[d], "cent", shift(d, 0)) for d in range(1, CHIPS)]
                passed = jnp.concatenate([ready[0]] + [x[1:2] for x in direct])
                arrived.append(direct + [lax.ppermute(passed, "cent", shift(0, 1))])
            if g == 0:
                answered, arrived[g][0] = tie((answered, arrived[g][0]))
                asked, arrived[g][1] = tie((asked, arrived[g][1]))

    with jax.named_scope("own_requests"):
        slots = jnp.sum(
            jnp.where(candidates.reshape(REQ)[:, None] == jnp.arange(panel_home.shape[0], dtype=jnp.int32), panel_home[None, :], 0),
            axis=1,
        )
        owners = slots // PAN_DEV
        seen = (chip - owners // 2) % CHIPS * 2 + (core - owners) % 2
        seen = jnp.stack([seen.reshape(GROUPS_DEV, CAND), (slots % PAN_DEV).reshape(GROUPS_DEV, CAND)], axis=1)
        seen = [seen[g].reshape(-1) for g in range(GROUPS_DEV)]

    with jax.named_scope("all_requests"):
        ring = answered[:, LOAD_TILES, 1:3, 0:REQ].astype(jnp.int32)
        ring = ring[:, 0] * PAN_DEV + ring[:, 1]
        everyone = exchange(jnp.broadcast_to(ring[None, :, :, None], (N_PTS, N_CENT, REQ, 128)), "pts")[..., 0]

        numbers = jnp.arange(N_CENT * PAN_DEV, dtype=jnp.int32)
        by_chip = jnp.transpose(everyone.reshape(N_PTS, CHIPS, 2 * REQ), (1, 0, 2)).reshape(CHIPS, -1)
        asked_by = jnp.any(by_chip[:, :, None] == numbers, axis=1).reshape(CHIPS, N_CENT, PAN_DEV)
        below = jnp.arange(PAN_DEV)[:, None] < jnp.arange(PAN_DEV)[None, :]
        ranks = lax.dot_general(
            asked_by.astype(BF16), below.astype(BF16), (((2,), (0,)), ((), ())), preferred_element_type=F32
        ).astype(jnp.int32)
        lengths = jnp.sum(asked_by.astype(jnp.int32), axis=2)
        off_chip = jnp.arange(N_CENT)[None, :] // 2 != jnp.arange(CHIPS)[:, None]
        too_long = jnp.any(off_chip & (lengths > LISTED))

        pair = jnp.stack(
            [lax.dynamic_index_in_dim(everyone, at, 1, keepdims=False) for at in (here, chip * 2 + 1 - core)]
        )
        pair = jnp.transpose(pair.reshape(2, N_PTS, GROUPS_DEV, CAND), (2, 0, 1, 3))
        owner = pair // PAN_DEV
        relative = (owner // 2 - chip) % CHIPS
        my_ranks = lax.dynamic_index_in_dim(ranks, chip, 0, keepdims=False).reshape(-1)
        rank = jnp.sum(jnp.where(pair[..., None] == numbers, my_ranks, 0), axis=4)
        ours = owner % 2 == core

        def sender(rows, rank):
            at = jnp.where(relative == 0, pair % PAN_DEV, rank)
            known = ours & ((relative == 0) | (rank < rows))
            first = jnp.where(relative == 0, 0, PAN_DEV + (relative - 1) * rows)
            places = jnp.where(known, first + at, PAN_DEV + 3 * rows)
            lane = jnp.where(known, relative * PAN_DEV + at, CHIPS * PAN_DEV)
            lanes = jnp.pad(
                jnp.concatenate([lane, lane], axis=3), ((0, 0), (0, 0), (0, 0), (0, LANE - 2 * CAND)),
                constant_values=CHIPS * PAN_DEV,
            )
            return [
                (places[g, n].reshape(-1), lanes[g, n]) for g in range(GROUPS_DEV) for n in range(2)
            ]

        def receiver(rows, count, panels):
            numbers = jnp.concatenate([count, panels[:, :rows].reshape(-1)])
            lane = jnp.where(jnp.arange(PAN_DEV) < jnp.minimum(count, rows)[:, None], panels, PAN_DEV)
            return numbers, jnp.concatenate([lane, lane], axis=1)

        behind = [(chip - d) % CHIPS for d in range(1, CHIPS)]
        pick = lambda x, y: lax.dynamic_index_in_dim(lax.dynamic_index_in_dim(x, y, 0, False), here, 0, False)
        named = jnp.stack([pick(asked_by, y) for y in behind])
        order = jnp.stack([pick(ranks, y) for y in behind])
        spots = jnp.arange(PAN_DEV, dtype=jnp.int32)
        listed = jnp.sum(
            jnp.where(named[:, None, :] & (order[:, None, :] == spots[None, :, None]), spots, 0), axis=2
        )
        count = jnp.minimum(jnp.sum(named.astype(jnp.int32), axis=1), LISTED)
        short = sender(LISTED, rank)
        short_back = receiver(LISTED, count, listed)
        seen[1], too_long, short, short_back = tie((seen[1], too_long, short, short_back))

    with jax.named_scope("loads"):
        load_table = answered[:, :LOAD_TILES].reshape(N_CENT * PAN_DEV, PANEL)
        loads = jnp.take(load_table, slots, axis=0, mode="clip").astype(F32)
        surcharge = jnp.log(loads).reshape(GROUPS_DEV, CAND * PANEL, 1)

    sources = []
    for g in range(GROUPS_DEV):
        with jax.named_scope("score"):
            pieces = score(g, seen[g], arrived[g], shelf, points, surcharge)
        with jax.named_scope("split_pieces"):
            if g == 0:
                sources.append(exchange(pieces, "pts"))
            else:
                with jax.named_scope("sum_over_chips"):
                    sources[0], pieces = tie((sources[0], pieces))
                    sources.append(lax.ppermute(sources[0], "cent", shift(0, 1)))
                    begun = spread(LISTED, *short[0], sources[0])
                    begun = spread(LISTED, *short[1], sources[1], before=begun)
                mine, begun = tie((exchange(pieces, "pts"), begun))
                sources += [mine, lax.ppermute(mine, "cent", shift(0, 1))]

    def sum_over_chips(rows, to, begun, numbers, back_lanes):
        own, own_weights, *far = spread(rows, *to[3], sources[3], before=begun, last=True)
        back = [lax.ppermute(far[d - 1], "cent", shift(d, 0)) for d in range(1, CHIPS)]
        return finish(rows, numbers, begin(me.reshape(1), own, shelf), own_weights, back, back_lanes)

    def send_all():
        everything = jnp.broadcast_to(spots, (CHIPS - 1, PAN_DEV))
        count = jnp.full((CHIPS - 1,), PAN_DEV, jnp.int32)
        to = sender(PAN_DEV, pair % PAN_DEV)
        begun = None
        for n in range(3):
            begun = spread(PAN_DEV, *to[n], sources[n], before=begun)
        return sum_over_chips(PAN_DEV, to, begun, *receiver(PAN_DEV, count, everything))

    with jax.named_scope("sum_over_chips"):
        begun = spread(LISTED, *short[2], sources[2], before=begun, join=True)
        begun, sources[3] = tie((begun, sources[3]))
        fresh = lax.cond(too_long, send_all, lambda: sum_over_chips(LISTED, short, begun, *short_back))

    with jax.named_scope("place"):
        new_centroids, new_loads = place(me.reshape(1), exchange(fresh, "pts"))
    return new_centroids.reshape(CAND * PANEL, WIDTH), new_loads.reshape(CAND * PANEL)


def solution(mesh):
    placed = (P(("pts", "cent"), None), P("cent", None), P("cent"), P(("pts", "cent"), None), P())
    return jax.shard_map(
        local,
        mesh=mesh,
        in_specs=placed,
        out_specs=(P(("cent", "pts"), None), P(("cent", "pts"))),
        check_vma=False,
    )
```

```python
import functools

import jax
import jax.numpy as jnp
from jax import lax
from jax.experimental import pallas as pl
from jax.experimental.pallas import tpu as pltpu
from jax.sharding import PartitionSpec as P

PANEL = 128
GROUP = 1024
CAND = 4
GROUPS_DEV = 2
REQ = CAND * GROUPS_DEV
PAN_DEV = 64
WIDTH = 1024
N_CENT = 8
CHIPS = 4
N_PTS = 16
ROWS = 16
HALF = 512
LANE = 128
TILES = HALF // LANE
SEND_TILES = CAND * TILES + 1
DENSE = PAN_DEV * TILES
LOAD_TILES = PAN_DEV // ROWS
LISTED = 24

sharpness_divisor = 16.0
evenness_coefficient = 1.0
prior_mass = 1.0

BF16 = jnp.bfloat16
F32 = jnp.float32
MIB = 1 << 20
LOG2E = 1.4426950408889634


def params(mib):
    return pltpu.CompilerParams(vmem_limit_bytes=mib * MIB)


def whole(shape):
    return pl.BlockSpec(shape, lambda *_: (0,) * len(shape))


def smem_spec():
    return pl.BlockSpec(memory_space=pltpu.SMEM)


def vmem_spec():
    return pl.BlockSpec(memory_space=pltpu.VMEM)


def hbm_spec():
    return pl.BlockSpec(memory_space=pltpu.HBM)


def ask_kernel(candidates_in, home_in, loads_in, out, candidates, home, loads, sems):
    copies = [
        pltpu.make_async_copy(source, target, sems.at[n])
        for n, (source, target) in enumerate(((candidates_in, candidates), (home_in, home), (loads_in, loads)))
    ]
    for copy in copies:
        copy.start()
    for copy in copies:
        copy.wait()
    row = lax.broadcasted_iota(jnp.int32, (ROWS, LANE), 0)
    lane = lax.broadcasted_iota(jnp.int32, (ROWS, LANE), 1)
    slots = [home[candidates[n // CAND, n % CAND]] for n in range(REQ)]
    common = jnp.zeros((ROWS, LANE), F32)
    for n, slot in enumerate(slots):
        common = jnp.where((row == 1) & (lane == n), (slot // PAN_DEV).astype(F32), common)
        common = jnp.where((row == 2) & (lane == n), (slot % PAN_DEV).astype(F32), common)
    for o in range(N_CENT):
        tile = common
        for n, slot in enumerate(slots):
            here = jnp.where(slot // PAN_DEV == o, slot % PAN_DEV + 1, 0).astype(F32)
            tile = jnp.where((row == 0) & (lane == n // CAND), tile + here, tile)
        for t in range(LOAD_TILES):
            out[o, t] = loads[t * ROWS : (t + 1) * ROWS]
        out[o, LOAD_TILES] = tile.astype(BF16)


def ask(candidates, home, loads):
    return pl.pallas_call(
        ask_kernel,
        in_specs=[hbm_spec()] * 3,
        out_specs=vmem_spec(),
        out_shape=jax.ShapeDtypeStruct((N_CENT, LOAD_TILES + 1, ROWS, LANE), BF16),
        scratch_shapes=[
            pltpu.SMEM(candidates.shape, jnp.int32),
            pltpu.SMEM(home.shape, jnp.int32),
            pltpu.VMEM(loads.shape, BF16),
            pltpu.SemaphoreType.DMA((3,)),
        ],
        compiler_params=params(60),
        cost_estimate=pl.CostEstimate(flops=1 << 16, bytes_accessed=1 << 18, transcendentals=0),
    )(candidates, home, loads)


def pick_kernel(group, paired, ids, place, table, *refs):
    *outs, held, sems = refs

    def fetch(n, at):
        return pltpu.make_async_copy(table.at[ids[at]], held.at[n], sems.at[0, n])

    def put(n):
        target = outs[(n + 1) // 2].at[n and (n + 1) % 2] if paired else outs[n]
        return pltpu.make_async_copy(held.at[n], target, sems.at[1, n])

    def each(work):
        for n in range(N_CENT - 1):
            reader = n + 1
            at = (place[0] // 2 + reader // 2) % CHIPS * 2 + (place[0] + reader) % 2

            @pl.when(ids[at * GROUPS_DEV + group] >= 0)
            def _(n=n, at=at):
                work(n, at * GROUPS_DEV + group)

    def pass_on(n, at):
        fetch(n, at).wait()
        put(n).start()

    each(lambda n, at: fetch(n, at).start())
    each(pass_on)
    each(lambda n, at: put(n).wait())


def pick_panels(group, paired, ids, place, table):
    count = N_CENT - 1
    one = jax.ShapeDtypeStruct((PANEL, WIDTH), BF16)
    pair = jax.ShapeDtypeStruct((2, PANEL, WIDTH), BF16)
    out = [jax.ShapeDtypeStruct((1, PANEL, WIDTH), BF16), pair, pair, pair] if paired else [one] * count
    return pl.pallas_call(
        functools.partial(pick_kernel, group, paired),
        out_shape=out,
        in_specs=[smem_spec(), smem_spec(), hbm_spec()],
        out_specs=[hbm_spec()] * len(out),
        scratch_shapes=[pltpu.VMEM((count, PANEL, WIDTH), BF16), pltpu.SemaphoreType.DMA((2, count))],
        compiler_params=params(60),
        cost_estimate=pl.CostEstimate(flops=0, bytes_accessed=4 * count * PANEL * WIDTH, transcendentals=0),
    )(ids, place, table)


def score_kernel(group, owners, *refs):
    *panels, table, points, surcharge, out, members, centers, shares, sems = refs
    if len(panels) == CHIPS:
        panels = [panels[o // 2 - 1].at[0] if o % 2 == 0 else panels[-1].at[o // 2] for o in range(1, N_CENT)]
    step = 256
    steps = GROUP // step

    def land(j, source):
        rows = pl.ds(j * PANEL, PANEL)
        return pltpu.make_async_copy(source, centers.at[rows], sems.at[0, j])

    def bring(n):
        rows = pl.ds(n * step, step)
        return pltpu.make_async_copy(points.at[pl.ds(group * GROUP + n * step, step)], members.at[rows], sems.at[1, n])

    for j in range(CAND):

        @pl.when(owners[j] == 0)
        def _(j=j):
            land(j, table.at[owners[CAND + j]]).start()

        for o in range(1, N_CENT):

            @pl.when(owners[j] == o)
            def _(j=j, o=o):
                land(j, panels[o - 1]).start()

    for s in range(steps):
        bring(s).start()
    for j in range(CAND):
        land(j, panels[0]).wait()
    for s in range(steps):
        bring(s).wait()
    wide = centers[...].astype(F32)
    squares = jnp.sum(wide * wide, axis=1, keepdims=True)
    bias = (squares * (1.0 / sharpness_divisor) + evenness_coefficient * surcharge[group]) * LOG2E
    weights = jnp.zeros((CAND * PANEL, LANE), F32)
    for s in range(steps):
        block = members[s * step : (s + 1) * step, :]
        inner = lax.dot_general(centers[...], block, (((1,), (1,)), ((), ())), preferred_element_type=F32)
        logits = inner * (2.0 / sharpness_divisor * LOG2E) - bias
        highest = jnp.max(logits, axis=0, keepdims=True)
        raised = jnp.exp2(logits - highest)
        scale = 1.0 / jnp.sum(raised, axis=0, keepdims=True)
        share = (raised * scale).astype(BF16)
        shares[:, s * step : (s + 1) * step] = share
        rounded = share.astype(F32)
        for part in range(step // LANE):
            weights = weights + rounded[:, part * LANE : (part + 1) * LANE]
    weight = jnp.sum(weights, axis=1, keepdims=True)
    coarse = weight.astype(BF16).astype(F32)
    fine = weight - coarse
    lane = lax.broadcasted_iota(jnp.int32, (PANEL, LANE), 1)
    tile = jnp.zeros((PANEL, LANE), F32)
    for j in range(CAND):
        rows = slice(j * PANEL, (j + 1) * PANEL)
        tile = jnp.where(lane == j, coarse[rows], tile)
        tile = jnp.where(lane == CAND + j, fine[rows], tile)
    wide_step = 256
    for s in range(WIDTH // wide_step):
        part = lax.dot_general(
            shares[...], members[:, s * wide_step : (s + 1) * wide_step], (((1,), (0,)), ((), ())),
            preferred_element_type=F32,
        ).astype(BF16)
        for t in range(wide_step // LANE):
            half, tile_at = divmod(s * (wide_step // LANE) + t, TILES)
            for j in range(CAND):
                for block_at in range(PANEL // ROWS):
                    row = j * PANEL + block_at * ROWS
                    out[block_at * 2 + half, j * TILES + tile_at] = part[row : row + ROWS, t * LANE : (t + 1) * LANE]
    tile = tile.astype(BF16)
    for block_at in range(PANEL // ROWS):
        for half in range(2):
            out[block_at * 2 + half, CAND * TILES] = tile[block_at * ROWS : (block_at + 1) * ROWS]


def score(group, owners, panels, table, points, surcharge):
    return pl.pallas_call(
        functools.partial(score_kernel, group),
        in_specs=[smem_spec()] + [hbm_spec()] * (len(panels) + 2) + [vmem_spec()],
        out_specs=vmem_spec(),
        out_shape=jax.ShapeDtypeStruct((N_PTS, SEND_TILES, ROWS, LANE), BF16),
        scratch_shapes=[
            pltpu.VMEM((GROUP, WIDTH), BF16),
            pltpu.VMEM((CAND * PANEL, WIDTH), BF16),
            pltpu.VMEM((CAND * PANEL, GROUP), BF16),
            pltpu.SemaphoreType.DMA((2, 4)),
        ],
        compiler_params=params(50),
        cost_estimate=pl.CostEstimate(flops=2 << 30, bytes_accessed=5 * MIB, transcendentals=1 << 19),
    )(owners, *panels, table, points, surcharge)


def add_pieces(places, source, total):
    def add(s, carry):
        for j in range(CAND):
            at = places[s * CAND + j] * TILES
            total[pl.ds(at, TILES)] += source[s, j * TILES : (j + 1) * TILES].astype(F32)
        return carry

    lax.fori_loop(0, N_PTS, add, 0, unroll=2)


def sum_weights(lanes, source):
    panel = lax.broadcasted_iota(jnp.int32, (CHIPS * PAN_DEV, LANE), 0)
    weights = jnp.zeros((ROWS, CHIPS * PAN_DEV), F32)
    for n in range(N_PTS):
        chosen = jnp.where(panel == lanes[n : n + 1, :], 1.0, 0.0).astype(BF16)
        weights = weights + lax.dot_general(
            source[n, CAND * TILES], chosen, (((1,), (1,)), ((), ())), preferred_element_type=F32
        )
    return weights


def spread_first_kernel(places, source, lanes, total, total_weights):
    total[...] = jnp.zeros_like(total)
    add_pieces(places, source, total)
    total_weights[...] = sum_weights(lanes, source)


def spread_more_kernel(places, source, lanes, total_in, weights_in, total, total_weights):
    total[...] = total_in[...]
    add_pieces(places, source, total)
    total_weights[...] = weights_in[...] + sum_weights(lanes, source)


def spread_last_kernel(rows, places, source, lanes, total_in, weights_in, total, own, own_weights, out1, out2, out3):
    total[...] = total_in[...]
    add_pieces(places, source, total)
    weights = weights_in[...] + sum_weights(lanes, source)
    coarse = weights.astype(BF16)
    fine = (weights - coarse.astype(F32)).astype(BF16)
    own[...] = total[0:DENSE]
    own_weights[...] = weights[:, 0:LANE]
    for d, out in ((1, out1), (2, out2), (3, out3)):
        first = DENSE + (d - 1) * rows * TILES
        out[0 : rows * TILES] = total[first : first + rows * TILES].astype(BF16)
        out[rows * TILES, :, 0:PAN_DEV] = coarse[:, d * PAN_DEV : (d + 1) * PAN_DEV]
        out[rows * TILES, :, PAN_DEV:LANE] = fine[:, d * PAN_DEV : (d + 1) * PAN_DEV]


def spread(rows, places, lanes, source, before=None, last=False):
    totals = [
        jax.ShapeDtypeStruct(((PAN_DEV + 3 * rows + 1) * TILES, ROWS, LANE), F32),
        jax.ShapeDtypeStruct((ROWS, CHIPS * PAN_DEV), F32),
    ]
    if last:
        chunk = jax.ShapeDtypeStruct((rows * TILES + 1, ROWS, LANE), BF16)
        kernel = functools.partial(spread_last_kernel, rows)
        own = jax.ShapeDtypeStruct((DENSE, ROWS, LANE), F32)
        out = [totals[0], own, jax.ShapeDtypeStruct((ROWS, LANE), F32), chunk, chunk, chunk]
    else:
        kernel = spread_first_kernel if before is None else spread_more_kernel
        out = totals
    before = before or []
    return pl.pallas_call(
        kernel,
        in_specs=[smem_spec()] + [vmem_spec()] * (2 + len(before)),
        out_specs=[vmem_spec()] * len(out),
        out_shape=out,
        input_output_aliases={3: 0} if before else {},
        compiler_params=params(16),
        cost_estimate=pl.CostEstimate(flops=1 << 21, bytes_accessed=4 * MIB, transcendentals=0),
    )(places, source, lanes, *before)


def begin_kernel(me, own, table, out, old, sem):
    row = pl.multiple_of(me[0] // 2 * ROWS, ROWS)
    column = pl.multiple_of(me[0] % 2 * HALF, HALF)
    fetch = pltpu.make_async_copy(table.at[:, pl.ds(row, ROWS), pl.ds(column, HALF)], old, sem)
    fetch.start()
    fetch.wait()
    for q in range(PAN_DEV):
        for t in range(TILES):
            previous = old[q, :, t * LANE : (t + 1) * LANE].astype(F32)
            out[q * TILES + t] = own[q * TILES + t] + prior_mass * previous


def begin(me, own, table):
    return pl.pallas_call(
        begin_kernel,
        in_specs=[smem_spec(), vmem_spec(), hbm_spec()],
        out_specs=vmem_spec(),
        out_shape=jax.ShapeDtypeStruct((DENSE, ROWS, LANE), F32),
        scratch_shapes=[pltpu.VMEM((PAN_DEV, ROWS, HALF), BF16), pltpu.SemaphoreType.DMA],
        compiler_params=params(48),
        cost_estimate=pl.CostEstimate(flops=1 << 22, bytes_accessed=5 * MIB, transcendentals=0),
    )(me, own, table)


def take_lists(rows, numbers, weights, arrivals, lanes, total):
    panel = lax.broadcasted_iota(jnp.int32, (PAN_DEV, LANE), 0)
    for d, arrived in enumerate(arrivals):
        chosen = jnp.where(panel == lanes[d : d + 1, :], 1.0, 0.0).astype(BF16)
        weights = weights + lax.dot_general(
            arrived[rows * TILES], chosen, (((1,), (1,)), ((), ())), preferred_element_type=F32
        )
        first = 3 + d * rows

        def add(n, carry, arrived=arrived, first=first):
            at = numbers[first + n] * TILES
            total[pl.ds(at, TILES)] += arrived[pl.ds(n * TILES, TILES)].astype(F32)
            return carry

        lax.fori_loop(0, numbers[d], add, 0)
    return weights


def middle_kernel(rows, numbers, begun, weights0, weights1, own, in1, in2, in3, lanes, total, weights):
    total[...] = begun[...] + own[...]
    both = weights0[:, 0:PAN_DEV] + weights1[:, 0:PAN_DEV]
    weights[:, 0:PAN_DEV] = take_lists(rows, numbers, both, (in1, in2, in3), lanes, total)
    weights[:, PAN_DEV:LANE] = jnp.zeros((ROWS, LANE - PAN_DEV), F32)


def middle(rows, lists, begun, weights0, weights1, own, arrived):
    numbers, lanes = lists
    return pl.pallas_call(
        functools.partial(middle_kernel, rows),
        in_specs=[smem_spec()] + [vmem_spec()] * 8,
        out_specs=[vmem_spec(), vmem_spec()],
        out_shape=[jax.ShapeDtypeStruct(begun.shape, F32), jax.ShapeDtypeStruct((ROWS, LANE), F32)],
        input_output_aliases={1: 0},
        compiler_params=params(32),
        cost_estimate=pl.CostEstimate(flops=1 << 22, bytes_accessed=6 * MIB, transcendentals=0),
    )(numbers, begun, weights0, weights1, own, *arrived, lanes)


def finish_kernel(rows, numbers, begun, own_weights, in1, in2, in3, lanes, out, total):
    total[...] = begun[...]
    weights = take_lists(rows, numbers, own_weights[:, 0:PAN_DEV], (in1, in2, in3), lanes, total)
    inverse = 1.0 / (weights + prior_mass)
    for q in range(PAN_DEV):
        scale = jnp.broadcast_to(inverse[:, q : q + 1], (ROWS, LANE))
        for t in range(TILES):
            out[q // CAND, (q % CAND) * TILES + t] = (total[q * TILES + t] * scale).astype(BF16)
    coarse = weights.astype(BF16)
    fine = (weights - coarse.astype(F32)).astype(BF16)
    for p in range(N_PTS):
        out[p, CAND * TILES, :, 0:PAN_DEV] = coarse
        out[p, CAND * TILES, :, PAN_DEV:LANE] = fine


def finish(rows, numbers, begun, own_weights, arrived, lanes):
    return pl.pallas_call(
        functools.partial(finish_kernel, rows),
        in_specs=[smem_spec()] + [vmem_spec()] * 6,
        out_specs=[vmem_spec(), vmem_spec()],
        out_shape=[
            jax.ShapeDtypeStruct((N_PTS, CAND * TILES + 1, ROWS, LANE), BF16),
            jax.ShapeDtypeStruct(begun.shape, F32),
        ],
        input_output_aliases={1: 1},
        compiler_params=params(32),
        cost_estimate=pl.CostEstimate(flops=1 << 22, bytes_accessed=6 * MIB, transcendentals=0),
    )(numbers, begun, own_weights, *arrived, lanes)[0]


def place_kernel(me, pieces, out, loads):
    for block_at in range(PANEL // ROWS):
        for half in range(2):
            for q in range(CAND):
                for t in range(TILES):
                    column = half * HALF + t * LANE
                    out[q, block_at * ROWS : (block_at + 1) * ROWS, column : column + LANE] = pieces[
                        block_at * 2 + half, q * TILES + t
                    ]
    lane = lax.broadcasted_iota(jnp.int32, (ROWS, LANE), 1)
    row = lax.broadcasted_iota(jnp.int32, (ROWS, LANE), 0)
    wanted = me[0] * CAND + row
    chosen = jnp.where((row < CAND) & (lane % PAN_DEV == wanted), 1.0, 0.0).astype(BF16)
    for block_at in range(PANEL // ROWS):
        pair = pieces[block_at * 2, CAND * TILES]
        part = lax.dot_general(chosen, pair, (((1,), (1,)), ((), ())), preferred_element_type=F32)
        loads[:, block_at * ROWS : (block_at + 1) * ROWS] = part[0:CAND]


def place(me, pieces):
    return pl.pallas_call(
        place_kernel,
        grid=(1,),
        in_specs=[smem_spec(), whole(pieces.shape)],
        out_specs=[whole((CAND, PANEL, WIDTH)), whole((CAND, PANEL))],
        out_shape=[
            jax.ShapeDtypeStruct((CAND, PANEL, WIDTH), BF16),
            jax.ShapeDtypeStruct((CAND, PANEL), F32),
        ],
        compiler_params=params(32),
        cost_estimate=pl.CostEstimate(flops=1 << 20, bytes_accessed=2 * MIB, transcendentals=0),
    )(me, pieces)


def shift(dy, dk):
    return [(y * 2 + k, ((y + dy) % CHIPS) * 2 + (k + dk) % 2) for y in range(CHIPS) for k in range(2)]


def exchange(x, axis):
    return lax.all_to_all(x, axis, split_axis=0, concat_axis=0, tiled=True)


def local(points, centroids, prev_loads, candidates, panel_home):
    me = lax.axis_index("pts")
    here = lax.axis_index("cent")
    chip, core = here // 2, here % 2
    shelf = centroids.reshape(PAN_DEV, PANEL, WIDTH)

    with jax.named_scope("requests"):
        answered = exchange(ask(candidates, panel_home, prev_loads.reshape(PAN_DEV, PANEL)), "cent")
        asked = answered[:, LOAD_TILES, 0, 0:GROUPS_DEV].astype(jnp.int32).reshape(-1) - 1

    tie = lax.optimization_barrier
    with jax.named_scope("gather_panels"):
        arrived = []
        for g in range(GROUPS_DEV):
            ready = pick_panels(g, g == 1, asked, here.reshape(1), shelf)
            if g == 0:
                arrived.append([lax.ppermute(x, "cent", shift((n + 1) // 2, (n + 1) % 2)) for n, x in enumerate(ready)])
            else:
                direct = [lax.ppermute(ready[d], "cent", shift(d, 0)) for d in range(1, CHIPS)]
                passed = jnp.concatenate([ready[0]] + [x[1:2] for x in direct])
                arrived.append(direct + [lax.ppermute(passed, "cent", shift(0, 1))])
            if g == 0:
                answered, arrived[g][0] = tie((answered, arrived[g][0]))
                asked, arrived[g][1] = tie((asked, arrived[g][1]))

    with jax.named_scope("own_requests"):
        slots = jnp.sum(
            jnp.where(candidates.reshape(REQ)[:, None] == jnp.arange(panel_home.shape[0], dtype=jnp.int32), panel_home[None, :], 0),
            axis=1,
        )
        owners = slots // PAN_DEV
        seen = (chip - owners // 2) % CHIPS * 2 + (core - owners) % 2
        seen = jnp.stack([seen.reshape(GROUPS_DEV, CAND), (slots % PAN_DEV).reshape(GROUPS_DEV, CAND)], axis=1)
        seen = [seen[g].reshape(-1) for g in range(GROUPS_DEV)]

    with jax.named_scope("all_requests"):
        ring = answered[:, LOAD_TILES, 1:3, 0:REQ].astype(jnp.int32)
        ring = ring[:, 0] * PAN_DEV + ring[:, 1]
        everyone = exchange(jnp.broadcast_to(ring[None, :, :, None], (N_PTS, N_CENT, REQ, 128)), "pts")[..., 0]

        numbers = jnp.arange(N_CENT * PAN_DEV, dtype=jnp.int32)
        by_chip = jnp.transpose(everyone.reshape(N_PTS, CHIPS, 2, GROUPS_DEV, CAND), (3, 1, 0, 2, 4))
        by_chip = by_chip.reshape(GROUPS_DEV, CHIPS, -1)
        asked_by = jnp.any(by_chip[..., None] == numbers, axis=2).reshape(GROUPS_DEV, CHIPS, N_CENT, PAN_DEV)
        below = jnp.arange(PAN_DEV)[:, None] < jnp.arange(PAN_DEV)[None, :]
        ranks = lax.dot_general(
            asked_by.astype(BF16), below.astype(BF16), (((3,), (0,)), ((), ())), preferred_element_type=F32
        ).astype(jnp.int32)
        lengths = jnp.sum(asked_by.astype(jnp.int32), axis=3)
        off_chip = jnp.arange(N_CENT)[None, :] // 2 != jnp.arange(CHIPS)[:, None]
        too_long = jnp.any(off_chip & (lengths > LISTED))

        pair = jnp.stack(
            [lax.dynamic_index_in_dim(everyone, at, 1, keepdims=False) for at in (here, chip * 2 + 1 - core)]
        )
        pair = jnp.transpose(pair.reshape(2, N_PTS, GROUPS_DEV, CAND), (2, 0, 1, 3))
        owner = pair // PAN_DEV
        relative = (owner // 2 - chip) % CHIPS
        my_ranks = lax.dynamic_index_in_dim(ranks, chip, 1, keepdims=False).reshape(GROUPS_DEV, 1, 1, 1, -1)
        rank = jnp.sum(jnp.where(pair[..., None] == numbers, my_ranks, 0), axis=4)
        ours = owner % 2 == core

        def sender(rows, rank):
            at = jnp.where(relative == 0, pair % PAN_DEV, rank)
            known = ours & ((relative == 0) | (rank < rows))
            first = jnp.where(relative == 0, 0, PAN_DEV + (relative - 1) * rows)
            places = jnp.where(known, first + at, PAN_DEV + 3 * rows)
            lane = jnp.where(known, relative * PAN_DEV + at, CHIPS * PAN_DEV)
            lanes = jnp.pad(
                jnp.concatenate([lane, lane], axis=3), ((0, 0), (0, 0), (0, 0), (0, LANE - 2 * CAND)),
                constant_values=CHIPS * PAN_DEV,
            )
            return [
                (places[g, n].reshape(-1), lanes[g, n]) for g in range(GROUPS_DEV) for n in range(2)
            ]

        def receiver(rows, count, panels):
            numbers = jnp.concatenate([count, panels[:, :rows].reshape(-1)])
            lane = jnp.where(jnp.arange(PAN_DEV) < jnp.minimum(count, rows)[:, None], panels, PAN_DEV)
            return numbers, jnp.concatenate([lane, lane], axis=1)

        behind = [(chip - d) % CHIPS for d in range(1, CHIPS)]
        pick = lambda x, y: lax.dynamic_index_in_dim(lax.dynamic_index_in_dim(x, y, 0, False), here, 0, False)
        named = jnp.stack([pick(asked_by[g], y) for g in range(GROUPS_DEV) for y in behind])
        order = jnp.stack([pick(ranks[g], y) for g in range(GROUPS_DEV) for y in behind])
        spots = jnp.arange(PAN_DEV, dtype=jnp.int32)
        listed = jnp.sum(
            jnp.where(named[:, None, :] & (order[:, None, :] == spots[None, :, None]), spots, 0), axis=2
        )
        count = jnp.minimum(jnp.sum(named.astype(jnp.int32), axis=1), LISTED)
        short = sender(LISTED, rank)
        short_back = [
            receiver(LISTED, count[3 * g : 3 * g + 3], listed[3 * g : 3 * g + 3]) for g in range(GROUPS_DEV)
        ]
        seen[1], too_long, short, short_back = tie((seen[1], too_long, short, short_back))

    with jax.named_scope("loads"):
        load_table = answered[:, :LOAD_TILES].reshape(N_CENT * PAN_DEV, PANEL)
        loads = jnp.take(load_table, slots, axis=0, mode="clip").astype(F32)
        surcharge = jnp.log(loads).reshape(GROUPS_DEV, CAND * PANEL, 1)

    where = me.reshape(1)

    def to_owners(far):
        return [lax.ppermute(far[d - 1], "cent", shift(d, 0)) for d in range(1, CHIPS)]

    def swap(x):
        return lax.ppermute(x, "cent", shift(0, 1))

    with jax.named_scope("group_0"):
        pieces = score(0, seen[0], arrived[0], shelf, points, surcharge)
        mine0 = exchange(pieces, "pts")
    with jax.named_scope("group_1"):
        pieces = score(1, seen[1], arrived[1], shelf, points, surcharge)
        mine0, pieces = tie((mine0, pieces))
        mine1 = exchange(pieces, "pts")
    with jax.named_scope("sums_0"):
        mate0 = swap(mine0)
        begun = spread(LISTED, *short[0], mine0)
        unused, own0, weights0, *far = spread(LISTED, *short[1], mate0, before=begun, last=True)
        back0 = to_owners(far)
        begun = begin(where, own0, shelf)
        mine1, back0, begun = tie((mine1, back0, begun))
    with jax.named_scope("sums_1"):
        mate1 = swap(mine1)
        own1 = spread(LISTED, *short[2], mine1)
        unused, own1, weights1, *far = spread(LISTED, *short[3], mate1, before=own1, last=True)
        back1 = to_owners(far)
        begun, weights = middle(LISTED, short_back[0], begun, weights0, weights1, own1, back0)
        begun, weights, back1, mate1 = tie((begun, weights, back1, mate1))

    def from_lists():
        return finish(LISTED, short_back[1][0], begun, weights, back1, short_back[1][1])

    def from_all():
        everything = jnp.broadcast_to(spots, (CHIPS - 1, PAN_DEV))
        numbers, back_lanes = receiver(PAN_DEV, jnp.full((CHIPS - 1,), PAN_DEV, jnp.int32), everything)
        total = None
        for n, (to, source) in enumerate(zip(sender(PAN_DEV, pair % PAN_DEV), (mine0, mate0, mine1, mate1))):
            total = spread(PAN_DEV, *to, source, before=total, last=n == 3)
        unused, own, own_weights, *far = total
        return finish(PAN_DEV, numbers, begin(where, own, shelf), own_weights, to_owners(far), back_lanes)

    with jax.named_scope("finish"):
        fresh = lax.cond(too_long, from_all, from_lists)

    with jax.named_scope("place"):
        new_centroids, new_loads = place(where, exchange(fresh, "pts"))
    return new_centroids.reshape(CAND * PANEL, WIDTH), new_loads.reshape(CAND * PANEL)


def solution(mesh):
    placed = (P(("pts", "cent"), None), P("cent", None), P("cent"), P(("pts", "cent"), None), P())
    return jax.shard_map(
        local,
        mesh=mesh,
        in_specs=placed,
        out_specs=(P(("cent", "pts"), None), P(("cent", "pts"))),
        check_vma=False,
    )
```

```python
import functools

import jax
import jax.numpy as jnp
from jax import lax
from jax.experimental import pallas as pl
from jax.experimental.pallas import tpu as pltpu
from jax.sharding import PartitionSpec as P

PANEL = 128
GROUP = 1024
CAND = 4
GROUPS_DEV = 2
REQ = CAND * GROUPS_DEV
PAN_DEV = 64
WIDTH = 1024
N_CENT = 8
CHIPS = 4
N_PTS = 16
ROWS = 16
HALF = 512
LANE = 128
TILES = HALF // LANE
SEND_TILES = CAND * TILES + 1
DENSE = PAN_DEV * TILES
LOAD_TILES = PAN_DEV // ROWS
LISTED = 34

sharpness_divisor = 16.0
evenness_coefficient = 1.0
prior_mass = 1.0

BF16 = jnp.bfloat16
F32 = jnp.float32
MIB = 1 << 20
LOG2E = 1.4426950408889634


def params(mib):
    return pltpu.CompilerParams(vmem_limit_bytes=mib * MIB)


def whole(shape):
    return pl.BlockSpec(shape, lambda *_: (0,) * len(shape))


def smem_spec():
    return pl.BlockSpec(memory_space=pltpu.SMEM)


def vmem_spec():
    return pl.BlockSpec(memory_space=pltpu.VMEM)


def hbm_spec():
    return pl.BlockSpec(memory_space=pltpu.HBM)


def ask_kernel(candidates_in, home_in, loads_in, out, candidates, home, loads, sems):
    copies = [
        pltpu.make_async_copy(source, target, sems.at[n])
        for n, (source, target) in enumerate(((candidates_in, candidates), (home_in, home), (loads_in, loads)))
    ]
    for copy in copies:
        copy.start()
    for copy in copies:
        copy.wait()
    row = lax.broadcasted_iota(jnp.int32, (ROWS, LANE), 0)
    lane = lax.broadcasted_iota(jnp.int32, (ROWS, LANE), 1)
    slots = [home[candidates[n // CAND, n % CAND]] for n in range(REQ)]
    common = jnp.zeros((ROWS, LANE), F32)
    for n, slot in enumerate(slots):
        common = jnp.where((row == 1) & (lane == n), (slot // PAN_DEV).astype(F32), common)
        common = jnp.where((row == 2) & (lane == n), (slot % PAN_DEV).astype(F32), common)
    for o in range(N_CENT):
        tile = common
        for n, slot in enumerate(slots):
            here = jnp.where(slot // PAN_DEV == o, slot % PAN_DEV + 1, 0).astype(F32)
            tile = jnp.where((row == 0) & (lane == n // CAND), tile + here, tile)
        for t in range(LOAD_TILES):
            out[o, t] = loads[t * ROWS : (t + 1) * ROWS]
        out[o, LOAD_TILES] = tile.astype(BF16)


def ask(candidates, home, loads):
    return pl.pallas_call(
        ask_kernel,
        in_specs=[hbm_spec()] * 3,
        out_specs=vmem_spec(),
        out_shape=jax.ShapeDtypeStruct((N_CENT, LOAD_TILES + 1, ROWS, LANE), BF16),
        scratch_shapes=[
            pltpu.SMEM(candidates.shape, jnp.int32),
            pltpu.SMEM(home.shape, jnp.int32),
            pltpu.VMEM(loads.shape, BF16),
            pltpu.SemaphoreType.DMA((3,)),
        ],
        compiler_params=params(60),
        cost_estimate=pl.CostEstimate(flops=1 << 16, bytes_accessed=1 << 18, transcendentals=0),
    )(candidates, home, loads)


def pick_kernel(group, paired, ids, place, table, *refs):
    *outs, held, sems = refs

    def fetch(n, at):
        return pltpu.make_async_copy(table.at[ids[at]], held.at[n], sems.at[0, n])

    def put(n):
        target = outs[(n + 1) // 2].at[n and (n + 1) % 2] if paired else outs[n]
        return pltpu.make_async_copy(held.at[n], target, sems.at[1, n])

    def each(work):
        for n in range(N_CENT - 1):
            reader = n + 1
            at = (place[0] // 2 + reader // 2) % CHIPS * 2 + (place[0] + reader) % 2

            @pl.when(ids[at * GROUPS_DEV + group] >= 0)
            def _(n=n, at=at):
                work(n, at * GROUPS_DEV + group)

    def pass_on(n, at):
        fetch(n, at).wait()
        put(n).start()

    each(lambda n, at: fetch(n, at).start())
    each(pass_on)
    each(lambda n, at: put(n).wait())


def pick_panels(group, paired, ids, place, table):
    count = N_CENT - 1
    one = jax.ShapeDtypeStruct((PANEL, WIDTH), BF16)
    pair = jax.ShapeDtypeStruct((2, PANEL, WIDTH), BF16)
    out = [jax.ShapeDtypeStruct((1, PANEL, WIDTH), BF16), pair, pair, pair] if paired else [one] * count
    return pl.pallas_call(
        functools.partial(pick_kernel, group, paired),
        out_shape=out,
        in_specs=[smem_spec(), smem_spec(), hbm_spec()],
        out_specs=[hbm_spec()] * len(out),
        scratch_shapes=[pltpu.VMEM((count, PANEL, WIDTH), BF16), pltpu.SemaphoreType.DMA((2, count))],
        compiler_params=params(60),
        cost_estimate=pl.CostEstimate(flops=0, bytes_accessed=4 * count * PANEL * WIDTH, transcendentals=0),
    )(ids, place, table)


def score_kernel(group, owners, *refs):
    *panels, table, points, surcharge, out, members, centers, shares, sems = refs
    if len(panels) == CHIPS:
        panels = [panels[o // 2 - 1].at[0] if o % 2 == 0 else panels[-1].at[o // 2] for o in range(1, N_CENT)]
    step = 256
    steps = GROUP // step

    def land(j, source):
        rows = pl.ds(j * PANEL, PANEL)
        return pltpu.make_async_copy(source, centers.at[rows], sems.at[0, j])

    def bring(n):
        rows = pl.ds(n * step, step)
        return pltpu.make_async_copy(points.at[pl.ds(group * GROUP + n * step, step)], members.at[rows], sems.at[1, n])

    for j in range(CAND):

        @pl.when(owners[j] == 0)
        def _(j=j):
            land(j, table.at[owners[CAND + j]]).start()

        for o in range(1, N_CENT):

            @pl.when(owners[j] == o)
            def _(j=j, o=o):
                land(j, panels[o - 1]).start()

    for s in range(steps):
        bring(s).start()
    for j in range(CAND):
        land(j, panels[0]).wait()
    for s in range(steps):
        bring(s).wait()
    wide = centers[...].astype(F32)
    squares = jnp.sum(wide * wide, axis=1, keepdims=True)
    bias = (squares * (1.0 / sharpness_divisor) + evenness_coefficient * surcharge[group]) * LOG2E
    weights = jnp.zeros((CAND * PANEL, LANE), F32)
    for s in range(steps):
        block = members[s * step : (s + 1) * step, :]
        inner = lax.dot_general(centers[...], block, (((1,), (1,)), ((), ())), preferred_element_type=F32)
        logits = inner * (2.0 / sharpness_divisor * LOG2E) - bias
        highest = jnp.max(logits, axis=0, keepdims=True)
        raised = jnp.exp2(logits - highest)
        scale = 1.0 / jnp.sum(raised, axis=0, keepdims=True)
        share = (raised * scale).astype(BF16)
        shares[:, s * step : (s + 1) * step] = share
        rounded = share.astype(F32)
        for part in range(step // LANE):
            weights = weights + rounded[:, part * LANE : (part + 1) * LANE]
    weight = jnp.sum(weights, axis=1, keepdims=True)
    coarse = weight.astype(BF16).astype(F32)
    fine = weight - coarse
    lane = lax.broadcasted_iota(jnp.int32, (PANEL, LANE), 1)
    tile = jnp.zeros((PANEL, LANE), F32)
    for j in range(CAND):
        rows = slice(j * PANEL, (j + 1) * PANEL)
        tile = jnp.where(lane == j, coarse[rows], tile)
        tile = jnp.where(lane == CAND + j, fine[rows], tile)
    wide_step = 256
    for s in range(WIDTH // wide_step):
        part = lax.dot_general(
            shares[...], members[:, s * wide_step : (s + 1) * wide_step], (((1,), (0,)), ((), ())),
            preferred_element_type=F32,
        ).astype(BF16)
        for t in range(wide_step // LANE):
            half, tile_at = divmod(s * (wide_step // LANE) + t, TILES)
            for j in range(CAND):
                for block_at in range(PANEL // ROWS):
                    row = j * PANEL + block_at * ROWS
                    out[block_at * 2 + half, j * TILES + tile_at] = part[row : row + ROWS, t * LANE : (t + 1) * LANE]
    tile = tile.astype(BF16)
    for block_at in range(PANEL // ROWS):
        for half in range(2):
            out[block_at * 2 + half, CAND * TILES] = tile[block_at * ROWS : (block_at + 1) * ROWS]


def score(group, owners, panels, table, points, surcharge):
    return pl.pallas_call(
        functools.partial(score_kernel, group),
        in_specs=[smem_spec()] + [hbm_spec()] * (len(panels) + 2) + [vmem_spec()],
        out_specs=vmem_spec(),
        out_shape=jax.ShapeDtypeStruct((N_PTS, SEND_TILES, ROWS, LANE), BF16),
        scratch_shapes=[
            pltpu.VMEM((GROUP, WIDTH), BF16),
            pltpu.VMEM((CAND * PANEL, WIDTH), BF16),
            pltpu.VMEM((CAND * PANEL, GROUP), BF16),
            pltpu.SemaphoreType.DMA((2, 4)),
        ],
        compiler_params=params(50),
        cost_estimate=pl.CostEstimate(flops=2 << 30, bytes_accessed=5 * MIB, transcendentals=1 << 19),
    )(owners, *panels, table, points, surcharge)


def add_pieces(places, source, total):
    def add(s, carry):
        for j in range(CAND):
            at = places[s * CAND + j] * TILES
            total[pl.ds(at, TILES)] += source[s, j * TILES : (j + 1) * TILES].astype(F32)
        return carry

    lax.fori_loop(0, N_PTS, add, 0, unroll=2)


def sum_weights(lanes, source):
    panel = lax.broadcasted_iota(jnp.int32, (CHIPS * PAN_DEV, LANE), 0)
    weights = jnp.zeros((ROWS, CHIPS * PAN_DEV), F32)
    for n in range(N_PTS):
        chosen = jnp.where(panel == lanes[n : n + 1, :], 1.0, 0.0).astype(BF16)
        weights = weights + lax.dot_general(
            source[n, CAND * TILES], chosen, (((1,), (1,)), ((), ())), preferred_element_type=F32
        )
    return weights


def spread_first_kernel(places, source, lanes, total, total_weights):
    total[...] = jnp.zeros_like(total)
    add_pieces(places, source, total)
    total_weights[...] = sum_weights(lanes, source)


def spread_more_kernel(places, source, lanes, total_in, weights_in, total, total_weights):
    total[...] = total_in[...]
    add_pieces(places, source, total)
    total_weights[...] = weights_in[...] + sum_weights(lanes, source)


def spread_join_kernel(places, source, lanes, total_in, weights_in, total, total_weights):
    total[...] = total_in[...]
    total_weights[...] = weights_in[...] + sum_weights(lanes, source)
    add_pieces(places, source, total)


def spread_last_kernel(rows, places, source, lanes, total_in, weights_in, total, own_weights, out1, out2, out3):
    total[...] = total_in[...]
    add_pieces(places, source, total)
    weights = weights_in[...] + sum_weights(lanes, source)
    coarse = weights.astype(BF16)
    fine = (weights - coarse.astype(F32)).astype(BF16)
    own_weights[...] = weights[:, 0:LANE]
    for d, out in ((1, out1), (2, out2), (3, out3)):
        first = DENSE + (d - 1) * rows * TILES
        out[0 : rows * TILES] = total[first : first + rows * TILES].astype(BF16)
        out[rows * TILES, :, 0:PAN_DEV] = coarse[:, d * PAN_DEV : (d + 1) * PAN_DEV]
        out[rows * TILES, :, PAN_DEV:LANE] = fine[:, d * PAN_DEV : (d + 1) * PAN_DEV]


def spread(rows, places, lanes, source, before=None, last=False, join=False):
    totals = [
        jax.ShapeDtypeStruct(((PAN_DEV + 3 * rows + 1) * TILES, ROWS, LANE), F32),
        jax.ShapeDtypeStruct((ROWS, CHIPS * PAN_DEV), F32),
    ]
    if last:
        chunk = jax.ShapeDtypeStruct((rows * TILES + 1, ROWS, LANE), BF16)
        kernel = functools.partial(spread_last_kernel, rows)
        out = [totals[0], jax.ShapeDtypeStruct((ROWS, LANE), F32), chunk, chunk, chunk]
    else:
        kernel = spread_join_kernel if join else spread_first_kernel if before is None else spread_more_kernel
        out = totals
    before = before or []
    return pl.pallas_call(
        kernel,
        in_specs=[smem_spec()] + [vmem_spec()] * (2 + len(before)),
        out_specs=[vmem_spec()] * len(out),
        out_shape=out,
        input_output_aliases={3: 0} if before and not join else {},
        compiler_params=params(16),
        cost_estimate=pl.CostEstimate(flops=1 << 21, bytes_accessed=4 * MIB, transcendentals=0),
    )(places, source, lanes, *before)


def begin_kernel(me, own, table, out, old, sem):
    row = pl.multiple_of(me[0] // 2 * ROWS, ROWS)
    column = pl.multiple_of(me[0] % 2 * HALF, HALF)
    fetch = pltpu.make_async_copy(table.at[:, pl.ds(row, ROWS), pl.ds(column, HALF)], old, sem)
    fetch.start()
    fetch.wait()
    for q in range(PAN_DEV):
        for t in range(TILES):
            previous = old[q, :, t * LANE : (t + 1) * LANE].astype(F32)
            out[q * TILES + t] = own[q * TILES + t] + prior_mass * previous


def begin(me, own, table):
    return pl.pallas_call(
        begin_kernel,
        in_specs=[smem_spec(), vmem_spec(), hbm_spec()],
        out_specs=vmem_spec(),
        out_shape=jax.ShapeDtypeStruct((DENSE, ROWS, LANE), F32),
        scratch_shapes=[pltpu.VMEM((PAN_DEV, ROWS, HALF), BF16), pltpu.SemaphoreType.DMA],
        compiler_params=params(48),
        cost_estimate=pl.CostEstimate(flops=1 << 22, bytes_accessed=5 * MIB, transcendentals=0),
    )(me, own, table)


def finish_kernel(rows, numbers, begun, own_weights, in1, in2, in3, lanes, out, total):
    total[...] = begun[...]
    weights = own_weights[:, 0:PAN_DEV]
    panel = lax.broadcasted_iota(jnp.int32, (PAN_DEV, LANE), 0)
    for d, arrived in enumerate((in1, in2, in3)):
        chosen = jnp.where(panel == lanes[d : d + 1, :], 1.0, 0.0).astype(BF16)
        weights = weights + lax.dot_general(
            arrived[rows * TILES], chosen, (((1,), (1,)), ((), ())), preferred_element_type=F32
        )
        first = 3 + d * rows

        def add(n, carry, arrived=arrived, first=first):
            at = numbers[first + n] * TILES
            total[pl.ds(at, TILES)] += arrived[pl.ds(n * TILES, TILES)].astype(F32)
            return carry

        lax.fori_loop(0, numbers[d], add, 0)
    inverse = 1.0 / (weights + prior_mass)
    for q in range(PAN_DEV):
        scale = jnp.broadcast_to(inverse[:, q : q + 1], (ROWS, LANE))
        for t in range(TILES):
            out[q // CAND, (q % CAND) * TILES + t] = (total[q * TILES + t] * scale).astype(BF16)
    coarse = weights.astype(BF16)
    fine = (weights - coarse.astype(F32)).astype(BF16)
    for p in range(N_PTS):
        out[p, CAND * TILES, :, 0:PAN_DEV] = coarse
        out[p, CAND * TILES, :, PAN_DEV:LANE] = fine


def finish(rows, numbers, begun, own_weights, arrived, lanes):
    return pl.pallas_call(
        functools.partial(finish_kernel, rows),
        in_specs=[smem_spec()] + [vmem_spec()] * 6,
        out_specs=[vmem_spec(), vmem_spec()],
        out_shape=[
            jax.ShapeDtypeStruct((N_PTS, CAND * TILES + 1, ROWS, LANE), BF16),
            jax.ShapeDtypeStruct(begun.shape, F32),
        ],
        input_output_aliases={1: 1},
        compiler_params=params(32),
        cost_estimate=pl.CostEstimate(flops=1 << 22, bytes_accessed=6 * MIB, transcendentals=0),
    )(numbers, begun, own_weights, *arrived, lanes)[0]


def place_kernel(me, pieces, out, loads):
    for block_at in range(PANEL // ROWS):
        for half in range(2):
            for q in range(CAND):
                for t in range(TILES):
                    column = half * HALF + t * LANE
                    out[q, block_at * ROWS : (block_at + 1) * ROWS, column : column + LANE] = pieces[
                        block_at * 2 + half, q * TILES + t
                    ]
    lane = lax.broadcasted_iota(jnp.int32, (ROWS, LANE), 1)
    row = lax.broadcasted_iota(jnp.int32, (ROWS, LANE), 0)
    wanted = me[0] * CAND + row
    chosen = jnp.where((row < CAND) & (lane % PAN_DEV == wanted), 1.0, 0.0).astype(BF16)
    for block_at in range(PANEL // ROWS):
        pair = pieces[block_at * 2, CAND * TILES]
        part = lax.dot_general(chosen, pair, (((1,), (1,)), ((), ())), preferred_element_type=F32)
        loads[:, block_at * ROWS : (block_at + 1) * ROWS] = part[0:CAND]


def place(me, pieces):
    return pl.pallas_call(
        place_kernel,
        grid=(1,),
        in_specs=[smem_spec(), whole(pieces.shape)],
        out_specs=[whole((CAND, PANEL, WIDTH)), whole((CAND, PANEL))],
        out_shape=[
            jax.ShapeDtypeStruct((CAND, PANEL, WIDTH), BF16),
            jax.ShapeDtypeStruct((CAND, PANEL), F32),
        ],
        compiler_params=params(32),
        cost_estimate=pl.CostEstimate(flops=1 << 20, bytes_accessed=2 * MIB, transcendentals=0),
    )(me, pieces)


def shift(dy, dk):
    return [(y * 2 + k, ((y + dy) % CHIPS) * 2 + (k + dk) % 2) for y in range(CHIPS) for k in range(2)]


def exchange(x, axis):
    return lax.all_to_all(x, axis, split_axis=0, concat_axis=0, tiled=True)


def local(points, centroids, prev_loads, candidates, panel_home):
    me = lax.axis_index("pts")
    here = lax.axis_index("cent")
    chip, core = here // 2, here % 2
    shelf = centroids.reshape(PAN_DEV, PANEL, WIDTH)

    with jax.named_scope("requests"):
        answered = exchange(ask(candidates, panel_home, prev_loads.reshape(PAN_DEV, PANEL)), "cent")
        asked = answered[:, LOAD_TILES, 0, 0:GROUPS_DEV].astype(jnp.int32).reshape(-1) - 1

    tie = lax.optimization_barrier
    with jax.named_scope("gather_panels"):
        arrived = []
        for g in range(GROUPS_DEV):
            ready = pick_panels(g, g == 1, asked, here.reshape(1), shelf)
            if g == 0:
                arrived.append([lax.ppermute(x, "cent", shift((n + 1) // 2, (n + 1) % 2)) for n, x in enumerate(ready)])
            else:
                direct = [lax.ppermute(ready[d], "cent", shift(d, 0)) for d in range(1, CHIPS)]
                passed = jnp.concatenate([ready[0]] + [x[1:2] for x in direct])
                arrived.append(direct + [lax.ppermute(passed, "cent", shift(0, 1))])
            if g == 0:
                answered, arrived[g][0] = tie((answered, arrived[g][0]))
                asked, arrived[g][1] = tie((asked, arrived[g][1]))

    with jax.named_scope("own_requests"):
        slots = jnp.sum(
            jnp.where(candidates.reshape(REQ)[:, None] == jnp.arange(panel_home.shape[0], dtype=jnp.int32), panel_home[None, :], 0),
            axis=1,
        )
        owners = slots // PAN_DEV
        seen = (chip - owners // 2) % CHIPS * 2 + (core - owners) % 2
        seen = jnp.stack([seen.reshape(GROUPS_DEV, CAND), (slots % PAN_DEV).reshape(GROUPS_DEV, CAND)], axis=1)
        seen = [seen[g].reshape(-1) for g in range(GROUPS_DEV)]

    with jax.named_scope("all_requests"):
        ring = answered[:, LOAD_TILES, 1:3, 0:REQ].astype(jnp.int32)
        ring = ring[:, 0] * PAN_DEV + ring[:, 1]
        everyone = exchange(jnp.broadcast_to(ring[None, :, :, None], (N_PTS, N_CENT, REQ, 128)), "pts")[..., 0]

        numbers = jnp.arange(N_CENT * PAN_DEV, dtype=jnp.int32)
        by_chip = jnp.transpose(everyone.reshape(N_PTS, CHIPS, 2 * REQ), (1, 0, 2)).reshape(CHIPS, -1)
        asked_by = jnp.any(by_chip[:, :, None] == numbers, axis=1).reshape(CHIPS, N_CENT, PAN_DEV)
        below = jnp.arange(PAN_DEV)[:, None] < jnp.arange(PAN_DEV)[None, :]
        ranks = lax.dot_general(
            asked_by.astype(BF16), below.astype(BF16), (((2,), (0,)), ((), ())), preferred_element_type=F32
        ).astype(jnp.int32)
        lengths = jnp.sum(asked_by.astype(jnp.int32), axis=2)
        off_chip = jnp.arange(N_CENT)[None, :] // 2 != jnp.arange(CHIPS)[:, None]
        too_long = jnp.any(off_chip & (lengths > LISTED))

        pair = jnp.stack(
            [lax.dynamic_index_in_dim(everyone, at, 1, keepdims=False) for at in (here, chip * 2 + 1 - core)]
        )
        pair = jnp.transpose(pair.reshape(2, N_PTS, GROUPS_DEV, CAND), (2, 0, 1, 3))
        owner = pair // PAN_DEV
        relative = (owner // 2 - chip) % CHIPS
        my_ranks = lax.dynamic_index_in_dim(ranks, chip, 0, keepdims=False).reshape(-1)
        rank = jnp.sum(jnp.where(pair[..., None] == numbers, my_ranks, 0), axis=4)
        ours = owner % 2 == core

        def sender(rows, rank):
            at = jnp.where(relative == 0, pair % PAN_DEV, rank)
            known = ours & ((relative == 0) | (rank < rows))
            first = jnp.where(relative == 0, 0, PAN_DEV + (relative - 1) * rows)
            places = jnp.where(known, first + at, PAN_DEV + 3 * rows)
            lane = jnp.where(known, relative * PAN_DEV + at, CHIPS * PAN_DEV)
            lanes = jnp.pad(
                jnp.concatenate([lane, lane], axis=3), ((0, 0), (0, 0), (0, 0), (0, LANE - 2 * CAND)),
                constant_values=CHIPS * PAN_DEV,
            )
            return [
                (places[g, n].reshape(-1), lanes[g, n]) for g in range(GROUPS_DEV) for n in range(2)
            ]

        def receiver(rows, count, panels):
            numbers = jnp.concatenate([count, panels[:, :rows].reshape(-1)])
            lane = jnp.where(jnp.arange(PAN_DEV) < jnp.minimum(count, rows)[:, None], panels, PAN_DEV)
            return numbers, jnp.concatenate([lane, lane], axis=1)

        behind = [(chip - d) % CHIPS for d in range(1, CHIPS)]
        pick = lambda x, y: lax.dynamic_index_in_dim(lax.dynamic_index_in_dim(x, y, 0, False), here, 0, False)
        named = jnp.stack([pick(asked_by, y) for y in behind])
        order = jnp.stack([pick(ranks, y) for y in behind])
        spots = jnp.arange(PAN_DEV, dtype=jnp.int32)
        listed = jnp.sum(
            jnp.where(named[:, None, :] & (order[:, None, :] == spots[None, :, None]), spots, 0), axis=2
        )
        count = jnp.minimum(jnp.sum(named.astype(jnp.int32), axis=1), LISTED)
        short = sender(LISTED, rank)
        short_back = receiver(LISTED, count, listed)
        seen[1], too_long, short, short_back = tie((seen[1], too_long, short, short_back))

    with jax.named_scope("loads"):
        load_table = answered[:, :LOAD_TILES].reshape(N_CENT * PAN_DEV, PANEL)
        loads = jnp.take(load_table, slots, axis=0, mode="clip").astype(F32)
        surcharge = jnp.log(loads).reshape(GROUPS_DEV, CAND * PANEL, 1)

    sources = []
    for g in range(GROUPS_DEV):
        with jax.named_scope("score"):
            pieces = score(g, seen[g], arrived[g], shelf, points, surcharge)
        with jax.named_scope("split_pieces"):
            if g == 0:
                sources.append(exchange(pieces, "pts"))
            else:
                with jax.named_scope("sum_over_chips"):
                    sources[0], pieces = tie((sources[0], pieces))
                    sources.append(lax.ppermute(sources[0], "cent", shift(0, 1)))
                    begun = spread(LISTED, *short[0], sources[0])
                    begun = spread(LISTED, *short[1], sources[1], before=begun)
                mine, begun = tie((exchange(pieces, "pts"), begun))
                sources += [mine, lax.ppermute(mine, "cent", shift(0, 1))]

    def sum_over_chips(rows, to, begun, numbers, back_lanes):
        own, own_weights, *far = spread(rows, *to[3], sources[3], before=begun, last=True)
        back = [lax.ppermute(far[d - 1], "cent", shift(d, 0)) for d in range(1, CHIPS)]
        return finish(rows, numbers, begin(me.reshape(1), own, shelf), own_weights, back, back_lanes)

    def send_all():
        everything = jnp.broadcast_to(spots, (CHIPS - 1, PAN_DEV))
        count = jnp.full((CHIPS - 1,), PAN_DEV, jnp.int32)
        to = sender(PAN_DEV, pair % PAN_DEV)
        begun = None
        for n in range(3):
            begun = spread(PAN_DEV, *to[n], sources[n], before=begun)
        return sum_over_chips(PAN_DEV, to, begun, *receiver(PAN_DEV, count, everything))

    with jax.named_scope("sum_over_chips"):
        begun = spread(LISTED, *short[2], sources[2], before=begun, join=True)
        begun, sources[3] = tie((begun, sources[3]))
        fresh = lax.cond(too_long, send_all, lambda: sum_over_chips(LISTED, short, begun, *short_back))

    with jax.named_scope("place"):
        new_centroids, new_loads = place(me.reshape(1), exchange(fresh, "pts"))
    return new_centroids.reshape(CAND * PANEL, WIDTH), new_loads.reshape(CAND * PANEL)


def solution(mesh):
    placed = (P(("pts", "cent"), None), P("cent", None), P("cent"), P(("pts", "cent"), None), P())
    return jax.shard_map(
        local,
        mesh=mesh,
        in_specs=placed,
        out_specs=(P(("cent", "pts"), None), P(("cent", "pts"))),
        check_vma=False,
    )
```
